32 devices in a mesh: row: 4 (over y, core), col: 8 (over z, x).
Axes of the slice: x: 2, y: 2, z: 4, core: 2. Of those that a mesh axis runs over, the one named last changes fastest.
Arguments:
- wavefunction: bfloat16 [4096, 4096], P('row', 'col'), may hold values from -6 to 6
- left_env: bfloat16 [4, 4096, 4096], P(None, 'row'), may hold values from -0.09375 to 0.09375
- right_env: bfloat16 [4, 4096, 4096], P(None, None, 'col'), may hold values from -0.09375 to 0.09375
- filled_blocks: int32 [32, 32], replicated, may hold values 0 or 1
- term_columns: int32 [4, 32], replicated, may hold values 0 or 1
Outputs:
- product: bfloat16 [4096, 4096], P('row', 'col')
The draws below stay inside these ranges and needn't reach their ends.
All inputs are finite; a program needn't handle non-finite values.
Results may differ from the reference program's by a relative error of at most 0.001.
Values may be sent and summed in bfloat16 or wider, within the bound.
No kernel may reach another device: no remote copies, remote signals or barrier semaphores. Data moves between devices by JAX's collectives and lax.ppermute only.
A program may use at most 128 MiB of HBM per device.

```python
import jax
import jax.numpy as jnp
from jax import lax

M = 4096
BLOCK = 128
TERMS = 4
NB = 32


def set_ends(drawn, stream_key, low, high):
    dims = drawn.shape
    spot = [jax.random.randint(jax.random.fold_in(stream_key, axis), (), 0, dims[axis]) for axis in range(len(dims))]
    drawn = drawn.at[tuple(spot)].set(low)
    longest = dims.index(max(dims))
    spot[longest] = (spot[longest] + 1) % dims[longest]
    return drawn.at[tuple(spot)].set(high)


def shard_levels(own_key, shape, split, low, largest):
    gain, own = 1.0, jax.random.fold_in(own_key, 6)
    for dim, shards_of in split:
        steps = jnp.exp(jax.random.uniform(jax.random.fold_in(own, dim), (shards_of,), jnp.float32, low / len(split), largest / len(split)))
        gain = gain * jnp.repeat(steps, shape[dim] // shards_of).reshape([-1 if axis == dim else 1 for axis in range(len(shape))])
    return gain


def scatter_about(stream_key, dims, deviation, limit, split=(), kind=jnp.bfloat16):
    entries = jax.random.normal(stream_key, dims, jnp.float32) * deviation
    if len(split) > 0:
        entries = shard_levels(stream_key, dims, split, -0.22, 0.18) * entries
    return jnp.clip(entries, min=-limit, max=limit).astype(kind)


def setup_inputs(seed: int = 0) -> dict:
    splits = jax.random.split(jax.random.key(seed), 6)
    wavefunction = scatter_about(splits[0], (M, M), 1.0, 6.0, ((0, 4), (1, 8)))
    left_env = scatter_about(splits[1], (TERMS, M, M), M ** -0.5, 0.09375, ((1, 4),))
    right_env = scatter_about(splits[2], (TERMS, M, M), M ** -0.5, 0.09375, ((2, 8),))
    filled_blocks = set_ends((jax.random.randint(splits[3], (NB, NB), 0, 8) < 3).astype(jnp.int32), jax.random.fold_in(splits[3], 1), 0, 1)
    term_columns = set_ends((jax.random.randint(splits[4], (TERMS, NB), 0, 4) < 3).astype(jnp.int32), jax.random.fold_in(splits[4], 1), 0, 1)
    return dict(wavefunction=wavefunction, left_env=left_env, right_env=right_env, filled_blocks=filled_blocks, term_columns=term_columns)


def reference(wavefunction, left_env, right_env, filled_blocks, term_columns):
    allowed = jnp.repeat(jnp.repeat(filled_blocks, BLOCK, axis=0), BLOCK, axis=1).astype(wavefunction.dtype)
    masked = wavefunction * allowed
    summed = jnp.zeros((M, M), jnp.float32)
    for term in range(TERMS):
        column_gate = jnp.repeat(term_columns[term], BLOCK).astype(left_env.dtype)
        acting = left_env[term] * column_gate[None, :]
        middle = jnp.dot(acting, masked, preferred_element_type=jnp.float32)
        summed = summed + jnp.dot(middle, right_env[term].astype(jnp.float32), precision=lax.Precision.HIGHEST, preferred_element_type=jnp.float32)
    return (summed * allowed.astype(jnp.float32)).astype(jnp.bfloat16)
```

```python
import functools

import jax
import jax.numpy as jnp
from jax import lax
from jax.experimental import pallas as pl
from jax.experimental.pallas import tpu as pltpu
from jax.sharding import PartitionSpec as P

BLOCK = 128
CORES = 2
GROUP = 4
CHUNK = 4
AXES = ("row", "col")
VMEM_LIMIT = 58 * 1024 * 1024


class Places:
    def __init__(self, row_devices, col_devices):
        self.rows, self.cols = row_devices, col_devices
        self.y = row_devices // CORES
        self.x = 1
        while self.x * self.x * 4 <= col_devices and col_devices % (self.x * 2) == 0:
            self.x *= 2
        self.z = col_devices // self.x

    def flat(self, y, core, z, x):
        return (y * CORES + core) * self.cols + z * self.x + x

    def shift(self, dy=0, dz=0, dx=0, dcore=0):
        perm = []
        for y in range(self.y):
            for core in range(CORES):
                for z in range(self.z):
                    for x in range(self.x):
                        there = self.flat(
                            (y + dy) % self.y, (core + dcore) % CORES, (z + dz) % self.z, (x + dx) % self.x
                        )
                        perm.append((self.flat(y, core, z, x), there))
        return perm


def compress_kernel(ranges, row_blocks, col_blocks, filled, psi, *rest):
    outs, sems = rest[: len(ranges)], rest[len(ranges)]
    row0 = lax.axis_index("row") * row_blocks
    col0 = lax.axis_index("col") * col_blocks

    def copy(out, low, spot, kb, cb):
        return pltpu.make_async_copy(
            psi.at[pl.ds(kb * BLOCK, BLOCK), pl.ds(cb * BLOCK, BLOCK)], out.at[spot - low], sems.at[spot]
        )

    count = jnp.int32(0)
    for kb in range(row_blocks):
        for cb in range(col_blocks):
            here = filled[row0 + kb, col0 + cb]
            for out, (low, high) in zip(outs, ranges):
                @pl.when((here != 0) & (count >= low) & (count < high))
                def _():
                    copy(out, low, count, kb, cb).start()
            count = count + here
    for out, (low, high) in zip(outs, ranges):
        for spot in range(low, high):
            @pl.when(spot < count)
            def _():
                copy(out, low, spot, 0, 0).wait()


def compress(psi, filled, ranges):
    row_blocks, col_blocks = psi.shape[0] // BLOCK, psi.shape[1] // BLOCK
    return pl.pallas_call(
        functools.partial(compress_kernel, ranges, row_blocks, col_blocks),
        out_shape=[jax.ShapeDtypeStruct((high - low, BLOCK, BLOCK), psi.dtype) for low, high in ranges],
        in_specs=[pl.BlockSpec(memory_space=pltpu.SMEM), pl.BlockSpec(memory_space=pl.ANY)],
        out_specs=[pl.BlockSpec(memory_space=pl.ANY)] * len(ranges),
        scratch_shapes=[pltpu.SemaphoreType.DMA((row_blocks * col_blocks,))],
        name="compress",
    )(filled, psi)


class Layout:
    def __init__(self, places, row_blocks, col_blocks, terms, base):
        self.places, self.row_blocks, self.col_blocks, self.terms, self.base = places, row_blocks, col_blocks, terms, base
        self.slots = row_blocks * col_blocks
        self.states = places.y * row_blocks
        self.old_right = places.cols * col_blocks
        self.shards = places.y * places.z * places.x
        self.stride = self.old_right + CHUNK
        self.pairs = self.states * terms + GROUP
        self.tile = 2 if col_blocks % 2 == 0 else 1
        self.tiles = col_blocks // self.tile
        self.new_left = CORES * row_blocks
        self.trash = self.new_left
        self.list_stride = self.new_left + 2

    def shapes(self):
        return [
            ((self.states + 1) * 1,),
            (self.states * self.stride,),
            (self.states * self.stride,),
            (self.pairs,),
            (self.pairs,),
            (self.tiles * self.list_stride,),
            (1 + self.tiles,),
        ]


def plan_kernel(lay, filled, terms, counts, spots, blocks, pair_q, pair_t, lefts, totals, used, base_of):
    pz, px, py = lay.places.z, lay.places.x, lay.places.y
    row, col = lax.axis_index("row"), lax.axis_index("col")
    core, y_me = row % CORES, row // CORES
    z_me, x_me = col // px, col % px
    for dev in range(lay.places.cols):
        dz = (z_me - dev // px + pz) % pz
        dx = (x_me - dev % px + px) % px
        base_of[dev] = dz * px + dx

    extra = lay.slots - lay.base

    def one_state(q, n_pairs):
        y = q // lay.row_blocks
        kb = q % lay.row_blocks

        @pl.when(kb == 0)
        def _():
            for dev in range(lay.places.cols):
                used[dev] = 0

        dy = (y_me - y + py) % py
        k_block = (y * CORES + core) * lay.row_blocks + kb
        n = jnp.int32(0)
        for c in range(lay.old_right):
            dev = c // lay.col_blocks
            here = filled[k_block, c]
            slot = used[dev]
            shard = dy * (pz * px) + base_of[dev]
            spot = jnp.where(
                slot < lay.base,
                1 + shard * lay.base + slot,
                1 + lay.shards * lay.base + shard * extra + slot - lay.base,
            )
            spots[q * lay.stride + n] = spot
            blocks[q * lay.stride + n] = c
            n = n + here
            used[dev] = slot + here
        for i in range(CHUNK):
            spots[q * lay.stride + n + i] = 0
            blocks[q * lay.stride + n + i] = 0
        counts[q] = n
        for t in range(lay.terms):
            pair_q[n_pairs] = q
            pair_t[n_pairs] = t
            n_pairs = n_pairs + jnp.where((terms[t, k_block] != 0) & (n > 0), 1, 0)
        return n_pairs

    n_pairs = lax.fori_loop(0, lay.states, one_state, jnp.int32(0))
    counts[lay.states] = 0
    for i in range(GROUP):
        pair_q[n_pairs + i] = lay.states
        pair_t[n_pairs + i] = 0
    totals[0] = (n_pairs + GROUP - 1) // GROUP
    for tile in range(lay.tiles):
        n = jnp.int32(0)
        for a in range(lay.new_left):
            side, ab = a // lay.row_blocks, a % lay.row_blocks
            a_block = (y_me * CORES + (core + side) % CORES) * lay.row_blocks + ab
            some = jnp.int32(0)
            for i in range(lay.tile):
                some = some | filled[a_block, col * lay.col_blocks + tile * lay.tile + i]
            lefts[tile * lay.list_stride + n] = a
            n = n + some
        lefts[tile * lay.list_stride + n] = lay.trash
        totals[1 + tile] = (n + 1) // 2


def plan(lay, filled, terms):
    smem = pl.BlockSpec(memory_space=pltpu.SMEM)
    shapes = lay.shapes()
    return pl.pallas_call(
        functools.partial(plan_kernel, lay),
        out_shape=[jax.ShapeDtypeStruct(s, jnp.int32) for s in shapes],
        in_specs=[smem, smem],
        out_specs=[smem] * len(shapes),
        scratch_shapes=[pltpu.SMEM((lay.places.cols,), jnp.int32), pltpu.SMEM((lay.places.cols,), jnp.int32)],
        name="plan",
    )(filled, terms)


def main_kernel(lay, widths, rows, n_sib, *refs):
    refs = list(refs)
    counts, spots, blocks, pair_q, pair_t, lefts, totals = refs[:7]
    right, left = refs[7], refs[8]
    sib = refs[9 : 9 + n_sib]
    n_psi = len(widths) * lay.shards
    psi_in = refs[9 + n_sib : 9 + n_sib + n_psi]
    out_own, out_sib = refs[9 + n_sib + n_psi : 11 + n_sib + n_psi]
    (right_v, psi_v, left_v, acc, w_hi, w_lo, w_acc, right_sem, psi_sem, left_sem, out_sem) = refs[11 + n_sib + n_psi :]
    core = lax.axis_index("row") % CORES
    terms = lay.terms

    def left_copies(g, slot, act):
        for i in range(GROUP):
            q = jnp.minimum(pair_q[g * GROUP + i], lay.states - 1)
            t = pair_t[g * GROUP + i]
            y, kb = q // lay.row_blocks, q % lay.row_blocks
            at = pl.multiple_of(((y * CORES + core) * lay.row_blocks + kb) * BLOCK, BLOCK)
            lanes = pl.ds(i * BLOCK, BLOCK)
            act(
                pltpu.make_async_copy(
                    left.at[t, :, pl.ds(at, BLOCK)], left_v.at[slot, pl.ds(0, rows), lanes], left_sem.at[slot, 2 * i]
                )
            )
            there = pl.multiple_of(kb * BLOCK, BLOCK)
            for yy in range(n_sib):
                @pl.when(y == yy)
                def _():
                    act(
                        pltpu.make_async_copy(
                            sib[yy].at[t, :, pl.ds(there, BLOCK)],
                            left_v.at[slot, pl.ds(rows, rows), lanes],
                            left_sem.at[slot, 2 * i + 1],
                        )
                    )

    loads = []
    for t in range(terms):
        loads.append(pltpu.make_async_copy(right.at[t], right_v.at[t], right_sem.at[t]))
    for part in range(len(widths)):
        for s in range(lay.shards):
            i = part * lay.shards + s
            loads.append(psi_load(lay, widths, part, s, psi_in[i], psi_v, psi_sem.at[i]))
    for load in loads:
        load.start()
    n_groups = totals[0]

    @pl.when(n_groups > 0)
    def _():
        left_copies(0, 0, lambda c: c.start())

    psi_v[0] = jnp.zeros((BLOCK, BLOCK), psi_v.dtype)
    acc[...] = jnp.zeros_like(acc)
    for load in loads:
        load.wait()

    def one_group(g, carry):
        slot = g % 2

        @pl.when(g + 1 < n_groups)
        def _():
            left_copies(g + 1, 1 - slot, lambda c: c.start())

        def one_pair(i, c0):
            q = pair_q[g * GROUP + i]
            t = pair_t[g * GROUP + i]
            w_acc[...] = jnp.zeros_like(w_acc)

            def one_chunk(j, c1):
                at = q * lay.stride + j * CHUNK
                lhs = jnp.concatenate([psi_v[spots[at + m]] for m in range(CHUNK)], axis=1)
                rhs = jnp.concatenate(
                    [
                        right_v[t, pl.ds(pl.multiple_of(blocks[at + m] * BLOCK, BLOCK), BLOCK), :]
                        for m in range(CHUNK)
                    ],
                    axis=0,
                )
                w_acc[...] += jnp.dot(lhs, rhs, preferred_element_type=jnp.float32)
                return c1

            lax.fori_loop(0, (counts[q] + CHUNK - 1) // CHUNK, one_chunk, 0)
            whole = w_acc[...]
            hi = whole.astype(jnp.bfloat16)
            at = pl.ds(pl.multiple_of(i * BLOCK, BLOCK), BLOCK)
            w_hi[at, :] = hi
            w_lo[at, :] = (whole - hi.astype(jnp.float32)).astype(jnp.bfloat16)
            return c0

        lax.fori_loop(0, GROUP, one_pair, 0)
        left_copies(g, slot, lambda c: c.wait())
        for tile in range(lay.tiles):
            width = lay.tile * BLOCK
            lanes = slice(tile * width, (tile + 1) * width)

            def two_lefts(m, c0):
                a0 = lefts[tile * lay.list_stride + 2 * m]
                a1 = lefts[tile * lay.list_stride + 2 * m + 1]
                from1 = jnp.minimum(a1, lay.new_left - 1)
                at0 = pl.ds(pl.multiple_of(a0 * BLOCK, BLOCK), BLOCK)
                at1 = pl.ds(pl.multiple_of(a1 * BLOCK, BLOCK), BLOCK)
                lhs = jnp.concatenate(
                    [left_v[slot, at0, :], left_v[slot, pl.ds(pl.multiple_of(from1 * BLOCK, BLOCK), BLOCK), :]], axis=0
                )
                gain = jnp.dot(lhs, w_hi[:, lanes], preferred_element_type=jnp.float32)
                gain = gain + jnp.dot(lhs, w_lo[:, lanes], preferred_element_type=jnp.float32)
                acc[at0, lanes] += gain[:BLOCK]
                acc[at1, lanes] += gain[BLOCK:]
                return c0

            lax.fori_loop(0, totals[1 + tile], two_lefts, 0)
        return carry

    lax.fori_loop(0, n_groups, one_group, 0)
    stores = [
        pltpu.make_async_copy(acc.at[pl.ds(rows, rows)], out_sib, out_sem.at[1]),
        pltpu.make_async_copy(acc.at[pl.ds(0, rows)], out_own, out_sem.at[0]),
    ]
    for store in stores:
        store.start()
    for store in stores:
        store.wait()


def psi_load(lay, widths, part, s, source, psi_v, sem):
    if part < 2:
        low = 1 + s * lay.base + sum(widths[:part])
    else:
        low = 1 + lay.shards * lay.base + s * (lay.slots - lay.base) + sum(widths[2:part])
    return pltpu.make_async_copy(source, psi_v.at[pl.ds(low, widths[part])], sem)


def contract(lay, tables, right, left, sib, parts):
    rows = lay.row_blocks * BLOCK
    cols = lay.col_blocks * BLOCK
    widths = [part[0].shape[0] for part in parts]
    flat = [array for part in parts for array in part]
    smem = pl.BlockSpec(memory_space=pltpu.SMEM)
    hbm = pl.BlockSpec(memory_space=pl.ANY)
    result = jax.ShapeDtypeStruct((rows, cols), jnp.float32)
    return pl.pallas_call(
        functools.partial(main_kernel, lay, widths, rows, len(sib)),
        out_shape=[result, result],
        in_specs=[smem] * len(tables) + [hbm] * (2 + len(sib) + len(flat)),
        out_specs=[hbm, hbm],
        scratch_shapes=[
            pltpu.VMEM(right.shape, jnp.bfloat16),
            pltpu.VMEM((1 + lay.shards * sum(widths), BLOCK, BLOCK), jnp.bfloat16),
            pltpu.VMEM((2, CORES * rows, GROUP * BLOCK), jnp.bfloat16),
            pltpu.VMEM((CORES * rows + BLOCK, cols), jnp.float32),
            pltpu.VMEM((GROUP * BLOCK, cols), jnp.bfloat16),
            pltpu.VMEM((GROUP * BLOCK, cols), jnp.bfloat16),
            pltpu.VMEM((BLOCK, cols), jnp.float32),
            pltpu.SemaphoreType.DMA((lay.terms,)),
            pltpu.SemaphoreType.DMA((len(flat),)),
            pltpu.SemaphoreType.DMA((2, 2 * GROUP)),
            pltpu.SemaphoreType.DMA((2,)),
        ],
        compiler_params=pltpu.CompilerParams(vmem_limit_bytes=VMEM_LIMIT),
        name="contract",
    )(*tables, right, left, *sib, *flat)


def spread(places, part, x_first):
    got = {(0, 0, 0): part}
    for dz in range(1, places.z):
        got[(0, dz, 0)] = lax.ppermute(part, AXES, places.shift(dz=dz))
    for axis in ("xy" if x_first else "yx"):
        have = dict(got)
        for (dy, dz, dx), array in have.items():
            if axis == "x":
                for step in range(1, places.x):
                    got[(dy, dz, step)] = lax.ppermute(array, AXES, places.shift(dx=step))
            else:
                for step in range(1, places.y):
                    got[(step, dz, dx)] = lax.ppermute(array, AXES, places.shift(dy=step))
    order = [(dy, dz, dx) for dy in range(places.y) for dz in range(places.z) for dx in range(places.x)]
    return [got[key] for key in order]


def on_device(wavefunction, left_env, right_env, filled_blocks, term_columns):
    rows, cols = wavefunction.shape
    row_blocks, col_blocks = rows // BLOCK, cols // BLOCK
    places = Places(lax.axis_size("row"), lax.axis_size("col"))
    slots = row_blocks * col_blocks
    base = -(-slots * 9 // 32) * 2
    extra = slots - base
    lay = Layout(places, row_blocks, col_blocks, left_env.shape[0], base)
    row_place, col_place = lax.axis_index("row"), lax.axis_index("col")

    cuts = [0, base // 2, base, base + extra // 2, slots]
    ranges = [(low, high) for low, high in zip(cuts[:-1], cuts[1:]) if high > low]
    packed = list(compress(wavefunction, filled_blocks, ranges))

    other = (row_place + 1) % CORES
    packed[0], left_late = lax.optimization_barrier((packed[0], left_env))
    parts = [spread(places, packed[0], True), spread(places, packed[1], False)]
    swap = places.shift(dcore=1)
    sib = [
        lax.ppermute(
            lax.dynamic_slice(left_late, (0, 0, (y * CORES + other) * rows), (left_env.shape[0], rows, rows)), AXES, swap
        )
        for y in range(places.y)
    ]
    tables = plan(lay, filled_blocks, term_columns)

    per_device = filled_blocks.reshape(places.rows, row_blocks, places.cols, col_blocks).sum(axis=(1, 3))

    def more(_):
        rest = [spread(places, part, i == 0) for i, part in enumerate(packed[2:])]
        return contract(lay, tables, right_env, left_env, sib, parts + rest)

    def enough(_):
        return contract(lay, tables, right_env, left_env, sib, parts)

    own, theirs = lax.cond(jnp.max(per_device) > base, more, enough, 0)
    summed = own + lax.ppermute(theirs, AXES, swap)
    here = lax.dynamic_slice(
        filled_blocks, (row_place * row_blocks, col_place * col_blocks), (row_blocks, col_blocks)
    )
    result = jnp.where(
        here[:, None, :, None] != 0, summed.reshape(row_blocks, BLOCK, col_blocks, BLOCK), jnp.float32(0)
    )
    return result.reshape(rows, cols).astype(jnp.bfloat16)


def solution(mesh):
    in_specs = (P("row", "col"), P(None, "row", None), P(None, None, "col"), P(), P())
    out_specs = P("row", "col")
    return jax.shard_map(
        on_device, mesh=mesh, in_specs=in_specs, out_specs=out_specs, check_vma=False
    )
```

```python
import functools

import jax
import jax.numpy as jnp
from jax import lax
from jax.experimental import pallas as pl
from jax.experimental.pallas import tpu as pltpu
from jax.sharding import PartitionSpec as P

BLOCK = 128
CORES = 2
GROUP = 4
CHUNK = 4
AXES = ("row", "col")
VMEM_LIMIT = 58 * 1024 * 1024


class Places:
    def __init__(self, row_devices, col_devices):
        self.rows, self.cols = row_devices, col_devices
        self.y = row_devices // CORES
        self.x = 1
        while self.x * self.x * 4 <= col_devices and col_devices % (self.x * 2) == 0:
            self.x *= 2
        self.z = col_devices // self.x

    def flat(self, y, core, z, x):
        return (y * CORES + core) * self.cols + z * self.x + x

    def shift(self, dy=0, dz=0, dx=0, dcore=0):
        perm = []
        for y in range(self.y):
            for core in range(CORES):
                for z in range(self.z):
                    for x in range(self.x):
                        there = self.flat(
                            (y + dy) % self.y, (core + dcore) % CORES, (z + dz) % self.z, (x + dx) % self.x
                        )
                        perm.append((self.flat(y, core, z, x), there))
        return perm


def compress_kernel(ranges, row_blocks, col_blocks, filled, psi, *rest):
    outs, sems = rest[: len(ranges)], rest[len(ranges)]
    row0 = lax.axis_index("row") * row_blocks
    col0 = lax.axis_index("col") * col_blocks

    def copy(i, slot, kb, cb):
        return pltpu.make_async_copy(
            psi.at[pl.ds(kb * BLOCK, BLOCK), pl.ds(cb * BLOCK, BLOCK)], outs[i].at[slot - ranges[i][0]], sems.at[i, slot]
        )

    count = jnp.int32(0)
    for kb in range(row_blocks):
        for cb in range(col_blocks):
            here = filled[row0 + kb, col0 + cb]
            for i, (low, high) in enumerate(ranges):
                @pl.when((here != 0) & (count >= low) & (count < high))
                def _():
                    copy(i, count, kb, cb).start()
            count = count + here
    for i, (low, high) in enumerate(ranges):
        for slot in range(low, high):
            @pl.when(slot < count)
            def _():
                copy(i, slot, 0, 0).wait()


def compress(psi, filled, ranges):
    row_blocks, col_blocks = psi.shape[0] // BLOCK, psi.shape[1] // BLOCK
    return pl.pallas_call(
        functools.partial(compress_kernel, ranges, row_blocks, col_blocks),
        out_shape=[jax.ShapeDtypeStruct((high - low, BLOCK, BLOCK), psi.dtype) for low, high in ranges],
        in_specs=[pl.BlockSpec(memory_space=pltpu.SMEM), pl.BlockSpec(memory_space=pl.ANY)],
        out_specs=[pl.BlockSpec(memory_space=pl.ANY)] * len(ranges),
        scratch_shapes=[pltpu.SemaphoreType.DMA((len(ranges), row_blocks * col_blocks))],
        name="compress",
    )(filled, psi)


class Layout:
    def __init__(self, places, row_blocks, col_blocks, terms, chunks):
        self.places, self.row_blocks, self.col_blocks, self.terms, self.chunks = places, row_blocks, col_blocks, terms, chunks
        self.slots = row_blocks * col_blocks
        self.states = places.y * row_blocks
        self.old_right = places.cols * col_blocks
        self.shards = places.y * places.z * places.x
        self.stride = self.old_right + CHUNK
        self.pairs = self.states * terms + GROUP
        self.tile = 2 if col_blocks % 2 == 0 else 1
        self.tiles = col_blocks // self.tile
        self.new_left = CORES * row_blocks
        self.trash = self.new_left
        self.list_stride = self.new_left + 2
        self.runs = []
        slot, place = 0, 1
        for wide in chunks:
            self.runs.append((slot, wide, place))
            slot += wide
            place += wide * self.shards

    def room(self, chunks):
        return 1 + self.shards * sum(self.chunks[:chunks])

    def shapes(self):
        return [
            (self.states + 1,),
            ((self.states + 1) * self.stride,),
            ((self.states + 1) * self.stride,),
            (2 * self.pairs,),
            (2 * self.pairs,),
            (self.tiles * self.list_stride,),
            (3,),
        ]


def plan_kernel(lay, filled, terms, counts, spots, blocks, pair_q, pair_t, lefts, totals, used):
    pz, px, py = lay.places.z, lay.places.x, lay.places.y
    row, col = lax.axis_index("row"), lax.axis_index("col")
    core, y_me = row % CORES, row // CORES
    z_me, x_me = col // px, col % px

    def one_state(q, carry):
        n_early, n_late = carry
        y = q // lay.row_blocks
        kb = q % lay.row_blocks

        @pl.when(kb == 0)
        def _():
            for dev in range(lay.places.cols):
                used[dev] = 0

        dy = (y_me - y + py) % py
        k_block = (y * CORES + core) * lay.row_blocks + kb
        n = jnp.int32(0)
        most = jnp.int32(0)
        for dev in range(lay.places.cols):
            dz = (z_me - dev // px + pz) % pz
            dx = (x_me - dev % px + px) % px
            shard = (dy * px + dx) * pz + dz
            slot = used[dev]
            for cb in range(lay.col_blocks):
                c = dev * lay.col_blocks + cb
                here = filled[k_block, c]
                spot = jnp.int32(0)
                for first, wide, place in lay.runs:
                    spot = jnp.where(slot >= first, place + shard * wide + slot - first, spot)
                spots[q * lay.stride + n] = spot
                blocks[q * lay.stride + n] = c
                n = n + here
                slot = slot + here
            used[dev] = slot
            most = jnp.maximum(most, slot)

        def pad(i, carry):
            spots[q * lay.stride + i] = 0
            blocks[q * lay.stride + i] = 0
            return carry

        lax.fori_loop(n, lay.stride, pad, 0)
        counts[q] = n
        early = most <= lay.chunks[0]
        for t in range(lay.terms):
            at = jnp.where(early, n_early, lay.pairs + n_late)
            pair_q[at] = q
            pair_t[at] = t
            on = (terms[t, k_block] != 0) & (n > 0)
            n_early = n_early + jnp.where(on & early, 1, 0)
            n_late = n_late + jnp.where(on & jnp.logical_not(early), 1, 0)
        return n_early, n_late

    n_early, n_late = lax.fori_loop(0, lay.states, one_state, (jnp.int32(0), jnp.int32(0)))
    counts[lay.states] = 0
    for i in range(lay.stride):
        spots[lay.states * lay.stride + i] = 0
        blocks[lay.states * lay.stride + i] = 0
    for i in range(GROUP):
        for at in (n_early + i, lay.pairs + n_late + i):
            pair_q[at] = lay.states
            pair_t[at] = 0
    totals[0] = (n_early + GROUP - 1) // GROUP
    totals[1] = (n_late + GROUP - 1) // GROUP
    most = jnp.int32(0)
    for tile in range(lay.tiles):
        n = jnp.int32(0)
        for a in range(lay.new_left):
            side, ab = a // lay.row_blocks, a % lay.row_blocks
            a_block = (y_me * CORES + (core + side) % CORES) * lay.row_blocks + ab
            some = jnp.int32(0)
            for i in range(lay.tile):
                some = some | filled[a_block, col * lay.col_blocks + tile * lay.tile + i]
            lefts[tile * lay.list_stride + n] = a
            n = n + some
        most = jnp.maximum(most, n)

        def pad(i, carry):
            lefts[tile * lay.list_stride + i] = lay.trash
            return carry

        lax.fori_loop(n, lay.list_stride, pad, 0)
    totals[2] = (most + 1) // 2


def plan(lay, filled, terms):
    smem = pl.BlockSpec(memory_space=pltpu.SMEM)
    shapes = lay.shapes()
    return pl.pallas_call(
        functools.partial(plan_kernel, lay),
        out_shape=[jax.ShapeDtypeStruct(s, jnp.int32) for s in shapes],
        in_specs=[smem, smem],
        out_specs=[smem] * len(shapes),
        scratch_shapes=[pltpu.SMEM((lay.places.cols,), jnp.int32)],
        name="plan",
    )(filled, terms)


def main_kernel(lay, stage, stages, places_of, rows, *refs):
    late = stage == stages
    n_psi = len(places_of)
    counts, spots, blocks, pair_q, pair_t, lefts, totals, right, left, sib = refs[:10]
    psi_in, refs = refs[10 : 10 + n_psi], refs[10 + n_psi :]
    before = None
    if stage > 0:
        before, refs = refs[0], refs[1:]
    if late:
        (out_own, out_sib), refs = refs[:2], refs[2:]
    else:
        out, refs = refs[0], refs[1:]
    right_v, psi_v, left_v, acc, w_hi, w_lo, w_acc, right_sem, psi_sem, left_sem, out_sem = refs
    core = lax.axis_index("row") % CORES
    list_at = lay.pairs if late else 0
    everything = CORES * rows

    def left_copies(g, slot, act):
        for i in range(GROUP):
            q = jnp.minimum(pair_q[list_at + g * GROUP + i], lay.states - 1)
            t = pair_t[list_at + g * GROUP + i]
            y, kb = q // lay.row_blocks, q % lay.row_blocks
            at = pl.ds(pl.multiple_of(((y * CORES + core) * lay.row_blocks + kb) * BLOCK, BLOCK), BLOCK)
            lanes = pl.ds(i * BLOCK, BLOCK)
            for side, source in enumerate((left, sib)):
                act(
                    pltpu.make_async_copy(
                        source.at[t, :, at], left_v.at[slot, pl.ds(side * rows, rows), lanes], left_sem.at[slot, 2 * i + side]
                    )
                )

    loads = [pltpu.make_async_copy(right.at[t], right_v.at[t], right_sem.at[t]) for t in range(lay.terms)]
    for i, (first, place, wide) in enumerate(places_of):
        loads.append(pltpu.make_async_copy(psi_in[i].at[pl.ds(first, wide)], psi_v.at[pl.ds(place, wide)], psi_sem.at[i]))
    if stage > 0:
        loads.append(pltpu.make_async_copy(before, acc.at[pl.ds(0, everything)], out_sem.at[0]))
    if late:
        start, stop = 0, totals[1]
    else:
        start, stop = totals[0] * stage // stages, totals[0] * (stage + 1) // stages

    @pl.when(stop > start)
    def _():
        left_copies(start, start % 2, lambda c: c.start())

    for load in loads:
        load.start()
    psi_v[0] = jnp.zeros((BLOCK, BLOCK), psi_v.dtype)
    if stage > 0:
        acc[pl.ds(everything, BLOCK), :] = jnp.zeros((BLOCK, acc.shape[1]), acc.dtype)
    else:
        acc[...] = jnp.zeros_like(acc)
    for load in loads:
        load.wait()

    def one_group(g, carry):
        slot = g % 2

        @pl.when(g + 1 < stop)
        def _():
            left_copies(g + 1, 1 - slot, lambda c: c.start())

        w_acc[...] = jnp.zeros_like(w_acc)
        qs = [pair_q[list_at + g * GROUP + i] for i in range(GROUP)]
        ts = [pair_t[list_at + g * GROUP + i] for i in range(GROUP)]
        longest = counts[qs[0]]
        for q in qs[1:]:
            longest = jnp.maximum(longest, counts[q])

        def one_chunk(j, c1):
            for i in range(GROUP):
                at = qs[i] * lay.stride + j * CHUNK
                lhs = jnp.concatenate([psi_v[spots[at + m]] for m in range(CHUNK)], axis=1)
                rhs = jnp.concatenate(
                    [
                        right_v[ts[i], pl.ds(pl.multiple_of(blocks[at + m] * BLOCK, BLOCK), BLOCK), :]
                        for m in range(CHUNK)
                    ],
                    axis=0,
                )
                w_acc[i * BLOCK : (i + 1) * BLOCK, :] += jnp.dot(lhs, rhs, preferred_element_type=jnp.float32)
            return c1

        lax.fori_loop(0, (longest + CHUNK - 1) // CHUNK, one_chunk, 0)
        whole = w_acc[...]
        hi = whole.astype(jnp.bfloat16)
        w_hi[...] = hi
        w_lo[...] = (whole - hi.astype(jnp.float32)).astype(jnp.bfloat16)
        left_copies(g, slot, lambda c: c.wait())

        def some_lefts(m, c0):
            for tile in range(lay.tiles):
                lanes = slice(tile * lay.tile * BLOCK, (tile + 1) * lay.tile * BLOCK)
                a = [lefts[tile * lay.list_stride + 2 * m + i] for i in range(2)]
                source = [pl.multiple_of(jnp.minimum(b, lay.new_left - 1) * BLOCK, BLOCK) for b in a]
                lhs = jnp.concatenate([left_v[slot, pl.ds(b, BLOCK), :] for b in source], axis=0)
                gain = jnp.dot(lhs, w_hi[:, lanes], preferred_element_type=jnp.float32)
                gain = gain + jnp.dot(lhs, w_lo[:, lanes], preferred_element_type=jnp.float32)
                for i in range(2):
                    acc[pl.ds(pl.multiple_of(a[i] * BLOCK, BLOCK), BLOCK), lanes] += gain[i * BLOCK : (i + 1) * BLOCK]
            return c0

        lax.fori_loop(0, totals[2], some_lefts, 0)
        return carry

    lax.fori_loop(start, stop, one_group, 0)
    if late:
        stores = [
            pltpu.make_async_copy(acc.at[pl.ds(rows, rows)], out_sib, out_sem.at[1]),
            pltpu.make_async_copy(acc.at[pl.ds(0, rows)], out_own, out_sem.at[0]),
        ]
    else:
        stores = [pltpu.make_async_copy(acc.at[pl.ds(0, everything)], out, out_sem.at[0])]
    for store in stores:
        store.start()
    for store in stores:
        store.wait()


def contract(lay, stage, stages, tables, right, left, sib, parts, before=None):
    late = stage == stages
    rows = lay.row_blocks * BLOCK
    cols = lay.col_blocks * BLOCK
    flat, places_of = [], []
    for (_, wide, place), part in zip(lay.runs, parts):
        for shard, array, first, count in part:
            flat.append(array)
            places_of.append((first, place + shard * wide, count))
    smem = pl.BlockSpec(memory_space=pltpu.SMEM)
    hbm = pl.BlockSpec(memory_space=pl.ANY)
    operands = [right, left, sib, *flat] + ([before] if stage > 0 else [])
    one = jax.ShapeDtypeStruct((rows, cols), jnp.float32)
    both = jax.ShapeDtypeStruct((CORES * rows, cols), jnp.float32)
    return pl.pallas_call(
        functools.partial(main_kernel, lay, stage, stages, places_of, rows),
        out_shape=[one, one] if late else both,
        in_specs=[smem] * len(tables) + [hbm] * len(operands),
        out_specs=[hbm, hbm] if late else hbm,
        scratch_shapes=[
            pltpu.VMEM(right.shape, jnp.bfloat16),
            pltpu.VMEM((lay.room(len(parts)), BLOCK, BLOCK), jnp.bfloat16),
            pltpu.VMEM((2, CORES * rows, GROUP * BLOCK), jnp.bfloat16),
            pltpu.VMEM((CORES * rows + BLOCK, cols), jnp.float32),
            pltpu.VMEM((GROUP * BLOCK, cols), jnp.bfloat16),
            pltpu.VMEM((GROUP * BLOCK, cols), jnp.bfloat16),
            pltpu.VMEM((GROUP * BLOCK, cols), jnp.float32),
            pltpu.SemaphoreType.DMA((lay.terms,)),
            pltpu.SemaphoreType.DMA((len(flat),)),
            pltpu.SemaphoreType.DMA((2, 2 * GROUP)),
            pltpu.SemaphoreType.DMA((2,)),
        ],
        compiler_params=pltpu.CompilerParams(vmem_limit_bytes=VMEM_LIMIT),
        cost_estimate=pl.CostEstimate(
            flops=2 * right.shape[0] * rows * right.shape[1] * cols, bytes_accessed=right.size * 4, transcendentals=0
        ),
        name="late_contract" if late else "early_contract",
    )(*tables, *operands)


def pack_kernel(copies, *refs):
    n_out = 1 + max(copy[3] for copy in copies)
    sources, outs, sems = refs[: -1 - n_out], refs[-1 - n_out : -1], refs[-1]
    moves = [
        pltpu.make_async_copy(sources[source].at[pl.ds(first, wide)], outs[out].at[pl.ds(at, wide)], sems.at[i])
        for i, (source, first, wide, out, at) in enumerate(copies)
    ]
    for move in moves:
        move.start()
    for move in moves:
        move.wait()


def pack(arrays, copies):
    n_out = 1 + max(copy[3] for copy in copies)
    sizes = [sum(copy[2] for copy in copies if copy[3] == out) for out in range(n_out)]
    hbm = pl.BlockSpec(memory_space=pl.ANY)
    return pl.pallas_call(
        functools.partial(pack_kernel, copies),
        out_shape=[jax.ShapeDtypeStruct((size, *arrays[0].shape[1:]), arrays[0].dtype) for size in sizes],
        in_specs=[hbm] * len(arrays),
        out_specs=[hbm] * n_out,
        scratch_shapes=[pltpu.SemaphoreType.DMA((len(copies),))],
        name="pack",
    )(*arrays)


def after(array, *others):
    return lax.optimization_barrier((array, *others))[0]


class Spread:
    def __init__(self, places, part, x_own, y_own, first):
        self.places, self.part, self.wide = places, part, part.shape[0]
        self.x_own, self.y_own, self.first = x_own, y_own, first

    def over_z(self, *others):
        part = after(self.part, *others) if others else self.part
        z = self.places.z
        up, down = {0: part}, {0: part}
        for far in range(1, z // 2 + 1):
            up[far] = move(self.places, up[far - 1], dz=1)
            if far < z - far:
                down[far] = move(self.places, down[far - 1], dz=z - 1)
        self.z = [up[dz] if dz in up else down[z - dz] for dz in range(1, z)]

    def pack_z(self, *others):
        z = [after(array, *others) for array in self.z] if others else self.z
        (self.q,) = pack(z, [(i, 0, self.wide, 0, i * self.wide) for i in range(len(self.z))])
        return self.q

    def over_xy(self, *others):
        q = after(self.q, *others) if others else self.q
        self.x_line = [move(self.places, q, dx=dx) for dx in range(1, self.places.x)]
        self.y_line = [move(self.places, q, dy=dy) for dy in range(1, self.places.y)]

    def pack_rest(self, *others):
        w, half = self.wide, self.places.z // 2
        n_x, n_y = len(self.x_own), len(self.y_own)
        y_line = [after(array, *others) for array in self.y_line] if others else self.y_line
        arrays = self.x_own + self.x_line + y_line
        copies = []
        for i in range(n_x):
            copies.append((i, self.first, w, i, 0))
            if half > 1:
                copies.append((n_x + i, 0, (half - 1) * w, i, w))
        for i in range(n_y):
            copies.append((2 * n_x + i, (half - 1) * w, (self.places.z - half) * w, n_x + i, 0))
        packed = pack(arrays, copies)
        self.from_x, self.from_y = packed[:n_x], packed[n_x:]
        return self.from_x[0]

    def rest(self):
        self.rest_over_y = {
            (dy, i + 1): move(self.places, array, dy=dy)
            for i, array in enumerate(self.from_x)
            for dy in range(1, self.places.y)
        }
        self.rest_over_x = {
            (i + 1, dx): move(self.places, array, dx=dx)
            for i, array in enumerate(self.from_y)
            for dx in range(1, self.places.x)
        }
        return [*self.rest_over_y.values(), *self.rest_over_x.values()]

    def arrays(self):
        x, z, w = self.places.x, self.places.z, self.wide
        got = [(0, self.part, 0, w), (1, self.q, 0, (z - 1) * w)]
        for own, line, step in ((self.x_own, self.x_line, z), (self.y_own, self.y_line, x * z)):
            for i in range(len(own)):
                got.append(((i + 1) * step, own[i], self.first, w))
                got.append(((i + 1) * step + 1, line[i], 0, (z - 1) * w))
        for (dy, dx), array in self.rest_over_y.items():
            got.append(((dy * x + dx) * z, array, 0, array.shape[0]))
        for (dy, dx), array in self.rest_over_x.items():
            got.append(((dy * x + dx) * z + z // 2, array, 0, array.shape[0]))
        return got


def move(places, array, **step):
    return lax.ppermute(array, AXES, places.shift(**step))


def on_device(wavefunction, left_env, right_env, filled_blocks, term_columns):
    rows, cols = wavefunction.shape
    row_blocks, col_blocks = rows // BLOCK, cols // BLOCK
    places = Places(lax.axis_size("row"), lax.axis_size("col"))
    slots = row_blocks * col_blocks
    chunks = [-(-slots * 10 // 32), slots * 8 // 32]
    base = sum(chunks)
    chunks.append(slots - base)
    lay = Layout(places, row_blocks, col_blocks, left_env.shape[0], chunks)
    row_place, col_place = lax.axis_index("row"), lax.axis_index("col")

    own, part1, part2, part3 = compress(
        wavefunction, filled_blocks, [(0, base), (0, chunks[0]), (chunks[0], base), (base, slots)]
    )
    x_own = [move(places, own, dx=dx) for dx in range(1, places.x)]
    y_own = [move(places, own, dy=dy) for dy in range(1, places.y)]
    one = Spread(places, part1, x_own, y_own, 0)
    two = Spread(places, part2, x_own, y_own, chunks[0])

    one.over_z()
    one.pack_z(*x_own, *y_own)
    one.over_xy()
    two.over_z(one.q)
    swap = places.shift(dcore=1)
    sib = lax.ppermute(left_env, AXES, swap)
    tables = plan(lay, filled_blocks, term_columns)
    two.pack_z()
    one.pack_rest(two.q)
    diagonal = one.rest()
    first = one.arrays()
    two.q = after(two.q, *diagonal)
    two.over_xy()
    early = contract(lay, 0, 2, tables, after(right_env, two.q), left_env, sib, [first])
    gone = two.pack_rest(early)
    two.rest()
    early = contract(lay, 1, 2, tables, after(right_env, gone), left_env, sib, [first], early)
    second = two.arrays()

    per_device = filled_blocks.reshape(places.rows, row_blocks, places.cols, col_blocks).sum(axis=(1, 3))

    def more(_):
        three = Spread(
            places,
            part3,
            [move(places, part3, dx=dx) for dx in range(1, places.x)],
            [move(places, part3, dy=dy) for dy in range(1, places.y)],
            0,
        )
        three.over_z()
        three.pack_z()
        three.over_xy()
        three.pack_rest()
        three.rest()
        return contract(lay, 2, 2, tables, right_env, left_env, sib, [first, second, three.arrays()], early)

    def enough(_):
        return contract(lay, 2, 2, tables, right_env, left_env, sib, [first, second], early)

    own, theirs = lax.cond(jnp.max(per_device) > base, more, enough, 0)
    summed = own + lax.ppermute(theirs, AXES, swap)
    here = lax.dynamic_slice(
        filled_blocks, (row_place * row_blocks, col_place * col_blocks), (row_blocks, col_blocks)
    )
    result = jnp.where(
        here[:, None, :, None] != 0, summed.reshape(row_blocks, BLOCK, col_blocks, BLOCK), jnp.float32(0)
    )
    return result.reshape(rows, cols).astype(jnp.bfloat16)


def solution(mesh):
    in_specs = (P("row", "col"), P(None, "row", None), P(None, None, "col"), P(), P())
    out_specs = P("row", "col")
    return jax.shard_map(
        on_device, mesh=mesh, in_specs=in_specs, out_specs=out_specs, check_vma=False
    )
```

```python
import functools

import jax
import jax.numpy as jnp
from jax import lax
from jax.experimental import pallas as pl
from jax.experimental.pallas import tpu as pltpu
from jax.sharding import PartitionSpec as P

BLOCK = 128
CORES = 2
ITEMS = 2
GROUP = 4
CHUNK = 4
AXES = ("row", "col")
VMEM_LIMIT = 58 * 1024 * 1024


class Places:
    def __init__(self, row_devices, col_devices):
        self.rows, self.cols = row_devices, col_devices
        self.y = row_devices // CORES
        self.x = 1
        while self.x * self.x * 4 <= col_devices and col_devices % (self.x * 2) == 0:
            self.x *= 2
        self.z = col_devices // self.x

    def flat(self, y, core, z, x):
        return (y * CORES + core) * self.cols + z * self.x + x

    def shift(self, dy=0, dz=0, dx=0, dcore=0):
        perm = []
        for y in range(self.y):
            for core in range(CORES):
                for z in range(self.z):
                    for x in range(self.x):
                        there = self.flat(
                            (y + dy) % self.y, (core + dcore) % CORES, (z + dz) % self.z, (x + dx) % self.x
                        )
                        perm.append((self.flat(y, core, z, x), there))
        return perm


def compress_kernel(ranges, row_blocks, col_blocks, filled, psi, *rest):
    outs, sems = rest[: len(ranges)], rest[len(ranges)]
    row0 = lax.axis_index("row") * row_blocks
    col0 = lax.axis_index("col") * col_blocks

    def copy(i, slot, kb, cb):
        return pltpu.make_async_copy(
            psi.at[pl.ds(kb * BLOCK, BLOCK), pl.ds(cb * BLOCK, BLOCK)], outs[i].at[slot - ranges[i][0]], sems.at[i, slot]
        )

    count = jnp.int32(0)
    for kb in range(row_blocks):
        for cb in range(col_blocks):
            here = filled[row0 + kb, col0 + cb]
            for i, (low, high) in enumerate(ranges):
                @pl.when((here != 0) & (count >= low) & (count < high))
                def _():
                    copy(i, count, kb, cb).start()
            count = count + here
    for i, (low, high) in enumerate(ranges):
        for slot in range(low, high):
            @pl.when(slot < count)
            def _():
                copy(i, slot, 0, 0).wait()


def compress(psi, filled, ranges):
    row_blocks, col_blocks = psi.shape[0] // BLOCK, psi.shape[1] // BLOCK
    return pl.pallas_call(
        functools.partial(compress_kernel, ranges, row_blocks, col_blocks),
        out_shape=[jax.ShapeDtypeStruct((high - low, BLOCK, BLOCK), psi.dtype) for low, high in ranges],
        in_specs=[pl.BlockSpec(memory_space=pltpu.SMEM), pl.BlockSpec(memory_space=pltpu.VMEM)],
        out_specs=[pl.BlockSpec(memory_space=pltpu.VMEM)] * len(ranges),
        scratch_shapes=[pltpu.SemaphoreType.DMA((len(ranges), row_blocks * col_blocks))],
        name="compress",
    )(filled, psi)


class Layout:
    def __init__(self, places, row_blocks, col_blocks, terms, chunks):
        self.places, self.row_blocks, self.col_blocks, self.terms, self.chunks = places, row_blocks, col_blocks, terms, chunks
        self.slots = row_blocks * col_blocks
        self.states = places.y * row_blocks
        self.old_right = places.cols * col_blocks
        self.shards = places.y * places.z * places.x
        self.stride = self.old_right + CHUNK
        self.pairs = self.states * terms + GROUP
        self.tile = 2 if col_blocks % 2 == 0 else 1
        self.tiles = col_blocks // self.tile
        self.new_left = CORES * row_blocks
        self.trash = self.new_left
        self.items = self.tiles * ((self.new_left + 1) // 2) + ITEMS
        self.runs = []
        slot, place = 0, 1
        for wide in chunks:
            self.runs.append((slot, wide, place))
            slot += wide
            place += wide * self.shards

    def room(self, chunks):
        return 1 + self.shards * sum(self.chunks[:chunks])

    def shapes(self):
        return [
            (self.states + 1,),
            ((self.states + 1) * self.stride,),
            ((self.states + 1) * self.stride,),
            (2 * self.pairs,),
            (2 * self.pairs,),
            (2 * self.items,),
            (self.items,),
            (3,),
        ]


def plan_kernel(lay, filled, terms, counts, spots, blocks, pair_q, pair_t, lefts, item_tile, totals, used, ready):
    pz, px, py = lay.places.z, lay.places.x, lay.places.y
    row, col = lax.axis_index("row"), lax.axis_index("col")
    core, y_me = row % CORES, row // CORES
    z_me, x_me = col // px, col % px

    def one_state(q, n_ready):
        y = q // lay.row_blocks
        kb = q % lay.row_blocks

        @pl.when(kb == 0)
        def _():
            for dev in range(lay.places.cols):
                used[dev] = 0

        dy = (y_me - y + py) % py
        k_block = (y * CORES + core) * lay.row_blocks + kb
        n = jnp.int32(0)
        most = jnp.int32(0)
        for dev in range(lay.places.cols):
            dz = (z_me - dev // px + pz) % pz
            dx = (x_me - dev % px + px) % px
            shard = (dy * px + dx) * pz + dz
            slot = used[dev]
            for cb in range(lay.col_blocks):
                c = dev * lay.col_blocks + cb
                here = filled[k_block, c]
                spot = jnp.int32(0)
                for first, wide, place in lay.runs:
                    spot = jnp.where(slot >= first, place + shard * wide + slot - first, spot)
                spots[q * lay.stride + n] = spot
                blocks[q * lay.stride + n] = c
                n = n + here
                slot = slot + here
            used[dev] = slot
            most = jnp.maximum(most, slot)

        def pad(i, carry):
            spots[q * lay.stride + i] = 0
            blocks[q * lay.stride + i] = 0
            return carry

        lax.fori_loop(n, lay.stride, pad, 0)
        counts[q] = n
        early = jnp.where(most <= lay.chunks[0], 1, 0)
        ready[q] = early
        for t in range(lay.terms):
            n_ready = n_ready + jnp.where((terms[t, k_block] != 0) & (n > 0), early, 0)
        return n_ready

    n_ready = lax.fori_loop(0, lay.states, one_state, jnp.int32(0))
    n_ready = n_ready // GROUP * GROUP
    n_early, n_late = jnp.int32(0), jnp.int32(0)
    for t in range(lay.terms):

        def one_pair(q, carry):
            n_early, n_late = carry
            k_block = (q // lay.row_blocks * CORES + core) * lay.row_blocks + q % lay.row_blocks
            on = jnp.where((terms[t, k_block] != 0) & (counts[q] > 0), 1, 0)
            early = jnp.where((ready[q] != 0) & (n_early < n_ready), on, 0)
            at = jnp.where(early != 0, n_early, lay.pairs + n_late)
            pair_q[at] = q
            pair_t[at] = t
            return n_early + early, n_late + on - early

        n_early, n_late = lax.fori_loop(0, lay.states, one_pair, (n_early, n_late))
    counts[lay.states] = 0

    def pad_state(i, carry):
        spots[lay.states * lay.stride + i] = 0
        blocks[lay.states * lay.stride + i] = 0
        return carry

    lax.fori_loop(0, lay.stride, pad_state, 0)
    for i in range(GROUP):
        pair_q[lay.pairs + n_late + i] = lay.states
        pair_t[lay.pairs + n_late + i] = lay.terms - 1
    totals[0] = n_early // GROUP
    totals[1] = (n_late + GROUP - 1) // GROUP
    items = jnp.int32(0)
    for tile in range(lay.tiles):
        n = jnp.int32(0)
        for a in range(lay.new_left):
            side, ab = a // lay.row_blocks, a % lay.row_blocks
            a_block = (y_me * CORES + (core + side) % CORES) * lay.row_blocks + ab
            some = jnp.int32(0)
            for i in range(lay.tile):
                some = some | filled[a_block, col * lay.col_blocks + tile * lay.tile + i]
            lefts[2 * items + n] = a
            item_tile[items + n // 2] = tile
            n = n + some
        lefts[2 * items + n] = lay.trash
        items = items + (n + 1) // 2
    for i in range(ITEMS):
        lefts[2 * (items + i)] = lay.trash
        lefts[2 * (items + i) + 1] = lay.trash
        item_tile[items + i] = 0
    totals[2] = (items + ITEMS - 1) // ITEMS


def plan(lay, filled, terms):
    smem = pl.BlockSpec(memory_space=pltpu.SMEM)
    shapes = lay.shapes()
    return pl.pallas_call(
        functools.partial(plan_kernel, lay),
        out_shape=[jax.ShapeDtypeStruct(s, jnp.int32) for s in shapes],
        in_specs=[smem, smem],
        out_specs=[smem] * len(shapes),
        scratch_shapes=[pltpu.SMEM((lay.places.cols,), jnp.int32), pltpu.SMEM((lay.states,), jnp.int32)],
        name="plan",
    )(filled, terms)


def main_kernel(lay, stage, stages, places_of, rows, *refs):
    late = stage == stages
    n_psi = len(places_of)
    counts, spots, blocks, pair_q, pair_t, lefts, item_tile, totals, right, left, sib = refs[:11]
    psi_in, refs = refs[11 : 11 + n_psi], refs[11 + n_psi :]
    before = None
    if stage > 0:
        before, refs = refs[0], refs[1:]
    if late:
        (out_own, out_sib), refs = refs[:2], refs[2:]
    else:
        out, refs = refs[0], refs[1:]
    right_v, psi_v, left_v, acc, w_hi, w_lo, w_acc, right_sem, psi_sem, left_sem, out_sem = refs
    core = lax.axis_index("row") % CORES
    list_at = lay.pairs if late else 0
    everything = CORES * rows

    def left_copies(g, slot, act):
        for i in range(GROUP):
            q = jnp.minimum(pair_q[list_at + g * GROUP + i], lay.states - 1)
            t = pair_t[list_at + g * GROUP + i]
            y, kb = q // lay.row_blocks, q % lay.row_blocks
            at = pl.ds(pl.multiple_of(((y * CORES + core) * lay.row_blocks + kb) * BLOCK, BLOCK), BLOCK)
            lanes = pl.ds(i * BLOCK, BLOCK)
            for side, source in enumerate((left, sib)):
                act(
                    pltpu.make_async_copy(
                        source.at[t, :, at], left_v.at[slot, pl.ds(side * rows, rows), lanes], left_sem.at[slot, 2 * i + side]
                    )
                )

    def right_copy(t):
        return pltpu.make_async_copy(right.at[t], right_v.at[t], right_sem.at[t])

    if late:
        start, stop = 0, totals[1]
    else:
        start, stop = totals[0] * stage // stages, totals[0] * (stage + 1) // stages
    loads = []
    for i, (first, place, wide) in enumerate(places_of):
        loads.append(pltpu.make_async_copy(psi_in[i].at[pl.ds(first, wide)], psi_v.at[pl.ds(place, wide)], psi_sem.at[i]))
    for load in loads:
        load.start()
    if stage > 0:
        sums = pltpu.make_async_copy(before, acc.at[pl.ds(0, everything)], out_sem.at[0])
    first_t = pair_t[list_at + start * GROUP]
    last_t = pair_t[list_at + jnp.maximum(stop * GROUP - 1, 0)]

    @pl.when(stop > start)
    def _():
        right_copy(first_t).start()
        left_copies(start, start % 2, lambda c: c.start())

    psi_v[0] = jnp.zeros((BLOCK, BLOCK), psi_v.dtype)
    if stage > 0:
        sums.start()
        acc[pl.ds(everything, BLOCK), :] = jnp.zeros((BLOCK, acc.shape[1]), acc.dtype)
    else:
        acc[...] = jnp.zeros_like(acc)
    for load in loads:
        load.wait()
    if stage > 0:
        sums.wait()

    def one_group(g, next_t):
        slot = g % 2
        need_t = pair_t[list_at + g * GROUP + GROUP - 1]

        def one_term(t, carry):
            right_copy(t).wait()

            @pl.when(t < last_t)
            def _():
                right_copy(t + 1).start()

            return carry

        lax.fori_loop(next_t, need_t + 1, one_term, 0)

        @pl.when(g + 1 < stop)
        def _():
            left_copies(g + 1, 1 - slot, lambda c: c.start())

        w_acc[...] = jnp.zeros_like(w_acc)
        qs = [pair_q[list_at + g * GROUP + i] for i in range(GROUP)]
        ts = [pair_t[list_at + g * GROUP + i] for i in range(GROUP)]
        longest = counts[qs[0]]
        for q in qs[1:]:
            longest = jnp.maximum(longest, counts[q])

        def one_chunk(j, c1):
            for i in range(GROUP):
                at = qs[i] * lay.stride + j * CHUNK
                lhs = jnp.concatenate([psi_v[spots[at + m]] for m in range(CHUNK)], axis=1)
                rhs = jnp.concatenate(
                    [
                        right_v[ts[i], pl.ds(pl.multiple_of(blocks[at + m] * BLOCK, BLOCK), BLOCK), :]
                        for m in range(CHUNK)
                    ],
                    axis=0,
                )
                w_acc[i * BLOCK : (i + 1) * BLOCK, :] += jnp.dot(lhs, rhs, preferred_element_type=jnp.float32)
            return c1

        lax.fori_loop(0, (longest + CHUNK - 1) // CHUNK, one_chunk, 0)
        whole = w_acc[...]
        hi = whole.astype(jnp.bfloat16)
        w_hi[...] = hi
        w_lo[...] = (whole - hi.astype(jnp.float32)).astype(jnp.bfloat16)
        left_copies(g, slot, lambda c: c.wait())

        def some_items(m, c0):
            for j in range(ITEMS):
                item = m * ITEMS + j
                width = lay.tile * BLOCK
                lanes = pl.ds(pl.multiple_of(item_tile[item] * width, width), width)
                a = [lefts[2 * item + i] for i in range(2)]
                source = [pl.multiple_of(jnp.minimum(b, lay.new_left - 1) * BLOCK, BLOCK) for b in a]
                lhs = jnp.concatenate([left_v[slot, pl.ds(b, BLOCK), :] for b in source], axis=0)
                gain = jnp.dot(lhs, w_hi[:, lanes], preferred_element_type=jnp.float32)
                gain = gain + jnp.dot(lhs, w_lo[:, lanes], preferred_element_type=jnp.float32)
                for i in range(2):
                    acc[pl.ds(pl.multiple_of(a[i] * BLOCK, BLOCK), BLOCK), lanes] += gain[i * BLOCK : (i + 1) * BLOCK]
            return c0

        lax.fori_loop(0, totals[2], some_items, 0)
        return jnp.maximum(next_t, need_t + 1)

    lax.fori_loop(start, stop, one_group, first_t)
    if late:
        stores = [
            pltpu.make_async_copy(acc.at[pl.ds(rows, rows)], out_sib, out_sem.at[1]),
            pltpu.make_async_copy(acc.at[pl.ds(0, rows)], out_own, out_sem.at[0]),
        ]
    else:
        stores = [pltpu.make_async_copy(acc.at[pl.ds(0, everything)], out, out_sem.at[0])]
    for store in stores:
        store.start()
    for store in stores:
        store.wait()


def contract(lay, stage, stages, tables, right, left, sib, parts, before=None):
    late = stage == stages
    rows = lay.row_blocks * BLOCK
    cols = lay.col_blocks * BLOCK
    flat, places_of = [], []
    for (_, wide, place), part in zip(lay.runs, parts):
        for shard, array, first, count in part:
            flat.append(array)
            places_of.append((first, place + shard * wide, count))
    smem = pl.BlockSpec(memory_space=pltpu.SMEM)
    hbm = pl.BlockSpec(memory_space=pl.ANY)
    operands = [right, left, sib, *flat] + ([before] if stage > 0 else [])
    one = jax.ShapeDtypeStruct((rows, cols), jnp.float32)
    both = jax.ShapeDtypeStruct((CORES * rows, cols), jnp.float32)
    return pl.pallas_call(
        functools.partial(main_kernel, lay, stage, stages, places_of, rows),
        out_shape=[one, one] if late else both,
        in_specs=[smem] * len(tables) + [hbm] * len(operands),
        out_specs=[hbm, hbm] if late else hbm,
        scratch_shapes=[
            pltpu.VMEM(right.shape, jnp.bfloat16),
            pltpu.VMEM((lay.room(len(parts)), BLOCK, BLOCK), jnp.bfloat16),
            pltpu.VMEM((2, CORES * rows, GROUP * BLOCK), jnp.bfloat16),
            pltpu.VMEM((CORES * rows + BLOCK, cols), jnp.float32),
            pltpu.VMEM((GROUP * BLOCK, cols), jnp.bfloat16),
            pltpu.VMEM((GROUP * BLOCK, cols), jnp.bfloat16),
            pltpu.VMEM((GROUP * BLOCK, cols), jnp.float32),
            pltpu.SemaphoreType.DMA((lay.terms,)),
            pltpu.SemaphoreType.DMA((len(flat),)),
            pltpu.SemaphoreType.DMA((2, 2 * GROUP)),
            pltpu.SemaphoreType.DMA((2,)),
        ],
        compiler_params=pltpu.CompilerParams(vmem_limit_bytes=VMEM_LIMIT),
        cost_estimate=pl.CostEstimate(
            flops=2 * right.shape[0] * rows * right.shape[1] * cols, bytes_accessed=right.size * 4, transcendentals=0
        ),
        name="late_contract" if late else "early_contract",
    )(*tables, *operands)


def pack_kernel(copies, *refs):
    n_out = 1 + max(copy[3] for copy in copies)
    sources, outs, sems = refs[: -1 - n_out], refs[-1 - n_out : -1], refs[-1]
    moves = [
        pltpu.make_async_copy(sources[source].at[pl.ds(first, wide)], outs[out].at[pl.ds(at, wide)], sems.at[i])
        for i, (source, first, wide, out, at) in enumerate(copies)
    ]
    for move in moves:
        move.start()
    for move in moves:
        move.wait()


def pack(arrays, copies):
    n_out = 1 + max(copy[3] for copy in copies)
    sizes = [sum(copy[2] for copy in copies if copy[3] == out) for out in range(n_out)]
    vmem = pl.BlockSpec(memory_space=pltpu.VMEM)
    return pl.pallas_call(
        functools.partial(pack_kernel, copies),
        out_shape=[jax.ShapeDtypeStruct((size, *arrays[0].shape[1:]), arrays[0].dtype) for size in sizes],
        in_specs=[vmem] * len(arrays),
        out_specs=[vmem] * n_out,
        scratch_shapes=[pltpu.SemaphoreType.DMA((len(copies),))],
        name="pack",
    )(*arrays)


def after(array, *others):
    return lax.optimization_barrier((array, *others))[0]


class Spread:
    def __init__(self, places, part, x_own, y_own, first):
        self.places, self.part, self.wide = places, part, part.shape[0]
        self.x_own, self.y_own, self.first = x_own, y_own, first

    def over_z(self, *others):
        part = after(self.part, *others) if others else self.part
        z = self.places.z
        up, down = {0: part}, {0: part}
        for far in range(1, z // 2 + 1):
            up[far] = move(self.places, up[far - 1], dz=1)
            if far < z - far:
                down[far] = move(self.places, down[far - 1], dz=z - 1)
        self.z = [up[dz] if dz in up else down[z - dz] for dz in range(1, z)]

    def pack_z(self, *others):
        z = [after(array, *others) for array in self.z] if others else self.z
        (self.q,) = pack(z, [(i, 0, self.wide, 0, i * self.wide) for i in range(len(self.z))])
        return self.q

    def over_xy(self, *others):
        q = after(self.q, *others) if others else self.q
        self.x_line = [move(self.places, q, dx=dx) for dx in range(1, self.places.x)]
        self.y_line = [move(self.places, q, dy=dy) for dy in range(1, self.places.y)]

    def pack_rest(self, *others):
        w, half = self.wide, self.places.z // 2
        n_x, n_y = len(self.x_own), len(self.y_own)
        y_line = [after(array, *others) for array in self.y_line] if others else self.y_line
        arrays = self.x_own + self.x_line + y_line
        copies = []
        for i in range(n_x):
            copies.append((i, self.first, w, i, 0))
            if half > 1:
                copies.append((n_x + i, 0, (half - 1) * w, i, w))
        for i in range(n_y):
            copies.append((2 * n_x + i, (half - 1) * w, (self.places.z - half) * w, n_x + i, 0))
        packed = pack(arrays, copies)
        self.from_x, self.from_y = packed[:n_x], packed[n_x:]
        return self.from_x[0]

    def rest(self):
        self.rest_over_y = {
            (dy, i + 1): move(self.places, array, dy=dy)
            for i, array in enumerate(self.from_x)
            for dy in range(1, self.places.y)
        }
        self.rest_over_x = {
            (i + 1, dx): move(self.places, array, dx=dx)
            for i, array in enumerate(self.from_y)
            for dx in range(1, self.places.x)
        }
        return [*self.rest_over_y.values(), *self.rest_over_x.values()]

    def arrays(self):
        x, z, w = self.places.x, self.places.z, self.wide
        got = [(0, self.part, 0, w), (1, self.q, 0, (z - 1) * w)]
        for own, line, step in ((self.x_own, self.x_line, z), (self.y_own, self.y_line, x * z)):
            for i in range(len(own)):
                got.append(((i + 1) * step, own[i], self.first, w))
                got.append(((i + 1) * step + 1, line[i], 0, (z - 1) * w))
        for (dy, dx), array in self.rest_over_y.items():
            got.append(((dy * x + dx) * z, array, 0, array.shape[0]))
        for (dy, dx), array in self.rest_over_x.items():
            got.append(((dy * x + dx) * z + z // 2, array, 0, array.shape[0]))
        return got


def move(places, array, **step):
    return lax.ppermute(array, AXES, places.shift(**step))


def on_device(wavefunction, left_env, right_env, filled_blocks, term_columns):
    rows, cols = wavefunction.shape
    row_blocks, col_blocks = rows // BLOCK, cols // BLOCK
    places = Places(lax.axis_size("row"), lax.axis_size("col"))
    slots = row_blocks * col_blocks
    chunks = [-(-slots * 10 // 32), slots * 8 // 32]
    base = sum(chunks)
    chunks.append(slots - base)
    lay = Layout(places, row_blocks, col_blocks, left_env.shape[0], chunks)
    row_place, col_place = lax.axis_index("row"), lax.axis_index("col")

    own, part1, part2, part3 = compress(
        wavefunction, filled_blocks, [(0, base), (0, chunks[0]), (chunks[0], base), (base, slots)]
    )
    x_own = [move(places, own, dx=dx) for dx in range(1, places.x)]
    y_own = [move(places, own, dy=dy) for dy in range(1, places.y)]
    one = Spread(places, part1, x_own, y_own, 0)
    two = Spread(places, part2, x_own, y_own, chunks[0])

    one.over_z()
    one.pack_z(*x_own, *y_own)
    one.over_xy()
    two.over_z(one.q)
    swap = places.shift(dcore=1)
    sib = lax.ppermute(left_env, AXES, swap)
    tables = plan(lay, filled_blocks, term_columns)
    two.pack_z()
    one.pack_rest(two.q)
    diagonal = one.rest()
    first = one.arrays()
    two.q = after(two.q, *diagonal)
    two.over_xy()
    early = contract(lay, 0, 2, tables, after(right_env, two.q), left_env, sib, [first])
    gone = two.pack_rest(early)
    two.rest()
    early = contract(lay, 1, 2, tables, after(right_env, gone), left_env, sib, [first], early)
    second = two.arrays()

    per_device = filled_blocks.reshape(places.rows, row_blocks, places.cols, col_blocks).sum(axis=(1, 3))

    def more(_):
        three = Spread(
            places,
            part3,
            [move(places, part3, dx=dx) for dx in range(1, places.x)],
            [move(places, part3, dy=dy) for dy in range(1, places.y)],
            0,
        )
        three.over_z()
        three.pack_z()
        three.over_xy()
        three.pack_rest()
        three.rest()
        return contract(lay, 2, 2, tables, right_env, left_env, sib, [first, second, three.arrays()], early)

    def enough(_):
        return contract(lay, 2, 2, tables, right_env, left_env, sib, [first, second], early)

    own, theirs = lax.cond(jnp.max(per_device) > base, more, enough, 0)
    summed = own + lax.ppermute(theirs, AXES, swap)
    here = lax.dynamic_slice(
        filled_blocks, (row_place * row_blocks, col_place * col_blocks), (row_blocks, col_blocks)
    )
    result = jnp.where(
        here[:, None, :, None] != 0, summed.reshape(row_blocks, BLOCK, col_blocks, BLOCK), jnp.float32(0)
    )
    return result.reshape(rows, cols).astype(jnp.bfloat16)


def solution(mesh):
    in_specs = (P("row", "col"), P(None, "row", None), P(None, None, "col"), P(), P())
    out_specs = P("row", "col")
    return jax.shard_map(
        on_device, mesh=mesh, in_specs=in_specs, out_specs=out_specs, check_vma=False
    )
```

```python
import functools

import jax
import jax.numpy as jnp
from jax import lax
from jax.experimental import pallas as pl
from jax.experimental.pallas import tpu as pltpu
from jax.sharding import PartitionSpec as P

BLOCK = 128
CORES = 2
ITEMS = 2
GROUP = 8
SIDE = 4
CHUNK = 8
AXES = ("row", "col")
VMEM_LIMIT = 58 * 1024 * 1024


class Places:
    def __init__(self, row_devices, col_devices):
        self.rows, self.cols = row_devices, col_devices
        self.y = row_devices // CORES
        self.x = 1
        while self.x * self.x * 4 <= col_devices and col_devices % (self.x * 2) == 0:
            self.x *= 2
        self.z = col_devices // self.x

    def flat(self, y, core, z, x):
        return (y * CORES + core) * self.cols + z * self.x + x

    def shift(self, dy=0, dz=0, dx=0, dcore=0):
        perm = []
        for y in range(self.y):
            for core in range(CORES):
                for z in range(self.z):
                    for x in range(self.x):
                        there = self.flat(
                            (y + dy) % self.y, (core + dcore) % CORES, (z + dz) % self.z, (x + dx) % self.x
                        )
                        perm.append((self.flat(y, core, z, x), there))
        return perm


def compress_kernel(ranges, row_blocks, col_blocks, filled, psi, *rest):
    outs, sems = rest[: len(ranges)], rest[len(ranges)]
    row0 = lax.axis_index("row") * row_blocks
    col0 = lax.axis_index("col") * col_blocks

    def copy(i, slot, kb, cb):
        return pltpu.make_async_copy(
            psi.at[pl.ds(kb * BLOCK, BLOCK), pl.ds(cb * BLOCK, BLOCK)], outs[i].at[slot - ranges[i][0]], sems.at[i, slot]
        )

    count = jnp.int32(0)
    for kb in range(row_blocks):
        for cb in range(col_blocks):
            here = filled[row0 + kb, col0 + cb]
            for i, (low, high) in enumerate(ranges):
                @pl.when((here != 0) & (count >= low) & (count < high))
                def _():
                    copy(i, count, kb, cb).start()
            count = count + here
    for i, (low, high) in enumerate(ranges):
        for slot in range(low, high):
            @pl.when(slot < count)
            def _():
                copy(i, slot, 0, 0).wait()


def compress(psi, filled, ranges):
    row_blocks, col_blocks = psi.shape[0] // BLOCK, psi.shape[1] // BLOCK
    return pl.pallas_call(
        functools.partial(compress_kernel, ranges, row_blocks, col_blocks),
        out_shape=[jax.ShapeDtypeStruct((high - low, BLOCK, BLOCK), psi.dtype) for low, high in ranges],
        in_specs=[pl.BlockSpec(memory_space=pltpu.SMEM), pl.BlockSpec(memory_space=pltpu.VMEM)],
        out_specs=[pl.BlockSpec(memory_space=pltpu.VMEM)] * len(ranges),
        scratch_shapes=[pltpu.SemaphoreType.DMA((len(ranges), row_blocks * col_blocks))],
        name="compress",
    )(filled, psi)


class Layout:
    def __init__(self, places, row_blocks, col_blocks, terms, chunks):
        self.places, self.row_blocks, self.col_blocks, self.terms, self.chunks = places, row_blocks, col_blocks, terms, chunks
        self.slots = row_blocks * col_blocks
        self.states = places.y * row_blocks
        self.old_right = places.cols * col_blocks
        self.shards = places.y * places.z * places.x
        self.stride = self.old_right + CHUNK
        self.pairs = self.states * terms + GROUP
        self.tile = 2 if col_blocks % 2 == 0 else 1
        self.tiles = col_blocks // self.tile
        self.new_left = CORES * row_blocks
        self.trash = self.new_left
        self.items = self.tiles * ((self.new_left + 1) // 2) + ITEMS
        self.runs = []
        slot, place = 0, 1
        for wide in chunks:
            self.runs.append((slot, wide, place))
            slot += wide
            place += wide * self.shards

    def room(self, chunks):
        return 1 + self.shards * sum(self.chunks[:chunks])

    def shapes(self):
        return [
            (self.states + 1,),
            ((self.states + 1) * self.stride,),
            ((self.states + 1) * self.stride,),
            (2 * self.pairs,),
            (2 * self.pairs,),
            (2 * self.items,),
            (self.items,),
            (3,),
        ]


def plan_kernel(lay, filled, terms, counts, spots, blocks, pair_q, pair_t, lefts, item_tile, totals, used, ready):
    pz, px, py = lay.places.z, lay.places.x, lay.places.y
    row, col = lax.axis_index("row"), lax.axis_index("col")
    core, y_me = row % CORES, row // CORES
    z_me, x_me = col // px, col % px

    def one_state(q, n_ready):
        y = q // lay.row_blocks
        kb = q % lay.row_blocks

        @pl.when(kb == 0)
        def _():
            for dev in range(lay.places.cols):
                used[dev] = 0

        dy = (y_me - y + py) % py
        k_block = (y * CORES + core) * lay.row_blocks + kb
        n = jnp.int32(0)
        most = jnp.int32(0)
        for dev in range(lay.places.cols):
            dz = (z_me - dev // px + pz) % pz
            dx = (x_me - dev % px + px) % px
            shard = (dy * px + dx) * pz + dz
            slot = used[dev]
            for cb in range(lay.col_blocks):
                c = dev * lay.col_blocks + cb
                here = filled[k_block, c]
                spot = jnp.int32(0)
                for first, wide, place in lay.runs:
                    spot = jnp.where(slot >= first, place + shard * wide + slot - first, spot)
                spots[q * lay.stride + n] = spot
                blocks[q * lay.stride + n] = c
                n = n + here
                slot = slot + here
            used[dev] = slot
            most = jnp.maximum(most, slot)

        def pad(i, carry):
            spots[q * lay.stride + i] = 0
            blocks[q * lay.stride + i] = 0
            return carry

        lax.fori_loop(n, lay.stride, pad, 0)
        counts[q] = n
        early = jnp.where(most <= lay.chunks[0], 1, 0)
        ready[q] = early
        for t in range(lay.terms):
            n_ready = n_ready + jnp.where((terms[t, k_block] != 0) & (n > 0), early, 0)
        return n_ready

    n_ready = lax.fori_loop(0, lay.states, one_state, jnp.int32(0))
    n_ready = n_ready // GROUP * GROUP
    n_early, n_late = jnp.int32(0), jnp.int32(0)
    for t in range(lay.terms):

        def one_pair(q, carry):
            n_early, n_late = carry
            k_block = (q // lay.row_blocks * CORES + core) * lay.row_blocks + q % lay.row_blocks
            on = jnp.where((terms[t, k_block] != 0) & (counts[q] > 0), 1, 0)
            early = jnp.where((ready[q] != 0) & (n_early < n_ready), on, 0)
            at = jnp.where(early != 0, n_early, lay.pairs + n_late)
            pair_q[at] = q
            pair_t[at] = t
            return n_early + early, n_late + on - early

        n_early, n_late = lax.fori_loop(0, lay.states, one_pair, (n_early, n_late))
    counts[lay.states] = 0

    def pad_state(i, carry):
        spots[lay.states * lay.stride + i] = 0
        blocks[lay.states * lay.stride + i] = 0
        return carry

    lax.fori_loop(0, lay.stride, pad_state, 0)
    for i in range(GROUP):
        pair_q[lay.pairs + n_late + i] = lay.states
        pair_t[lay.pairs + n_late + i] = lay.terms - 1
    totals[0] = n_early // GROUP
    totals[1] = (n_late + GROUP - 1) // GROUP
    items = jnp.int32(0)
    for tile in range(lay.tiles):
        n = jnp.int32(0)
        for a in range(lay.new_left):
            side, ab = a // lay.row_blocks, a % lay.row_blocks
            a_block = (y_me * CORES + (core + side) % CORES) * lay.row_blocks + ab
            some = jnp.int32(0)
            for i in range(lay.tile):
                some = some | filled[a_block, col * lay.col_blocks + tile * lay.tile + i]
            lefts[2 * items + n] = a
            item_tile[items + n // 2] = tile
            n = n + some
        lefts[2 * items + n] = lay.trash
        items = items + (n + 1) // 2
    for i in range(ITEMS):
        lefts[2 * (items + i)] = lay.trash
        lefts[2 * (items + i) + 1] = lay.trash
        item_tile[items + i] = 0
    totals[2] = (items + ITEMS - 1) // ITEMS


def plan(lay, filled, terms):
    smem = pl.BlockSpec(memory_space=pltpu.SMEM)
    shapes = lay.shapes()
    return pl.pallas_call(
        functools.partial(plan_kernel, lay),
        out_shape=[jax.ShapeDtypeStruct(s, jnp.int32) for s in shapes],
        in_specs=[smem, smem],
        out_specs=[smem] * len(shapes),
        scratch_shapes=[pltpu.SMEM((lay.places.cols,), jnp.int32), pltpu.SMEM((lay.states,), jnp.int32)],
        name="plan",
    )(filled, terms)


def main_kernel(lay, stage, stages, places_of, rows, *refs):
    late = stage == stages
    n_psi = len(places_of)
    counts, spots, blocks, pair_q, pair_t, lefts, item_tile, totals, right, left, sib = refs[:11]
    psi_in, refs = refs[11 : 11 + n_psi], refs[11 + n_psi :]
    before = None
    if stage > 0:
        before, refs = refs[0], refs[1:]
    if late:
        (out_own, out_sib), refs = refs[:2], refs[2:]
    else:
        out, refs = refs[0], refs[1:]
    right_v, psi_v, left_v, acc, w_hi, w_lo, w_acc, right_sem, psi_sem, left_sem, out_sem = refs
    core = lax.axis_index("row") % CORES
    list_at = lay.pairs if late else 0
    everything = CORES * rows

    def left_copies(g, slot, act):
        for i in range(GROUP):
            q = jnp.minimum(pair_q[list_at + g * GROUP + i], lay.states - 1)
            t = pair_t[list_at + g * GROUP + i]
            y, kb = q // lay.row_blocks, q % lay.row_blocks
            at = pl.ds(pl.multiple_of(((y * CORES + core) * lay.row_blocks + kb) * BLOCK, BLOCK), BLOCK)
            lanes = pl.ds(i * BLOCK, BLOCK)
            for side, source in enumerate((left, sib)):
                act(
                    pltpu.make_async_copy(
                        source.at[t, :, at], left_v.at[slot, pl.ds(side * rows, rows), lanes], left_sem.at[slot, 2 * i + side]
                    )
                )

    def right_copy(t):
        return pltpu.make_async_copy(right.at[t], right_v.at[t], right_sem.at[t])

    if late:
        start, stop = 0, totals[1]
    else:
        start, stop = totals[0] * stage // stages, totals[0] * (stage + 1) // stages
    loads = []
    for i, (first, place, wide) in enumerate(places_of):
        loads.append(pltpu.make_async_copy(psi_in[i].at[pl.ds(first, wide)], psi_v.at[pl.ds(place, wide)], psi_sem.at[i]))
    for load in loads:
        load.start()
    if stage > 0:
        sums = pltpu.make_async_copy(before, acc.at[pl.ds(0, everything)], out_sem.at[0])
    first_t = pair_t[list_at + start * GROUP]
    last_t = pair_t[list_at + jnp.maximum(stop * GROUP - 1, 0)]

    @pl.when(stop > start)
    def _():
        right_copy(first_t).start()
        left_copies(start, start % 2, lambda c: c.start())

    psi_v[0] = jnp.zeros((BLOCK, BLOCK), psi_v.dtype)
    if stage > 0:
        sums.start()
        acc[pl.ds(everything, BLOCK), :] = jnp.zeros((BLOCK, acc.shape[1]), acc.dtype)
    else:
        acc[...] = jnp.zeros_like(acc)
    for load in loads:
        load.wait()

    def one_group(g, next_t):
        slot = g % 2
        need_t = pair_t[list_at + g * GROUP + GROUP - 1]

        def one_term(t, carry):
            right_copy(t).wait()

            @pl.when(t < last_t)
            def _():
                right_copy(t + 1).start()

            return carry

        lax.fori_loop(next_t, need_t + 1, one_term, 0)

        @pl.when(g + 1 < stop)
        def _():
            left_copies(g + 1, 1 - slot, lambda c: c.start())

        for low in range(0, GROUP, SIDE):
            qs = [pair_q[list_at + g * GROUP + low + i] for i in range(SIDE)]
            ts = [pair_t[list_at + g * GROUP + low + i] for i in range(SIDE)]
            longest = counts[qs[0]]
            for q in qs[1:]:
                longest = jnp.maximum(longest, counts[q])
            w_acc[...] = jnp.zeros_like(w_acc)

            def one_chunk(j, c1):
                for i in range(SIDE):
                    at = qs[i] * lay.stride + j * CHUNK
                    lhs = jnp.concatenate([psi_v[spots[at + m]] for m in range(CHUNK)], axis=1)
                    rhs = jnp.concatenate(
                        [
                            right_v[ts[i], pl.ds(pl.multiple_of(blocks[at + m] * BLOCK, BLOCK), BLOCK), :]
                            for m in range(CHUNK)
                        ],
                        axis=0,
                    )
                    w_acc[i * BLOCK : (i + 1) * BLOCK, :] += jnp.dot(lhs, rhs, preferred_element_type=jnp.float32)
                return c1

            lax.fori_loop(0, (longest + CHUNK - 1) // CHUNK, one_chunk, 0)
            whole = w_acc[...]
            hi = whole.astype(jnp.bfloat16)
            w_hi[low * BLOCK : (low + SIDE) * BLOCK, :] = hi
            w_lo[low * BLOCK : (low + SIDE) * BLOCK, :] = (whole - hi.astype(jnp.float32)).astype(jnp.bfloat16)
        left_copies(g, slot, lambda c: c.wait())
        if stage > 0:

            @pl.when(g == start)
            def _():
                sums.wait()


        def some_items(m, c0):
            for j in range(ITEMS):
                item = m * ITEMS + j
                width = lay.tile * BLOCK
                lanes = pl.ds(pl.multiple_of(item_tile[item] * width, width), width)
                a = [lefts[2 * item + i] for i in range(2)]
                source = [pl.multiple_of(jnp.minimum(b, lay.new_left - 1) * BLOCK, BLOCK) for b in a]
                lhs = jnp.concatenate([left_v[slot, pl.ds(b, BLOCK), :] for b in source], axis=0)
                gain = jnp.dot(lhs, w_hi[:, lanes], preferred_element_type=jnp.float32)
                gain = gain + jnp.dot(lhs, w_lo[:, lanes], preferred_element_type=jnp.float32)
                for i in range(2):
                    acc[pl.ds(pl.multiple_of(a[i] * BLOCK, BLOCK), BLOCK), lanes] += gain[i * BLOCK : (i + 1) * BLOCK]
            return c0

        lax.fori_loop(0, totals[2], some_items, 0)
        return jnp.maximum(next_t, need_t + 1)

    lax.fori_loop(start, stop, one_group, first_t)
    if stage > 0:

        @pl.when(stop <= start)
        def _():
            sums.wait()

    if late:
        stores = [
            pltpu.make_async_copy(acc.at[pl.ds(rows, rows)], out_sib, out_sem.at[1]),
            pltpu.make_async_copy(acc.at[pl.ds(0, rows)], out_own, out_sem.at[0]),
        ]
    else:
        stores = [pltpu.make_async_copy(acc.at[pl.ds(0, everything)], out, out_sem.at[0])]
    for store in stores:
        store.start()
    for store in stores:
        store.wait()


def contract(lay, stage, stages, tables, right, left, sib, parts, before=None):
    late = stage == stages
    rows = lay.row_blocks * BLOCK
    cols = lay.col_blocks * BLOCK
    flat, places_of = [], []
    for (_, wide, place), part in zip(lay.runs, parts):
        for shard, array, first, count in part:
            flat.append(array)
            places_of.append((first, place + shard * wide, count))
    smem = pl.BlockSpec(memory_space=pltpu.SMEM)
    hbm = pl.BlockSpec(memory_space=pl.ANY)
    operands = [right, left, sib, *flat] + ([before] if stage > 0 else [])
    one = jax.ShapeDtypeStruct((rows, cols), jnp.float32)
    both = jax.ShapeDtypeStruct((CORES * rows, cols), jnp.float32)
    return pl.pallas_call(
        functools.partial(main_kernel, lay, stage, stages, places_of, rows),
        out_shape=[one, one] if late else both,
        in_specs=[smem] * len(tables) + [hbm] * len(operands),
        out_specs=[hbm, hbm] if late else hbm,
        scratch_shapes=[
            pltpu.VMEM(right.shape, jnp.bfloat16),
            pltpu.VMEM((lay.room(len(parts)), BLOCK, BLOCK), jnp.bfloat16),
            pltpu.VMEM((2, CORES * rows, GROUP * BLOCK), jnp.bfloat16),
            pltpu.VMEM((CORES * rows + BLOCK, cols), jnp.float32),
            pltpu.VMEM((GROUP * BLOCK, cols), jnp.bfloat16),
            pltpu.VMEM((GROUP * BLOCK, cols), jnp.bfloat16),
            pltpu.VMEM((SIDE * BLOCK, cols), jnp.float32),
            pltpu.SemaphoreType.DMA((lay.terms,)),
            pltpu.SemaphoreType.DMA((len(flat),)),
            pltpu.SemaphoreType.DMA((2, 2 * GROUP)),
            pltpu.SemaphoreType.DMA((2,)),
        ],
        compiler_params=pltpu.CompilerParams(vmem_limit_bytes=VMEM_LIMIT),
        cost_estimate=pl.CostEstimate(
            flops=2 * right.shape[0] * rows * right.shape[1] * cols, bytes_accessed=right.size * 4, transcendentals=0
        ),
        name="late_contract" if late else "early_contract",
    )(*tables, *operands)


def pack_kernel(copies, *refs):
    n_out = 1 + max(copy[3] for copy in copies)
    sources, outs, sems = refs[: -1 - n_out], refs[-1 - n_out : -1], refs[-1]
    moves = [
        pltpu.make_async_copy(sources[source].at[pl.ds(first, wide)], outs[out].at[pl.ds(at, wide)], sems.at[i])
        for i, (source, first, wide, out, at) in enumerate(copies)
    ]
    for move in moves:
        move.start()
    for move in moves:
        move.wait()


def pack(arrays, copies):
    n_out = 1 + max(copy[3] for copy in copies)
    sizes = [sum(copy[2] for copy in copies if copy[3] == out) for out in range(n_out)]
    vmem = pl.BlockSpec(memory_space=pltpu.VMEM)
    return pl.pallas_call(
        functools.partial(pack_kernel, copies),
        out_shape=[jax.ShapeDtypeStruct((size, *arrays[0].shape[1:]), arrays[0].dtype) for size in sizes],
        in_specs=[vmem] * len(arrays),
        out_specs=[vmem] * n_out,
        scratch_shapes=[pltpu.SemaphoreType.DMA((len(copies),))],
        name="pack",
    )(*arrays)


def after(array, *others):
    return lax.optimization_barrier((array, *others))[0]


class Spread:
    def __init__(self, places, part, x_own, y_own, first):
        self.places, self.part, self.wide = places, part, part.shape[0]
        self.x_own, self.y_own, self.first = x_own, y_own, first

    def over_z(self, *others):
        part = after(self.part, *others) if others else self.part
        z = self.places.z
        up, down = {0: part}, {0: part}
        for far in range(1, z // 2 + 1):
            up[far] = move(self.places, up[far - 1], dz=1)
            if far < z - far:
                down[far] = move(self.places, down[far - 1], dz=z - 1)
        self.z = [up[dz] if dz in up else down[z - dz] for dz in range(1, z)]

    def pack_z(self, *others):
        z = [after(array, *others) for array in self.z] if others else self.z
        (self.q,) = pack(z, [(i, 0, self.wide, 0, i * self.wide) for i in range(len(self.z))])
        return self.q

    def over_xy(self, *others):
        q = after(self.q, *others) if others else self.q
        self.x_line = [move(self.places, q, dx=dx) for dx in range(1, self.places.x)]
        self.y_line = [move(self.places, q, dy=dy) for dy in range(1, self.places.y)]

    def pack_rest(self, *others):
        w, half = self.wide, self.places.z // 2
        n_x, n_y = len(self.x_own), len(self.y_own)
        y_line = [after(array, *others) for array in self.y_line] if others else self.y_line
        arrays = self.x_own + self.x_line + y_line
        copies = []
        for i in range(n_x):
            copies.append((i, self.first, w, i, 0))
            if half > 1:
                copies.append((n_x + i, 0, (half - 1) * w, i, w))
        for i in range(n_y):
            copies.append((2 * n_x + i, (half - 1) * w, (self.places.z - half) * w, n_x + i, 0))
        packed = pack(arrays, copies)
        self.from_x, self.from_y = packed[:n_x], packed[n_x:]
        return self.from_x[0]

    def rest(self):
        self.rest_over_y = {
            (dy, i + 1): move(self.places, array, dy=dy)
            for i, array in enumerate(self.from_x)
            for dy in range(1, self.places.y)
        }
        self.rest_over_x = {
            (i + 1, dx): move(self.places, array, dx=dx)
            for i, array in enumerate(self.from_y)
            for dx in range(1, self.places.x)
        }
        return [*self.rest_over_y.values(), *self.rest_over_x.values()]

    def arrays(self):
        x, z, w = self.places.x, self.places.z, self.wide
        got = [(0, self.part, 0, w), (1, self.q, 0, (z - 1) * w)]
        for own, line, step in ((self.x_own, self.x_line, z), (self.y_own, self.y_line, x * z)):
            for i in range(len(own)):
                got.append(((i + 1) * step, own[i], self.first, w))
                got.append(((i + 1) * step + 1, line[i], 0, (z - 1) * w))
        for (dy, dx), array in self.rest_over_y.items():
            got.append(((dy * x + dx) * z, array, 0, array.shape[0]))
        for (dy, dx), array in self.rest_over_x.items():
            got.append(((dy * x + dx) * z + z // 2, array, 0, array.shape[0]))
        return got


def move(places, array, **step):
    return lax.ppermute(array, AXES, places.shift(**step))


def on_device(wavefunction, left_env, right_env, filled_blocks, term_columns):
    rows, cols = wavefunction.shape
    row_blocks, col_blocks = rows // BLOCK, cols // BLOCK
    places = Places(lax.axis_size("row"), lax.axis_size("col"))
    slots = row_blocks * col_blocks
    chunks = [-(-slots * 10 // 32), slots * 8 // 32]
    base = sum(chunks)
    chunks.append(slots - base)
    lay = Layout(places, row_blocks, col_blocks, left_env.shape[0], chunks)
    row_place, col_place = lax.axis_index("row"), lax.axis_index("col")

    own, part1, part2, part3 = compress(
        wavefunction, filled_blocks, [(0, base), (0, chunks[0]), (chunks[0], base), (base, slots)]
    )
    x_own = [move(places, own, dx=dx) for dx in range(1, places.x)]
    y_own = [move(places, own, dy=dy) for dy in range(1, places.y)]
    one = Spread(places, part1, x_own, y_own, 0)
    two = Spread(places, part2, x_own, y_own, chunks[0])

    one.over_z()
    one.pack_z(*x_own, *y_own)
    one.over_xy()
    two.over_z(one.q)
    swap = places.shift(dcore=1)
    sib = lax.ppermute(left_env, AXES, swap)
    tables = plan(lay, filled_blocks, term_columns)
    two.pack_z()
    one.pack_rest(two.q)
    diagonal = one.rest()
    first = one.arrays()
    two.q = after(two.q, *diagonal)
    two.over_xy()
    early = contract(lay, 0, 2, tables, after(right_env, two.q), left_env, sib, [first])
    gone = two.pack_rest(early)
    two.rest()
    early = contract(lay, 1, 2, tables, after(right_env, gone), left_env, sib, [first], early)
    second = two.arrays()

    per_device = filled_blocks.reshape(places.rows, row_blocks, places.cols, col_blocks).sum(axis=(1, 3))

    def more(_):
        three = Spread(
            places,
            part3,
            [move(places, part3, dx=dx) for dx in range(1, places.x)],
            [move(places, part3, dy=dy) for dy in range(1, places.y)],
            0,
        )
        three.over_z()
        three.pack_z()
        three.over_xy()
        three.pack_rest()
        three.rest()
        return contract(lay, 2, 2, tables, right_env, left_env, sib, [first, second, three.arrays()], early)

    def enough(_):
        return contract(lay, 2, 2, tables, right_env, left_env, sib, [first, second], early)

    own, theirs = lax.cond(jnp.max(per_device) > base, more, enough, 0)
    summed = own + lax.ppermute(theirs, AXES, swap)
    here = lax.dynamic_slice(
        filled_blocks, (row_place * row_blocks, col_place * col_blocks), (row_blocks, col_blocks)
    )
    result = jnp.where(
        here[:, None, :, None] != 0, summed.reshape(row_blocks, BLOCK, col_blocks, BLOCK), jnp.float32(0)
    )
    return result.reshape(rows, cols).astype(jnp.bfloat16)


def solution(mesh):
    in_specs = (P("row", "col"), P(None, "row", None), P(None, None, "col"), P(), P())
    out_specs = P("row", "col")
    return jax.shard_map(
        on_device, mesh=mesh, in_specs=in_specs, out_specs=out_specs, check_vma=False
    )
```

```python
import functools

import jax
import jax.numpy as jnp
from jax import lax
from jax.experimental import pallas as pl
from jax.experimental.pallas import tpu as pltpu
from jax.sharding import PartitionSpec as P

BLOCK = 128
CORES = 2
ITEMS = 2
GROUP = 8
SIDE = 4
CHUNK = 8
AXES = ("row", "col")
VMEM_LIMIT = 58 * 1024 * 1024


class Places:
    def __init__(self, row_devices, col_devices):
        self.rows, self.cols = row_devices, col_devices
        self.y = row_devices // CORES
        self.x = 1
        while self.x * self.x * 4 <= col_devices and col_devices % (self.x * 2) == 0:
            self.x *= 2
        self.z = col_devices // self.x

    def flat(self, y, core, z, x):
        return (y * CORES + core) * self.cols + z * self.x + x

    def shift(self, dy=0, dz=0, dx=0, dcore=0):
        perm = []
        for y in range(self.y):
            for core in range(CORES):
                for z in range(self.z):
                    for x in range(self.x):
                        there = self.flat(
                            (y + dy) % self.y, (core + dcore) % CORES, (z + dz) % self.z, (x + dx) % self.x
                        )
                        perm.append((self.flat(y, core, z, x), there))
        return perm


def compress_kernel(ranges, row_blocks, col_blocks, filled, psi, *rest):
    outs, sems = rest[: len(ranges)], rest[len(ranges)]
    row0 = lax.axis_index("row") * row_blocks
    col0 = lax.axis_index("col") * col_blocks

    def copy(i, slot, kb, cb):
        return pltpu.make_async_copy(
            psi.at[pl.ds(kb * BLOCK, BLOCK), pl.ds(cb * BLOCK, BLOCK)], outs[i].at[slot - ranges[i][0]], sems.at[i, slot]
        )

    count = jnp.int32(0)
    for kb in range(row_blocks):
        for cb in range(col_blocks):
            here = filled[row0 + kb, col0 + cb]
            for i, (low, high) in enumerate(ranges):
                @pl.when((here != 0) & (count >= low) & (count < high))
                def _():
                    copy(i, count, kb, cb).start()
            count = count + here
    for i, (low, high) in enumerate(ranges):
        for slot in range(low, high):
            @pl.when(slot < count)
            def _():
                copy(i, slot, 0, 0).wait()


def compress(psi, filled, ranges):
    row_blocks, col_blocks = psi.shape[0] // BLOCK, psi.shape[1] // BLOCK
    return pl.pallas_call(
        functools.partial(compress_kernel, ranges, row_blocks, col_blocks),
        out_shape=[jax.ShapeDtypeStruct((high - low, BLOCK, BLOCK), psi.dtype) for low, high in ranges],
        in_specs=[pl.BlockSpec(memory_space=pltpu.SMEM), pl.BlockSpec(memory_space=pltpu.VMEM)],
        out_specs=[pl.BlockSpec(memory_space=pltpu.VMEM)] * len(ranges),
        scratch_shapes=[pltpu.SemaphoreType.DMA((len(ranges), row_blocks * col_blocks))],
        name="compress",
    )(filled, psi)


class Layout:
    def __init__(self, places, row_blocks, col_blocks, terms, chunks):
        self.places, self.row_blocks, self.col_blocks, self.terms, self.chunks = places, row_blocks, col_blocks, terms, chunks
        self.slots = row_blocks * col_blocks
        self.states = places.y * row_blocks
        self.old_right = places.cols * col_blocks
        self.shards = places.y * places.z * places.x
        self.stride = self.old_right + CHUNK
        self.pairs = self.states * terms + GROUP
        self.tile = 2 if col_blocks % 2 == 0 else 1
        self.tiles = col_blocks // self.tile
        self.new_left = CORES * row_blocks
        self.trash = self.new_left
        self.items = self.tiles * ((self.new_left + 1) // 2) + ITEMS
        self.runs = []
        slot, place = 0, 1
        for wide in chunks:
            self.runs.append((slot, wide, place))
            slot += wide
            place += wide * self.shards

        self.lengths = [
            self.states + 1,
            (self.states + 1) * self.stride,
            (self.states + 1) * self.stride,
            2 * self.pairs,
            2 * self.pairs,
            2 * self.items,
            self.items,
            self.new_left * col_blocks,
            3,
        ]

    def room(self, chunks):
        return 1 + self.shards * sum(self.chunks[:chunks])

    def lists(self, table):
        at, lists = 0, []
        for length in self.lengths:
            lists.append(List(table, at))
            at += length
        return lists


class List:
    def __init__(self, table, at):
        self.table, self.at = table, at

    def __getitem__(self, i):
        return self.table[self.at + i]

    def __setitem__(self, i, value):
        self.table[self.at + i] = jnp.int32(value)


def plan_kernel(lay, filled, terms, table, used, ready):
    counts, spots, blocks, pair_q, pair_t, lefts, item_tile, allowed, totals = lay.lists(table)
    pz, px, py = lay.places.z, lay.places.x, lay.places.y
    row, col = lax.axis_index("row"), lax.axis_index("col")
    core, y_me = row % CORES, row // CORES
    z_me, x_me = col // px, col % px

    def one_state(q, n_ready):
        y = q // lay.row_blocks
        kb = q % lay.row_blocks

        @pl.when(kb == 0)
        def _():
            for dev in range(lay.places.cols):
                used[dev] = 0

        dy = (y_me - y + py) % py
        k_block = (y * CORES + core) * lay.row_blocks + kb
        n = jnp.int32(0)
        most = jnp.int32(0)
        for dev in range(lay.places.cols):
            dz = (z_me - dev // px + pz) % pz
            dx = (x_me - dev % px + px) % px
            shard = (dy * px + dx) * pz + dz
            slot = used[dev]
            for cb in range(lay.col_blocks):
                c = dev * lay.col_blocks + cb
                here = filled[k_block, c]
                spot = jnp.int32(0)
                for first, wide, place in lay.runs:
                    spot = jnp.where(slot >= first, place + shard * wide + slot - first, spot)
                spots[q * lay.stride + n] = spot
                blocks[q * lay.stride + n] = c
                n = n + here
                slot = slot + here
            used[dev] = slot
            most = jnp.maximum(most, slot)

        def pad(i, carry):
            spots[q * lay.stride + i] = 0
            blocks[q * lay.stride + i] = 0
            return carry

        lax.fori_loop(n, lay.stride, pad, 0)
        counts[q] = n
        early = jnp.where(most <= lay.chunks[0], 1, 0)
        ready[q] = early
        for t in range(lay.terms):
            n_ready = n_ready + jnp.where((terms[t, k_block] != 0) & (n > 0), early, 0)
        return n_ready

    n_ready = lax.fori_loop(0, lay.states, one_state, jnp.int32(0))
    n_ready = n_ready // GROUP * GROUP
    n_early, n_late = jnp.int32(0), jnp.int32(0)
    for t in range(lay.terms):

        def one_pair(q, carry):
            n_early, n_late = carry
            k_block = (q // lay.row_blocks * CORES + core) * lay.row_blocks + q % lay.row_blocks
            on = jnp.where((terms[t, k_block] != 0) & (counts[q] > 0), 1, 0)
            early = jnp.where((ready[q] != 0) & (n_early < n_ready), on, 0)
            at = jnp.where(early != 0, n_early, lay.pairs + n_late)
            pair_q[at] = q
            pair_t[at] = t
            return n_early + early, n_late + on - early

        n_early, n_late = lax.fori_loop(0, lay.states, one_pair, (n_early, n_late))
    counts[lay.states] = 0

    def pad_state(i, carry):
        spots[lay.states * lay.stride + i] = 0
        blocks[lay.states * lay.stride + i] = 0
        return carry

    lax.fori_loop(0, lay.stride, pad_state, 0)
    for i in range(GROUP):
        pair_q[lay.pairs + n_late + i] = lay.states
        pair_t[lay.pairs + n_late + i] = lay.terms - 1
    totals[0] = n_early // GROUP
    totals[1] = (n_late + GROUP - 1) // GROUP
    items = jnp.int32(0)
    for tile in range(lay.tiles):
        n = jnp.int32(0)
        for a in range(lay.new_left):
            side, ab = a // lay.row_blocks, a % lay.row_blocks
            a_block = (y_me * CORES + (core + side) % CORES) * lay.row_blocks + ab
            some = jnp.int32(0)
            for i in range(lay.tile):
                here = filled[a_block, col * lay.col_blocks + tile * lay.tile + i]
                allowed[a * lay.col_blocks + tile * lay.tile + i] = here
                some = some | here
            lefts[2 * items + n] = a
            item_tile[items + n // 2] = tile
            n = n + some
        lefts[2 * items + n] = lay.trash
        items = items + (n + 1) // 2
    for i in range(ITEMS):
        lefts[2 * (items + i)] = lay.trash
        lefts[2 * (items + i) + 1] = lay.trash
        item_tile[items + i] = 0
    totals[2] = (items + ITEMS - 1) // ITEMS


def plan(lay, filled, terms):
    smem = pl.BlockSpec(memory_space=pltpu.SMEM)
    return pl.pallas_call(
        functools.partial(plan_kernel, lay),
        out_shape=jax.ShapeDtypeStruct((sum(lay.lengths),), jnp.int32),
        in_specs=[smem, smem],
        out_specs=smem,
        scratch_shapes=[pltpu.SMEM((lay.places.cols,), jnp.int32), pltpu.SMEM((lay.states,), jnp.int32)],
        name="plan",
    )(filled, terms)


def main_kernel(lay, stage, stages, places_of, rows, *refs):
    late = stage == stages
    n_psi = len(places_of)
    table, right, left, sib = refs[:4]
    counts, spots, blocks, pair_q, pair_t, lefts, item_tile, allowed, totals = lay.lists(table)
    psi_in, refs = refs[4 : 4 + n_psi], refs[4 + n_psi :]
    before = None
    if stage > 0:
        before, refs = refs[0], refs[1:]
    if late:
        (out_own, out_sib), refs = refs[:2], refs[2:]
    else:
        out, refs = refs[0], refs[1:]
    right_v, psi_v, left_v, acc, w_hi, w_lo, w_acc, right_sem, psi_sem, left_sem, out_sem = refs
    core = lax.axis_index("row") % CORES
    list_at = lay.pairs if late else 0
    everything = CORES * rows

    def left_copies(g, slot, act):
        for i in range(GROUP):
            q = jnp.minimum(pair_q[list_at + g * GROUP + i], lay.states - 1)
            t = pair_t[list_at + g * GROUP + i]
            y, kb = q // lay.row_blocks, q % lay.row_blocks
            at = pl.ds(pl.multiple_of(((y * CORES + core) * lay.row_blocks + kb) * BLOCK, BLOCK), BLOCK)
            lanes = pl.ds(i * BLOCK, BLOCK)
            for side, source in enumerate((left, sib)):
                act(
                    pltpu.make_async_copy(
                        source.at[t, :, at], left_v.at[slot, pl.ds(side * rows, rows), lanes], left_sem.at[slot, 2 * i + side]
                    )
                )

    def right_copy(t):
        return pltpu.make_async_copy(right.at[t], right_v.at[t], right_sem.at[t])

    if late:
        start, stop = 0, totals[1]
    else:
        start, stop = totals[0] * stage // stages, totals[0] * (stage + 1) // stages
    loads = []
    for i, (first, place, wide) in enumerate(places_of):
        loads.append(pltpu.make_async_copy(psi_in[i].at[pl.ds(first, wide)], psi_v.at[pl.ds(place, wide)], psi_sem.at[i]))
    for load in loads:
        load.start()
    if stage > 0:
        sums = pltpu.make_async_copy(before, acc.at[pl.ds(0, everything)], out_sem.at[0])
    first_t = pair_t[list_at + start * GROUP]
    last_t = pair_t[list_at + jnp.maximum(stop * GROUP - 1, 0)]

    @pl.when(stop > start)
    def _():
        right_copy(first_t).start()

    psi_v[0] = jnp.zeros((BLOCK, BLOCK), psi_v.dtype)
    if stage > 0:
        acc[pl.ds(everything, BLOCK), :] = jnp.zeros((BLOCK, acc.shape[1]), acc.dtype)
    else:
        acc[...] = jnp.zeros_like(acc)
    for load in loads:
        load.wait()

    @pl.when(stop > start)
    def _():
        left_copies(start, start % 2, lambda c: c.start())

    if stage > 0:
        sums.start()

    def one_group(g, next_t):
        slot = g % 2
        need_t = pair_t[list_at + g * GROUP + GROUP - 1]

        def one_term(t, carry):
            right_copy(t).wait()

            @pl.when(t < last_t)
            def _():
                right_copy(t + 1).start()

            return carry

        lax.fori_loop(next_t, need_t + 1, one_term, 0)

        @pl.when(g + 1 < stop)
        def _():
            left_copies(g + 1, 1 - slot, lambda c: c.start())

        for low in range(0, GROUP, SIDE):
            qs = [pair_q[list_at + g * GROUP + low + i] for i in range(SIDE)]
            ts = [pair_t[list_at + g * GROUP + low + i] for i in range(SIDE)]
            longest = counts[qs[0]]
            for q in qs[1:]:
                longest = jnp.maximum(longest, counts[q])
            w_acc[...] = jnp.zeros_like(w_acc)

            def one_chunk(j, c1):
                for i in range(SIDE):
                    at = qs[i] * lay.stride + j * CHUNK
                    lhs = jnp.concatenate([psi_v[spots[at + m]] for m in range(CHUNK)], axis=1)
                    rhs = jnp.concatenate(
                        [
                            right_v[ts[i], pl.ds(pl.multiple_of(blocks[at + m] * BLOCK, BLOCK), BLOCK), :]
                            for m in range(CHUNK)
                        ],
                        axis=0,
                    )
                    w_acc[i * BLOCK : (i + 1) * BLOCK, :] += jnp.dot(lhs, rhs, preferred_element_type=jnp.float32)
                return c1

            lax.fori_loop(0, (longest + CHUNK - 1) // CHUNK, one_chunk, 0)
            whole = w_acc[...]
            hi = whole.astype(jnp.bfloat16)
            w_hi[low * BLOCK : (low + SIDE) * BLOCK, :] = hi
            w_lo[low * BLOCK : (low + SIDE) * BLOCK, :] = (whole - hi.astype(jnp.float32)).astype(jnp.bfloat16)
        left_copies(g, slot, lambda c: c.wait())
        if stage > 0:

            @pl.when(g == start)
            def _():
                sums.wait()


        def some_items(m, c0):
            for j in range(ITEMS):
                item = m * ITEMS + j
                width = lay.tile * BLOCK
                lanes = pl.ds(pl.multiple_of(item_tile[item] * width, width), width)
                a = [lefts[2 * item + i] for i in range(2)]
                source = [pl.multiple_of(jnp.minimum(b, lay.new_left - 1) * BLOCK, BLOCK) for b in a]
                lhs = jnp.concatenate([left_v[slot, pl.ds(b, BLOCK), :] for b in source], axis=0)
                gain = jnp.dot(lhs, w_hi[:, lanes], preferred_element_type=jnp.float32)
                gain = gain + jnp.dot(lhs, w_lo[:, lanes], preferred_element_type=jnp.float32)
                for i in range(2):
                    acc[pl.ds(pl.multiple_of(a[i] * BLOCK, BLOCK), BLOCK), lanes] += gain[i * BLOCK : (i + 1) * BLOCK]
            return c0

        lax.fori_loop(0, totals[2], some_items, 0)
        return jnp.maximum(next_t, need_t + 1)

    lax.fori_loop(start, stop, one_group, first_t)
    if stage > 0:

        @pl.when(stop <= start)
        def _():
            sums.wait()

    if late:
        for a in range(lay.new_left):
            for cb in range(lay.col_blocks):
                @pl.when(allowed[a * lay.col_blocks + cb] == 0)
                def _():
                    acc[pl.ds(a * BLOCK, BLOCK), pl.ds(cb * BLOCK, BLOCK)] = jnp.zeros((BLOCK, BLOCK), acc.dtype)

        stores = [
            pltpu.make_async_copy(acc.at[pl.ds(rows, rows)], out_sib, out_sem.at[1]),
            pltpu.make_async_copy(acc.at[pl.ds(0, rows)], out_own, out_sem.at[0]),
        ]
    else:
        stores = [pltpu.make_async_copy(acc.at[pl.ds(0, everything)], out, out_sem.at[0])]
    for store in stores:
        store.start()
    for store in stores:
        store.wait()


def contract(lay, stage, stages, table, right, left, sib, parts, before=None):
    late = stage == stages
    rows = lay.row_blocks * BLOCK
    cols = lay.col_blocks * BLOCK
    flat, places_of = [], []
    for (_, wide, place), part in zip(lay.runs, parts):
        for shard, array, first, count in part:
            flat.append(array)
            places_of.append((first, place + shard * wide, count))
    smem = pl.BlockSpec(memory_space=pltpu.SMEM)
    hbm = pl.BlockSpec(memory_space=pl.ANY)
    operands = [right, left, sib, *flat] + ([before] if stage > 0 else [])
    one = jax.ShapeDtypeStruct((rows, cols), jnp.float32)
    both = jax.ShapeDtypeStruct((CORES * rows, cols), jnp.float32)
    return pl.pallas_call(
        functools.partial(main_kernel, lay, stage, stages, places_of, rows),
        out_shape=[one, one] if late else both,
        in_specs=[smem] + [hbm] * len(operands),
        out_specs=[hbm, hbm] if late else hbm,
        scratch_shapes=[
            pltpu.VMEM(right.shape, jnp.bfloat16),
            pltpu.VMEM((lay.room(len(parts)), BLOCK, BLOCK), jnp.bfloat16),
            pltpu.VMEM((2, CORES * rows, GROUP * BLOCK), jnp.bfloat16),
            pltpu.VMEM((CORES * rows + BLOCK, cols), jnp.float32),
            pltpu.VMEM((GROUP * BLOCK, cols), jnp.bfloat16),
            pltpu.VMEM((GROUP * BLOCK, cols), jnp.bfloat16),
            pltpu.VMEM((SIDE * BLOCK, cols), jnp.float32),
            pltpu.SemaphoreType.DMA((lay.terms,)),
            pltpu.SemaphoreType.DMA((len(flat),)),
            pltpu.SemaphoreType.DMA((2, 2 * GROUP)),
            pltpu.SemaphoreType.DMA((2,)),
        ],
        compiler_params=pltpu.CompilerParams(vmem_limit_bytes=VMEM_LIMIT),
        cost_estimate=pl.CostEstimate(
            flops=2 * right.shape[0] * rows * right.shape[1] * cols, bytes_accessed=right.size * 4, transcendentals=0
        ),
        name="late_contract" if late else "early_contract",
    )(table, *operands)


def pack_kernel(copies, *refs):
    n_out = 1 + max(copy[3] for copy in copies)
    sources, outs, sems = refs[: -1 - n_out], refs[-1 - n_out : -1], refs[-1]
    moves = [
        pltpu.make_async_copy(sources[source].at[pl.ds(first, wide)], outs[out].at[pl.ds(at, wide)], sems.at[i])
        for i, (source, first, wide, out, at) in enumerate(copies)
    ]
    for move in moves:
        move.start()
    for move in moves:
        move.wait()


def pack(arrays, copies):
    n_out = 1 + max(copy[3] for copy in copies)
    sizes = [sum(copy[2] for copy in copies if copy[3] == out) for out in range(n_out)]
    vmem = pl.BlockSpec(memory_space=pltpu.VMEM)
    return pl.pallas_call(
        functools.partial(pack_kernel, copies),
        out_shape=[jax.ShapeDtypeStruct((size, *arrays[0].shape[1:]), arrays[0].dtype) for size in sizes],
        in_specs=[vmem] * len(arrays),
        out_specs=[vmem] * n_out,
        scratch_shapes=[pltpu.SemaphoreType.DMA((len(copies),))],
        name="pack",
    )(*arrays)


def after(array, *others):
    return lax.optimization_barrier((array, *others))[0]


class Spread:
    def __init__(self, places, part, x_own, y_own, first):
        self.places, self.part, self.wide = places, part, part.shape[0]
        self.x_own, self.y_own, self.first = x_own, y_own, first

    def over_z(self, *others):
        part = after(self.part, *others) if others else self.part
        z = self.places.z
        up, down = {0: part}, {0: part}
        for far in range(1, z // 2 + 1):
            up[far] = move(self.places, up[far - 1], dz=1)
            if far < z - far:
                down[far] = move(self.places, down[far - 1], dz=z - 1)
        self.z = [up[dz] if dz in up else down[z - dz] for dz in range(1, z)]

    def pack_z(self, *others):
        z = [after(array, *others) for array in self.z] if others else self.z
        (self.q,) = pack(z, [(i, 0, self.wide, 0, i * self.wide) for i in range(len(self.z))])
        return self.q

    def over_xy(self, *others):
        q = after(self.q, *others) if others else self.q
        self.x_line = [move(self.places, q, dx=dx) for dx in range(1, self.places.x)]
        self.y_line = [move(self.places, q, dy=dy) for dy in range(1, self.places.y)]

    def pack_rest(self, *others):
        w, half = self.wide, self.places.z // 2
        n_x, n_y = len(self.x_own), len(self.y_own)
        y_line = [after(array, *others) for array in self.y_line] if others else self.y_line
        arrays = self.x_own + self.x_line + y_line
        copies = []
        for i in range(n_x):
            copies.append((i, self.first, w, i, 0))
            if half > 1:
                copies.append((n_x + i, 0, (half - 1) * w, i, w))
        for i in range(n_y):
            copies.append((2 * n_x + i, (half - 1) * w, (self.places.z - half) * w, n_x + i, 0))
        packed = pack(arrays, copies)
        self.from_x, self.from_y = packed[:n_x], packed[n_x:]
        return self.from_x[0]

    def rest(self):
        self.rest_over_y = {
            (dy, i + 1): move(self.places, array, dy=dy)
            for i, array in enumerate(self.from_x)
            for dy in range(1, self.places.y)
        }
        self.rest_over_x = {
            (i + 1, dx): move(self.places, array, dx=dx)
            for i, array in enumerate(self.from_y)
            for dx in range(1, self.places.x)
        }
        return [*self.rest_over_y.values(), *self.rest_over_x.values()]

    def arrays(self):
        x, z, w = self.places.x, self.places.z, self.wide
        got = [(0, self.part, 0, w), (1, self.q, 0, (z - 1) * w)]
        for own, line, step in ((self.x_own, self.x_line, z), (self.y_own, self.y_line, x * z)):
            for i in range(len(own)):
                got.append(((i + 1) * step, own[i], self.first, w))
                got.append(((i + 1) * step + 1, line[i], 0, (z - 1) * w))
        for (dy, dx), array in self.rest_over_y.items():
            got.append(((dy * x + dx) * z, array, 0, array.shape[0]))
        for (dy, dx), array in self.rest_over_x.items():
            got.append(((dy * x + dx) * z + z // 2, array, 0, array.shape[0]))
        return got


def move(places, array, **step):
    return lax.ppermute(array, AXES, places.shift(**step))


def on_device(wavefunction, left_env, right_env, filled_blocks, term_columns):
    rows, cols = wavefunction.shape
    row_blocks, col_blocks = rows // BLOCK, cols // BLOCK
    places = Places(lax.axis_size("row"), lax.axis_size("col"))
    slots = row_blocks * col_blocks
    chunks = [-(-slots * 10 // 32), -(-slots * 10 // 32), slots * 4 // 32]
    base = chunks[0] + chunks[1]
    chunks.append(slots - sum(chunks))
    lay = Layout(places, row_blocks, col_blocks, left_env.shape[0], chunks)

    own, part1, part2 = compress(wavefunction, filled_blocks, [(0, base), (0, chunks[0]), (chunks[0], base)])
    x_own = [move(places, own, dx=dx) for dx in range(1, places.x)]
    y_own = [move(places, own, dy=dy) for dy in range(1, places.y)]
    one = Spread(places, part1, x_own, y_own, 0)
    two = Spread(places, part2, x_own, y_own, chunks[0])
    swap = places.shift(dcore=1)
    sib = lax.ppermute(left_env, AXES, swap)
    table = plan(lay, filled_blocks, term_columns)
    most = jnp.max(filled_blocks.reshape(places.rows, row_blocks, places.cols, col_blocks).sum(axis=(1, 3)))

    one.over_z()
    one.pack_z(*x_own, *y_own)
    one.q, table, most = lax.optimization_barrier((one.q, table, most))
    one.over_xy()
    two.over_z(one.q)
    two.pack_z()
    one.pack_rest(two.q)
    diagonal = one.rest()
    first = one.arrays()
    two.q = after(two.q, *diagonal)
    two.over_xy()
    early = contract(lay, 0, 2, table, after(right_env, two.q), left_env, sib, [first])
    gone = two.pack_rest(early)
    two.rest()
    early = contract(lay, 1, 2, table, after(right_env, gone), left_env, sib, [first], early)
    second = two.arrays()

    def finish(extra, _):
        low, parts = base, [first, second]
        for wide in chunks[2 : 2 + extra]:
            (part,) = compress(wavefunction, filled_blocks, [(low, low + wide)])
            more = Spread(
                places,
                part,
                [move(places, part, dx=dx) for dx in range(1, places.x)],
                [move(places, part, dy=dy) for dy in range(1, places.y)],
                0,
            )
            more.over_z()
            more.pack_z()
            more.over_xy()
            more.pack_rest()
            more.rest()
            parts.append(more.arrays())
            low += wide
        return contract(lay, 2, 2, table, right_env, left_env, sib, parts, early)

    levels = jnp.where(most > base, 1, 0) + jnp.where(most > base + chunks[2], 1, 0)
    own, theirs = lax.switch(levels, [functools.partial(finish, extra) for extra in range(3)], 0)
    return (own + lax.ppermute(theirs, AXES, swap)).astype(jnp.bfloat16)


def solution(mesh):
    in_specs = (P("row", "col"), P(None, "row", None), P(None, None, "col"), P(), P())
    out_specs = P("row", "col")
    return jax.shard_map(
        on_device, mesh=mesh, in_specs=in_specs, out_specs=out_specs, check_vma=False
    )
```

```python
import functools

import jax
import jax.numpy as jnp
from jax import lax
from jax.experimental import pallas as pl
from jax.experimental.pallas import tpu as pltpu
from jax.sharding import PartitionSpec as P

BLOCK = 128
CORES = 2
ITEMS = 2
GROUP = 8
SIDE = 4
CHUNK = 8
AXES = ("row", "col")
VMEM_LIMIT = 58 * 1024 * 1024


class Places:
    def __init__(self, row_devices, col_devices):
        self.rows, self.cols = row_devices, col_devices
        self.y = row_devices // CORES
        self.x = 1
        while self.x * self.x * 4 <= col_devices and col_devices % (self.x * 2) == 0:
            self.x *= 2
        self.z = col_devices // self.x

    def flat(self, y, core, z, x):
        return (y * CORES + core) * self.cols + z * self.x + x

    def shift(self, dy=0, dz=0, dx=0, dcore=0):
        perm = []
        for y in range(self.y):
            for core in range(CORES):
                for z in range(self.z):
                    for x in range(self.x):
                        there = self.flat(
                            (y + dy) % self.y, (core + dcore) % CORES, (z + dz) % self.z, (x + dx) % self.x
                        )
                        perm.append((self.flat(y, core, z, x), there))
        return perm


def compress_kernel(ranges, row_blocks, col_blocks, filled, psi, *rest):
    outs, sems = rest[: len(ranges)], rest[len(ranges)]
    row0 = lax.axis_index("row") * row_blocks
    col0 = lax.axis_index("col") * col_blocks

    def copy(i, slot, kb, cb):
        return pltpu.make_async_copy(
            psi.at[pl.ds(kb * BLOCK, BLOCK), pl.ds(cb * BLOCK, BLOCK)], outs[i].at[slot - ranges[i][0]], sems.at[i, slot]
        )

    count = jnp.int32(0)
    for kb in range(row_blocks):
        for cb in range(col_blocks):
            here = filled[row0 + kb, col0 + cb]
            for i, (low, high) in enumerate(ranges):
                @pl.when((here != 0) & (count >= low) & (count < high))
                def _():
                    copy(i, count, kb, cb).start()
            count = count + here
    for i, (low, high) in enumerate(ranges):
        for slot in range(low, high):
            @pl.when(slot < count)
            def _():
                copy(i, slot, 0, 0).wait()


def compress(psi, filled, ranges):
    row_blocks, col_blocks = psi.shape[0] // BLOCK, psi.shape[1] // BLOCK
    return pl.pallas_call(
        functools.partial(compress_kernel, ranges, row_blocks, col_blocks),
        out_shape=[jax.ShapeDtypeStruct((high - low, BLOCK, BLOCK), psi.dtype) for low, high in ranges],
        in_specs=[pl.BlockSpec(memory_space=pltpu.SMEM), pl.BlockSpec(memory_space=pltpu.VMEM)],
        out_specs=[pl.BlockSpec(memory_space=pltpu.VMEM)] * len(ranges),
        scratch_shapes=[pltpu.SemaphoreType.DMA((len(ranges), row_blocks * col_blocks))],
        name="compress",
    )(filled, psi)


class Layout:
    def __init__(self, places, row_blocks, col_blocks, terms, chunks):
        self.places, self.row_blocks, self.col_blocks, self.terms, self.chunks = places, row_blocks, col_blocks, terms, chunks
        self.slots = row_blocks * col_blocks
        self.states = places.y * row_blocks
        self.old_right = places.cols * col_blocks
        self.shards = places.y * places.z * places.x
        self.stride = self.old_right + CHUNK
        self.pairs = self.states * terms + GROUP
        self.tile = 2 if col_blocks % 2 == 0 else 1
        self.tiles = col_blocks // self.tile
        self.new_left = CORES * row_blocks
        self.trash = self.new_left
        self.items = self.tiles * ((self.new_left + 1) // 2) + ITEMS
        self.runs = []
        slot, place = 0, 1
        for wide in chunks:
            self.runs.append((slot, wide, place))
            slot += wide
            place += wide * self.shards

        self.lengths = [
            self.states + 1,
            (self.states + 1) * self.stride,
            (self.states + 1) * self.stride,
            2 * self.pairs,
            2 * self.pairs,
            2 * self.items,
            self.items,
            self.new_left * col_blocks,
            3,
        ]

    def room(self, chunks):
        return 1 + self.shards * sum(self.chunks[:chunks])

    def lists(self, table):
        at, lists = 0, []
        for length in self.lengths:
            lists.append(List(table, at))
            at += length
        return lists


class List:
    def __init__(self, table, at):
        self.table, self.at = table, at

    def __getitem__(self, i):
        return self.table[self.at + i]

    def __setitem__(self, i, value):
        self.table[self.at + i] = jnp.int32(value)


def plan_kernel(lay, filled, terms, table, used, ready):
    counts, spots, blocks, pair_q, pair_t, lefts, item_tile, allowed, totals = lay.lists(table)
    pz, px, py = lay.places.z, lay.places.x, lay.places.y
    row, col = lax.axis_index("row"), lax.axis_index("col")
    core, y_me = row % CORES, row // CORES
    z_me, x_me = col // px, col % px

    def one_state(q, n_ready):
        y = q // lay.row_blocks
        kb = q % lay.row_blocks

        @pl.when(kb == 0)
        def _():
            for dev in range(lay.places.cols):
                used[dev] = 0

        dy = (y_me - y + py) % py
        k_block = (y * CORES + core) * lay.row_blocks + kb
        n = jnp.int32(0)
        for dev in range(lay.places.cols):
            dz = (z_me - dev // px + pz) % pz
            dx = (x_me - dev % px + px) % px
            shard = (dy * px + dx) * pz + dz
            slot = used[dev]
            for cb in range(lay.col_blocks):
                c = dev * lay.col_blocks + cb
                here = filled[k_block, c]
                spot = jnp.int32(0)
                for first, wide, place in lay.runs:
                    spot = jnp.where(slot >= first, place + shard * wide + slot - first, spot)
                spots[q * lay.stride + n] = spot
                blocks[q * lay.stride + n] = c
                n = n + here
                slot = slot + here
            used[dev] = slot

        def pad(i, carry):
            spots[q * lay.stride + i] = 0
            blocks[q * lay.stride + i] = 0
            return carry

        lax.fori_loop(n, lay.stride, pad, 0)
        counts[q] = n
        early = jnp.where(y == y_me, 1, 0)
        ready[q] = early
        for t in range(lay.terms):
            n_ready = n_ready + jnp.where((terms[t, k_block] != 0) & (n > 0), early, 0)
        return n_ready

    n_ready = lax.fori_loop(0, lay.states, one_state, jnp.int32(0))
    n_ready = n_ready // GROUP * GROUP
    n_early, n_late = jnp.int32(0), jnp.int32(0)
    for t in range(lay.terms):

        def one_pair(q, carry):
            n_early, n_late = carry
            k_block = (q // lay.row_blocks * CORES + core) * lay.row_blocks + q % lay.row_blocks
            on = jnp.where((terms[t, k_block] != 0) & (counts[q] > 0), 1, 0)
            early = jnp.where((ready[q] != 0) & (n_early < n_ready), on, 0)
            at = jnp.where(early != 0, n_early, lay.pairs + n_late)
            pair_q[at] = q
            pair_t[at] = t
            return n_early + early, n_late + on - early

        n_early, n_late = lax.fori_loop(0, lay.states, one_pair, (n_early, n_late))
    counts[lay.states] = 0

    def pad_state(i, carry):
        spots[lay.states * lay.stride + i] = 0
        blocks[lay.states * lay.stride + i] = 0
        return carry

    lax.fori_loop(0, lay.stride, pad_state, 0)
    for i in range(GROUP):
        pair_q[lay.pairs + n_late + i] = lay.states
        pair_t[lay.pairs + n_late + i] = lay.terms - 1
    totals[0] = n_early // GROUP
    totals[1] = (n_late + GROUP - 1) // GROUP
    items = jnp.int32(0)
    for tile in range(lay.tiles):
        n = jnp.int32(0)
        for a in range(lay.new_left):
            side, ab = a // lay.row_blocks, a % lay.row_blocks
            a_block = (y_me * CORES + (core + side) % CORES) * lay.row_blocks + ab
            some = jnp.int32(0)
            for i in range(lay.tile):
                here = filled[a_block, col * lay.col_blocks + tile * lay.tile + i]
                allowed[a * lay.col_blocks + tile * lay.tile + i] = here
                some = some | here
            lefts[2 * items + n] = a
            item_tile[items + n // 2] = tile
            n = n + some
        lefts[2 * items + n] = lay.trash
        items = items + (n + 1) // 2
    for i in range(ITEMS):
        lefts[2 * (items + i)] = lay.trash
        lefts[2 * (items + i) + 1] = lay.trash
        item_tile[items + i] = 0
    totals[2] = (items + ITEMS - 1) // ITEMS


def plan(lay, filled, terms):
    smem = pl.BlockSpec(memory_space=pltpu.SMEM)
    return pl.pallas_call(
        functools.partial(plan_kernel, lay),
        out_shape=jax.ShapeDtypeStruct((sum(lay.lengths),), jnp.int32),
        in_specs=[smem, smem],
        out_specs=smem,
        scratch_shapes=[pltpu.SMEM((lay.places.cols,), jnp.int32), pltpu.SMEM((lay.states,), jnp.int32)],
        name="plan",
    )(filled, terms)


def main_kernel(lay, stage, stages, places_of, rows, *refs):
    late = stage == stages
    n_psi = len(places_of)
    table, right, left, sib = refs[:4]
    counts, spots, blocks, pair_q, pair_t, lefts, item_tile, allowed, totals = lay.lists(table)
    psi_in, refs = refs[4 : 4 + n_psi], refs[4 + n_psi :]
    before = None
    if stage > 0:
        before, refs = refs[0], refs[1:]
    if late:
        (out_own, out_sib), refs = refs[:2], refs[2:]
    else:
        out, refs = refs[0], refs[1:]
    right_v, psi_v, left_v, acc, w_hi, w_lo, w_acc, right_sem, psi_sem, left_sem, out_sem = refs
    core = lax.axis_index("row") % CORES
    list_at = lay.pairs if late else 0
    everything = CORES * rows

    def left_copies(g, slot, act):
        for i in range(GROUP):
            q = jnp.minimum(pair_q[list_at + g * GROUP + i], lay.states - 1)
            t = pair_t[list_at + g * GROUP + i]
            y, kb = q // lay.row_blocks, q % lay.row_blocks
            at = pl.ds(pl.multiple_of(((y * CORES + core) * lay.row_blocks + kb) * BLOCK, BLOCK), BLOCK)
            lanes = pl.ds(i * BLOCK, BLOCK)
            for side, source in enumerate((left, sib)):
                act(
                    pltpu.make_async_copy(
                        source.at[t, :, at], left_v.at[slot, pl.ds(side * rows, rows), lanes], left_sem.at[slot, 2 * i + side]
                    )
                )

    def right_copy(t):
        return pltpu.make_async_copy(right.at[t], right_v.at[t], right_sem.at[t])

    if late:
        start, stop = 0, totals[1]
    else:
        start, stop = totals[0] * stage // stages, totals[0] * (stage + 1) // stages
    loads = []
    for i, (first, place, wide) in enumerate(places_of):
        loads.append(pltpu.make_async_copy(psi_in[i].at[pl.ds(first, wide)], psi_v.at[pl.ds(place, wide)], psi_sem.at[i]))
    for load in loads:
        load.start()
    if stage > 0:
        sums = pltpu.make_async_copy(before, acc.at[pl.ds(0, everything)], out_sem.at[0])
    first_t = pair_t[list_at + start * GROUP]
    last_t = pair_t[list_at + jnp.maximum(stop * GROUP - 1, 0)]

    @pl.when(stop > start)
    def _():
        right_copy(first_t).start()

    psi_v[0] = jnp.zeros((BLOCK, BLOCK), psi_v.dtype)
    if stage > 0:
        acc[pl.ds(everything, BLOCK), :] = jnp.zeros((BLOCK, acc.shape[1]), acc.dtype)
    else:
        acc[...] = jnp.zeros_like(acc)
    for load in loads:
        load.wait()

    @pl.when(stop > start)
    def _():
        left_copies(start, start % 2, lambda c: c.start())

    if stage > 0:
        sums.start()

    def one_group(g, next_t):
        slot = g % 2
        need_t = pair_t[list_at + g * GROUP + GROUP - 1]

        def one_term(t, carry):
            right_copy(t).wait()

            @pl.when(t < last_t)
            def _():
                right_copy(t + 1).start()

            return carry

        lax.fori_loop(next_t, need_t + 1, one_term, 0)

        @pl.when(g + 1 < stop)
        def _():
            left_copies(g + 1, 1 - slot, lambda c: c.start())

        for low in range(0, GROUP, SIDE):
            qs = [pair_q[list_at + g * GROUP + low + i] for i in range(SIDE)]
            ts = [pair_t[list_at + g * GROUP + low + i] for i in range(SIDE)]
            longest = counts[qs[0]]
            for q in qs[1:]:
                longest = jnp.maximum(longest, counts[q])
            w_acc[...] = jnp.zeros_like(w_acc)

            def one_chunk(j, c1):
                for i in range(SIDE):
                    at = qs[i] * lay.stride + j * CHUNK
                    lhs = jnp.concatenate([psi_v[spots[at + m]] for m in range(CHUNK)], axis=1)
                    rhs = jnp.concatenate(
                        [
                            right_v[ts[i], pl.ds(pl.multiple_of(blocks[at + m] * BLOCK, BLOCK), BLOCK), :]
                            for m in range(CHUNK)
                        ],
                        axis=0,
                    )
                    w_acc[i * BLOCK : (i + 1) * BLOCK, :] += jnp.dot(lhs, rhs, preferred_element_type=jnp.float32)
                return c1

            lax.fori_loop(0, (longest + CHUNK - 1) // CHUNK, one_chunk, 0)
            whole = w_acc[...]
            hi = whole.astype(jnp.bfloat16)
            w_hi[low * BLOCK : (low + SIDE) * BLOCK, :] = hi
            w_lo[low * BLOCK : (low + SIDE) * BLOCK, :] = (whole - hi.astype(jnp.float32)).astype(jnp.bfloat16)
        left_copies(g, slot, lambda c: c.wait())
        if stage > 0:

            @pl.when(g == start)
            def _():
                sums.wait()


        def some_items(m, c0):
            for j in range(ITEMS):
                item = m * ITEMS + j
                width = lay.tile * BLOCK
                lanes = pl.ds(pl.multiple_of(item_tile[item] * width, width), width)
                a = [lefts[2 * item + i] for i in range(2)]
                source = [pl.multiple_of(jnp.minimum(b, lay.new_left - 1) * BLOCK, BLOCK) for b in a]
                lhs = jnp.concatenate([left_v[slot, pl.ds(b, BLOCK), :] for b in source], axis=0)
                gain = jnp.dot(lhs, w_hi[:, lanes], preferred_element_type=jnp.float32)
                gain = gain + jnp.dot(lhs, w_lo[:, lanes], preferred_element_type=jnp.float32)
                for i in range(2):
                    acc[pl.ds(pl.multiple_of(a[i] * BLOCK, BLOCK), BLOCK), lanes] += gain[i * BLOCK : (i + 1) * BLOCK]
            return c0

        lax.fori_loop(0, totals[2], some_items, 0)
        return jnp.maximum(next_t, need_t + 1)

    lax.fori_loop(start, stop, one_group, first_t)
    if stage > 0:

        @pl.when(stop <= start)
        def _():
            sums.wait()

    if late:
        for a in range(lay.new_left):
            for cb in range(lay.col_blocks):
                @pl.when(allowed[a * lay.col_blocks + cb] == 0)
                def _():
                    acc[pl.ds(a * BLOCK, BLOCK), pl.ds(cb * BLOCK, BLOCK)] = jnp.zeros((BLOCK, BLOCK), acc.dtype)

        stores = [
            pltpu.make_async_copy(acc.at[pl.ds(rows, rows)], out_sib, out_sem.at[1]),
            pltpu.make_async_copy(acc.at[pl.ds(0, rows)], out_own, out_sem.at[0]),
        ]
    else:
        stores = [pltpu.make_async_copy(acc.at[pl.ds(0, everything)], out, out_sem.at[0])]
    for store in stores:
        store.start()
    for store in stores:
        store.wait()


def contract(lay, stage, stages, table, right, left, sib, parts, before=None):
    late = stage == stages
    rows = lay.row_blocks * BLOCK
    cols = lay.col_blocks * BLOCK
    flat, places_of = [], []
    for (_, wide, place), part in zip(lay.runs, parts):
        for shard, array, first, count in part:
            flat.append(array)
            places_of.append((first, place + shard * wide, count))
    smem = pl.BlockSpec(memory_space=pltpu.SMEM)
    hbm = pl.BlockSpec(memory_space=pl.ANY)
    operands = [right, left, sib, *flat] + ([before] if stage > 0 else [])
    one = jax.ShapeDtypeStruct((rows, cols), jnp.float32)
    both = jax.ShapeDtypeStruct((CORES * rows, cols), jnp.float32)
    return pl.pallas_call(
        functools.partial(main_kernel, lay, stage, stages, places_of, rows),
        out_shape=[one, one] if late else both,
        in_specs=[smem] + [hbm] * len(operands),
        out_specs=[hbm, hbm] if late else hbm,
        scratch_shapes=[
            pltpu.VMEM(right.shape, jnp.bfloat16),
            pltpu.VMEM((lay.room(len(parts)), BLOCK, BLOCK), jnp.bfloat16),
            pltpu.VMEM((2, CORES * rows, GROUP * BLOCK), jnp.bfloat16),
            pltpu.VMEM((CORES * rows + BLOCK, cols), jnp.float32),
            pltpu.VMEM((GROUP * BLOCK, cols), jnp.bfloat16),
            pltpu.VMEM((GROUP * BLOCK, cols), jnp.bfloat16),
            pltpu.VMEM((SIDE * BLOCK, cols), jnp.float32),
            pltpu.SemaphoreType.DMA((lay.terms,)),
            pltpu.SemaphoreType.DMA((len(flat),)),
            pltpu.SemaphoreType.DMA((2, 2 * GROUP)),
            pltpu.SemaphoreType.DMA((2,)),
        ],
        compiler_params=pltpu.CompilerParams(vmem_limit_bytes=VMEM_LIMIT),
        cost_estimate=pl.CostEstimate(
            flops=2 * right.shape[0] * rows * right.shape[1] * cols, bytes_accessed=right.size * 4, transcendentals=0
        ),
        name="late_contract" if late else "early_contract",
    )(table, *operands)


def pack_kernel(copies, *refs):
    n_out = 1 + max(copy[3] for copy in copies)
    sources, outs, sems = refs[: -1 - n_out], refs[-1 - n_out : -1], refs[-1]
    moves = [
        pltpu.make_async_copy(sources[source].at[pl.ds(first, wide)], outs[out].at[pl.ds(at, wide)], sems.at[i])
        for i, (source, first, wide, out, at) in enumerate(copies)
    ]
    for move in moves:
        move.start()
    for move in moves:
        move.wait()


def pack(arrays, copies):
    n_out = 1 + max(copy[3] for copy in copies)
    sizes = [sum(copy[2] for copy in copies if copy[3] == out) for out in range(n_out)]
    vmem = pl.BlockSpec(memory_space=pltpu.VMEM)
    return pl.pallas_call(
        functools.partial(pack_kernel, copies),
        out_shape=[jax.ShapeDtypeStruct((size, *arrays[0].shape[1:]), arrays[0].dtype) for size in sizes],
        in_specs=[vmem] * len(arrays),
        out_specs=[vmem] * n_out,
        scratch_shapes=[pltpu.SemaphoreType.DMA((len(copies),))],
        name="pack",
    )(*arrays)


def after(array, *others):
    return lax.optimization_barrier((array, *others))[0]


class Spread:
    def __init__(self, places, part, x_own, y_own, first):
        self.places, self.part, self.wide = places, part, part.shape[0]
        self.x_own, self.y_own, self.first = x_own, y_own, first

    def over_z(self, *others):
        part = after(self.part, *others) if others else self.part
        z = self.places.z
        up, down = {0: part}, {0: part}
        for far in range(1, z // 2 + 1):
            up[far] = move(self.places, up[far - 1], dz=1)
            if far < z - far:
                down[far] = move(self.places, down[far - 1], dz=z - 1)
        self.z = [up[dz] if dz in up else down[z - dz] for dz in range(1, z)]

    def pack_z(self, *others):
        z = [after(array, *others) for array in self.z] if others else self.z
        (self.q,) = pack(z, [(i, 0, self.wide, 0, i * self.wide) for i in range(len(self.z))])
        return self.q

    def over_xy(self, *others):
        q = after(self.q, *others) if others else self.q
        self.x_line = [move(self.places, q, dx=dx) for dx in range(1, self.places.x)]
        self.y_line = [move(self.places, q, dy=dy) for dy in range(1, self.places.y)]

    def pack_rest(self, *others):
        w, half = self.wide, self.places.z // 2
        n_x, n_y = len(self.x_own), len(self.y_own)
        y_line = [after(array, *others) for array in self.y_line] if others else self.y_line
        arrays = self.x_own + self.x_line + y_line
        copies = []
        for i in range(n_x):
            copies.append((i, self.first, w, i, 0))
            if half > 1:
                copies.append((n_x + i, 0, (half - 1) * w, i, w))
        for i in range(n_y):
            copies.append((2 * n_x + i, (half - 1) * w, (self.places.z - half) * w, n_x + i, 0))
        packed = pack(arrays, copies)
        self.from_x, self.from_y = packed[:n_x], packed[n_x:]
        return self.from_x[0]

    def rest(self):
        self.rest_over_y = {
            (dy, i + 1): move(self.places, array, dy=dy)
            for i, array in enumerate(self.from_x)
            for dy in range(1, self.places.y)
        }
        self.rest_over_x = {
            (i + 1, dx): move(self.places, array, dx=dx)
            for i, array in enumerate(self.from_y)
            for dx in range(1, self.places.x)
        }
        return [*self.rest_over_y.values(), *self.rest_over_x.values()]

    def own_y(self):
        z, w = self.places.z, self.wide
        got = [(0, self.part, 0, w), (1, self.q, 0, (z - 1) * w)]
        for i in range(len(self.x_own)):
            got.append(((i + 1) * z, self.x_own[i], self.first, w))
            got.append(((i + 1) * z + 1, self.x_line[i], 0, (z - 1) * w))
        return got

    def arrays(self):
        x, z, w = self.places.x, self.places.z, self.wide
        got = self.own_y()
        for i in range(len(self.y_own)):
            got.append(((i + 1) * x * z, self.y_own[i], self.first, w))
            got.append(((i + 1) * x * z + 1, self.y_line[i], 0, (z - 1) * w))
        for (dy, dx), array in self.rest_over_y.items():
            got.append(((dy * x + dx) * z, array, 0, array.shape[0]))
        for (dy, dx), array in self.rest_over_x.items():
            got.append(((dy * x + dx) * z + z // 2, array, 0, array.shape[0]))
        return got


def move(places, array, **step):
    return lax.ppermute(array, AXES, places.shift(**step))


def on_device(wavefunction, left_env, right_env, filled_blocks, term_columns):
    rows, cols = wavefunction.shape
    row_blocks, col_blocks = rows // BLOCK, cols // BLOCK
    places = Places(lax.axis_size("row"), lax.axis_size("col"))
    slots = row_blocks * col_blocks
    chunks = [-(-slots * 10 // 32), -(-slots * 10 // 32), slots * 4 // 32]
    base = chunks[0] + chunks[1]
    chunks.append(slots - sum(chunks))
    lay = Layout(places, row_blocks, col_blocks, left_env.shape[0], chunks)

    own, part1, part2 = compress(wavefunction, filled_blocks, [(0, base), (0, chunks[0]), (chunks[0], base)])
    x_own = [move(places, own, dx=dx) for dx in range(1, places.x)]
    y_own = [move(places, own, dy=dy) for dy in range(1, places.y)]
    one = Spread(places, part1, x_own, y_own, 0)
    two = Spread(places, part2, x_own, y_own, chunks[0])
    swap = places.shift(dcore=1)
    sib = lax.ppermute(left_env, AXES, swap)
    table = plan(lay, filled_blocks, term_columns)
    most = jnp.max(filled_blocks.reshape(places.rows, row_blocks, places.cols, col_blocks).sum(axis=(1, 3)))

    one.over_z()
    one.pack_z(*x_own, *y_own)
    one.q, table, most = lax.optimization_barrier((one.q, table, most))
    one.over_xy()
    two.over_z(one.q)
    two.pack_z(*one.x_line, *one.y_line)
    two.over_xy()
    gone = [one.pack_rest(*two.x_line, *two.y_line), two.pack_rest()]
    first, second = one.own_y(), two.own_y()
    early = contract(lay, 0, 1, table, after(right_env, *gone), left_env, sib, [first, second])
    one.rest()
    two.rest()
    first, second = one.arrays(), two.arrays()

    def finish(extra, _):
        low, parts = base, [first, second]
        for wide in chunks[2 : 2 + extra]:
            (part,) = compress(wavefunction, filled_blocks, [(low, low + wide)])
            more = Spread(
                places,
                part,
                [move(places, part, dx=dx) for dx in range(1, places.x)],
                [move(places, part, dy=dy) for dy in range(1, places.y)],
                0,
            )
            more.over_z()
            more.pack_z()
            more.over_xy()
            more.pack_rest()
            more.rest()
            parts.append(more.arrays())
            low += wide
        return contract(lay, 1, 1, table, right_env, left_env, sib, parts, early)

    levels = jnp.where(most > base, 1, 0) + jnp.where(most > base + chunks[2], 1, 0)
    own, theirs = lax.switch(levels, [functools.partial(finish, extra) for extra in range(3)], 0)
    return (own + lax.ppermute(theirs, AXES, swap)).astype(jnp.bfloat16)


def solution(mesh):
    in_specs = (P("row", "col"), P(None, "row", None), P(None, None, "col"), P(), P())
    out_specs = P("row", "col")
    return jax.shard_map(
        on_device, mesh=mesh, in_specs=in_specs, out_specs=out_specs, check_vma=False
    )
```

```python
import functools

import jax
import jax.numpy as jnp
from jax import lax
from jax.experimental import pallas as pl
from jax.experimental.pallas import tpu as pltpu
from jax.sharding import PartitionSpec as P

BLOCK = 128
CORES = 2
STAGES = 3
ITEMS = 2
GROUP = 8
SIDE = 4
CHUNK = 8
AXES = ("row", "col")
VMEM_LIMIT = 58 * 1024 * 1024


class Places:
    def __init__(self, row_devices, col_devices):
        self.rows, self.cols = row_devices, col_devices
        self.y = row_devices // CORES
        self.x = 1
        while self.x * self.x * 4 <= col_devices and col_devices % (self.x * 2) == 0:
            self.x *= 2
        self.z = col_devices // self.x

    def flat(self, y, core, z, x):
        return (y * CORES + core) * self.cols + z * self.x + x

    def shift(self, dy=0, dz=0, dx=0, dcore=0):
        perm = []
        for y in range(self.y):
            for core in range(CORES):
                for z in range(self.z):
                    for x in range(self.x):
                        there = self.flat(
                            (y + dy) % self.y, (core + dcore) % CORES, (z + dz) % self.z, (x + dx) % self.x
                        )
                        perm.append((self.flat(y, core, z, x), there))
        return perm


def compress_kernel(ranges, row_blocks, col_blocks, filled, psi, *rest):
    outs, sems = rest[: len(ranges)], rest[len(ranges)]
    row0 = lax.axis_index("row") * row_blocks
    col0 = lax.axis_index("col") * col_blocks

    def copy(i, slot, kb, cb):
        return pltpu.make_async_copy(
            psi.at[pl.ds(kb * BLOCK, BLOCK), pl.ds(cb * BLOCK, BLOCK)], outs[i].at[slot - ranges[i][0]], sems.at[i, slot]
        )

    count = jnp.int32(0)
    for kb in range(row_blocks):
        for cb in range(col_blocks):
            here = filled[row0 + kb, col0 + cb]
            for i, (low, high) in enumerate(ranges):
                @pl.when((here != 0) & (count >= low) & (count < high))
                def _():
                    copy(i, count, kb, cb).start()
            count = count + here
    for i, (low, high) in enumerate(ranges):
        for slot in range(low, high):
            @pl.when(slot < count)
            def _():
                copy(i, slot, 0, 0).wait()


def compress(psi, filled, ranges):
    row_blocks, col_blocks = psi.shape[0] // BLOCK, psi.shape[1] // BLOCK
    return pl.pallas_call(
        functools.partial(compress_kernel, ranges, row_blocks, col_blocks),
        out_shape=[jax.ShapeDtypeStruct((high - low, BLOCK, BLOCK), psi.dtype) for low, high in ranges],
        in_specs=[pl.BlockSpec(memory_space=pltpu.SMEM), pl.BlockSpec(memory_space=pltpu.VMEM)],
        out_specs=[pl.BlockSpec(memory_space=pltpu.VMEM)] * len(ranges),
        scratch_shapes=[pltpu.SemaphoreType.DMA((len(ranges), row_blocks * col_blocks))],
        name="compress",
    )(filled, psi)


class Layout:
    def __init__(self, places, row_blocks, col_blocks, terms, chunks):
        self.places, self.row_blocks, self.col_blocks, self.terms, self.chunks = places, row_blocks, col_blocks, terms, chunks
        self.slots = row_blocks * col_blocks
        self.states = places.y * row_blocks
        self.old_right = places.cols * col_blocks
        self.shards = places.y * places.z * places.x
        self.stride = self.old_right + CHUNK
        self.pairs = self.states * terms + GROUP
        self.tile = 2 if col_blocks % 2 == 0 else 1
        self.tiles = col_blocks // self.tile
        self.new_left = CORES * row_blocks
        self.trash = self.new_left
        self.items = self.tiles * ((self.new_left + 1) // 2) + ITEMS
        self.runs = []
        slot, place = 0, 1
        for wide in chunks:
            self.runs.append((slot, wide, place))
            slot += wide
            place += wide * self.shards

        self.lengths = [
            self.states + 1,
            (self.states + 1) * self.stride,
            (self.states + 1) * self.stride,
            STAGES * self.pairs,
            STAGES * self.pairs,
            2 * self.items,
            self.items,
            self.new_left * col_blocks,
            STAGES + 1,
        ]

    def room(self, chunks):
        return 1 + self.shards * sum(self.chunks[:chunks])

    def lists(self, table):
        at, lists = 0, []
        for length in self.lengths:
            lists.append(List(table, at))
            at += length
        return lists


class List:
    def __init__(self, table, at):
        self.table, self.at = table, at

    def __getitem__(self, i):
        return self.table[self.at + i]

    def __setitem__(self, i, value):
        self.table[self.at + i] = jnp.int32(value)


def plan_kernel(lay, filled, terms, table, used, ready):
    counts, spots, blocks, pair_q, pair_t, lefts, item_tile, allowed, totals = lay.lists(table)
    pz, px, py = lay.places.z, lay.places.x, lay.places.y
    row, col = lax.axis_index("row"), lax.axis_index("col")
    core, y_me = row % CORES, row // CORES
    z_me, x_me = col // px, col % px

    def one_state(q, carry):
        y = q // lay.row_blocks
        kb = q % lay.row_blocks

        @pl.when(kb == 0)
        def _():
            for dev in range(lay.places.cols):
                used[dev] = 0

        dy = (y_me - y + py) % py
        k_block = (y * CORES + core) * lay.row_blocks + kb
        n = jnp.int32(0)
        most = jnp.int32(0)
        for dev in range(lay.places.cols):
            dz = (z_me - dev // px + pz) % pz
            dx = (x_me - dev % px + px) % px
            shard = (dy * px + dx) * pz + dz
            slot = used[dev]
            for cb in range(lay.col_blocks):
                c = dev * lay.col_blocks + cb
                here = filled[k_block, c]
                spot = jnp.int32(0)
                for first, wide, place in lay.runs:
                    spot = jnp.where(slot >= first, place + shard * wide + slot - first, spot)
                spots[q * lay.stride + n] = spot
                blocks[q * lay.stride + n] = c
                n = n + here
                slot = slot + here
            used[dev] = slot
            most = jnp.maximum(most, slot)

        def pad(i, carry):
            spots[q * lay.stride + i] = 0
            blocks[q * lay.stride + i] = 0
            return carry

        lax.fori_loop(n, lay.stride, pad, 0)
        counts[q] = n
        when = jnp.where(y == y_me, jnp.where(most <= lay.chunks[0], 0, 1), 2)
        ready[q] = when
        n_first, n_own = carry
        for t in range(lay.terms):
            on = jnp.where((terms[t, k_block] != 0) & (n > 0), 1, 0)
            n_first = n_first + jnp.where(when == 0, on, 0)
            n_own = n_own + jnp.where(when <= 1, on, 0)
        return n_first, n_own

    n_first, n_own = lax.fori_loop(0, lay.states, one_state, (jnp.int32(0), jnp.int32(0)))
    n_first = n_first // GROUP * GROUP
    n_own = (n_own - n_first) // GROUP * GROUP
    have = (jnp.int32(0), jnp.int32(0), jnp.int32(0))
    for t in range(lay.terms):

        def one_pair(q, have):
            n0, n1, n2 = have
            k_block = (q // lay.row_blocks * CORES + core) * lay.row_blocks + q % lay.row_blocks
            on = jnp.where((terms[t, k_block] != 0) & (counts[q] > 0), 1, 0)
            to0 = jnp.where((ready[q] == 0) & (n0 < n_first), on, 0)
            to1 = jnp.where((ready[q] <= 1) & (n1 < n_own), on - to0, 0)
            at = jnp.where(to0 != 0, n0, jnp.where(to1 != 0, lay.pairs + n1, 2 * lay.pairs + n2))
            pair_q[at] = q
            pair_t[at] = t
            return n0 + to0, n1 + to1, n2 + on - to0 - to1

        have = lax.fori_loop(0, lay.states, one_pair, have)
    n_late = have[2]
    counts[lay.states] = 0

    def pad_state(i, carry):
        spots[lay.states * lay.stride + i] = 0
        blocks[lay.states * lay.stride + i] = 0
        return carry

    lax.fori_loop(0, lay.stride, pad_state, 0)
    for i in range(GROUP):
        pair_q[2 * lay.pairs + n_late + i] = lay.states
        pair_t[2 * lay.pairs + n_late + i] = lay.terms - 1
    totals[0] = n_first // GROUP
    totals[1] = n_own // GROUP
    totals[2] = (n_late + GROUP - 1) // GROUP
    items = jnp.int32(0)
    for tile in range(lay.tiles):
        n = jnp.int32(0)
        for a in range(lay.new_left):
            side, ab = a // lay.row_blocks, a % lay.row_blocks
            a_block = (y_me * CORES + (core + side) % CORES) * lay.row_blocks + ab
            some = jnp.int32(0)
            for i in range(lay.tile):
                here = filled[a_block, col * lay.col_blocks + tile * lay.tile + i]
                allowed[a * lay.col_blocks + tile * lay.tile + i] = here
                some = some | here
            lefts[2 * items + n] = a
            item_tile[items + n // 2] = tile
            n = n + some
        lefts[2 * items + n] = lay.trash
        items = items + (n + 1) // 2
    for i in range(ITEMS):
        lefts[2 * (items + i)] = lay.trash
        lefts[2 * (items + i) + 1] = lay.trash
        item_tile[items + i] = 0
    totals[STAGES] = (items + ITEMS - 1) // ITEMS


def plan(lay, filled, terms):
    smem = pl.BlockSpec(memory_space=pltpu.SMEM)
    return pl.pallas_call(
        functools.partial(plan_kernel, lay),
        out_shape=jax.ShapeDtypeStruct((sum(lay.lengths),), jnp.int32),
        in_specs=[smem, smem],
        out_specs=smem,
        scratch_shapes=[pltpu.SMEM((lay.places.cols,), jnp.int32), pltpu.SMEM((lay.states,), jnp.int32)],
        name="plan",
    )(filled, terms)


def main_kernel(lay, stage, places_of, rows, *refs):
    late = stage == STAGES - 1
    n_psi = len(places_of)
    table, right, left, sib = refs[:4]
    counts, spots, blocks, pair_q, pair_t, lefts, item_tile, allowed, totals = lay.lists(table)
    psi_in, refs = refs[4 : 4 + n_psi], refs[4 + n_psi :]
    before = None
    if stage > 0:
        before, refs = refs[0], refs[1:]
    if late:
        (out_own, out_sib), refs = refs[:2], refs[2:]
    else:
        out, refs = refs[0], refs[1:]
    right_v, psi_v, left_v, acc, w_hi, w_lo, w_acc, right_sem, psi_sem, left_sem, out_sem = refs
    core = lax.axis_index("row") % CORES
    list_at = stage * lay.pairs
    everything = CORES * rows

    def left_copies(g, slot, act):
        for i in range(GROUP):
            q = jnp.minimum(pair_q[list_at + g * GROUP + i], lay.states - 1)
            t = pair_t[list_at + g * GROUP + i]
            y, kb = q // lay.row_blocks, q % lay.row_blocks
            at = pl.ds(pl.multiple_of(((y * CORES + core) * lay.row_blocks + kb) * BLOCK, BLOCK), BLOCK)
            lanes = pl.ds(i * BLOCK, BLOCK)
            for side, source in enumerate((left, sib)):
                act(
                    pltpu.make_async_copy(
                        source.at[t, :, at], left_v.at[slot, pl.ds(side * rows, rows), lanes], left_sem.at[slot, 2 * i + side]
                    )
                )

    def right_copy(t):
        return pltpu.make_async_copy(right.at[t], right_v.at[t], right_sem.at[t])

    start, stop = 0, totals[stage]
    loads = []
    for i, (first, place, wide) in enumerate(places_of):
        loads.append(pltpu.make_async_copy(psi_in[i].at[pl.ds(first, wide)], psi_v.at[pl.ds(place, wide)], psi_sem.at[i]))
    for load in loads:
        load.start()
    if stage > 0:
        sums = pltpu.make_async_copy(before, acc.at[pl.ds(0, everything)], out_sem.at[0])
    first_t = pair_t[list_at + start * GROUP]
    last_t = pair_t[list_at + jnp.maximum(stop * GROUP - 1, 0)]

    @pl.when(stop > start)
    def _():
        right_copy(first_t).start()

    psi_v[0] = jnp.zeros((BLOCK, BLOCK), psi_v.dtype)
    if stage > 0:
        acc[pl.ds(everything, BLOCK), :] = jnp.zeros((BLOCK, acc.shape[1]), acc.dtype)
    else:
        acc[...] = jnp.zeros_like(acc)
    for load in loads:
        load.wait()

    @pl.when(stop > start)
    def _():
        left_copies(start, start % 2, lambda c: c.start())

    if stage > 0:
        sums.start()

    def one_group(g, next_t):
        slot = g % 2
        need_t = pair_t[list_at + g * GROUP + GROUP - 1]

        def one_term(t, carry):
            right_copy(t).wait()

            @pl.when(t < last_t)
            def _():
                right_copy(t + 1).start()

            return carry

        lax.fori_loop(next_t, need_t + 1, one_term, 0)

        @pl.when(g + 1 < stop)
        def _():
            left_copies(g + 1, 1 - slot, lambda c: c.start())

        for low in range(0, GROUP, SIDE):
            qs = [pair_q[list_at + g * GROUP + low + i] for i in range(SIDE)]
            ts = [pair_t[list_at + g * GROUP + low + i] for i in range(SIDE)]
            longest = counts[qs[0]]
            for q in qs[1:]:
                longest = jnp.maximum(longest, counts[q])
            w_acc[...] = jnp.zeros_like(w_acc)

            def one_chunk(j, c1):
                for i in range(SIDE):
                    at = qs[i] * lay.stride + j * CHUNK
                    lhs = jnp.concatenate([psi_v[spots[at + m]] for m in range(CHUNK)], axis=1)
                    rhs = jnp.concatenate(
                        [
                            right_v[ts[i], pl.ds(pl.multiple_of(blocks[at + m] * BLOCK, BLOCK), BLOCK), :]
                            for m in range(CHUNK)
                        ],
                        axis=0,
                    )
                    w_acc[i * BLOCK : (i + 1) * BLOCK, :] += jnp.dot(lhs, rhs, preferred_element_type=jnp.float32)
                return c1

            lax.fori_loop(0, (longest + CHUNK - 1) // CHUNK, one_chunk, 0)
            whole = w_acc[...]
            hi = whole.astype(jnp.bfloat16)
            w_hi[low * BLOCK : (low + SIDE) * BLOCK, :] = hi
            w_lo[low * BLOCK : (low + SIDE) * BLOCK, :] = (whole - hi.astype(jnp.float32)).astype(jnp.bfloat16)
        left_copies(g, slot, lambda c: c.wait())
        if stage > 0:

            @pl.when(g == start)
            def _():
                sums.wait()


        def some_items(m, c0):
            for j in range(ITEMS):
                item = m * ITEMS + j
                width = lay.tile * BLOCK
                lanes = pl.ds(pl.multiple_of(item_tile[item] * width, width), width)
                a = [lefts[2 * item + i] for i in range(2)]
                source = [pl.multiple_of(jnp.minimum(b, lay.new_left - 1) * BLOCK, BLOCK) for b in a]
                lhs = jnp.concatenate([left_v[slot, pl.ds(b, BLOCK), :] for b in source], axis=0)
                gain = jnp.dot(lhs, w_hi[:, lanes], preferred_element_type=jnp.float32)
                gain = gain + jnp.dot(lhs, w_lo[:, lanes], preferred_element_type=jnp.float32)
                for i in range(2):
                    acc[pl.ds(pl.multiple_of(a[i] * BLOCK, BLOCK), BLOCK), lanes] += gain[i * BLOCK : (i + 1) * BLOCK]
            return c0

        lax.fori_loop(0, totals[STAGES], some_items, 0)
        return jnp.maximum(next_t, need_t + 1)

    lax.fori_loop(start, stop, one_group, first_t)
    if stage > 0:

        @pl.when(stop <= start)
        def _():
            sums.wait()

    if late:
        for a in range(lay.new_left):
            for cb in range(lay.col_blocks):
                @pl.when(allowed[a * lay.col_blocks + cb] == 0)
                def _():
                    acc[pl.ds(a * BLOCK, BLOCK), pl.ds(cb * BLOCK, BLOCK)] = jnp.zeros((BLOCK, BLOCK), acc.dtype)

        stores = [
            pltpu.make_async_copy(acc.at[pl.ds(rows, rows)], out_sib, out_sem.at[1]),
            pltpu.make_async_copy(acc.at[pl.ds(0, rows)], out_own, out_sem.at[0]),
        ]
    else:
        stores = [pltpu.make_async_copy(acc.at[pl.ds(0, everything)], out, out_sem.at[0])]
    for store in stores:
        store.start()
    for store in stores:
        store.wait()


def contract(lay, stage, table, right, left, sib, parts, before=None):
    late = stage == STAGES - 1
    rows = lay.row_blocks * BLOCK
    cols = lay.col_blocks * BLOCK
    flat, places_of = [], []
    for (_, wide, place), part in zip(lay.runs, parts):
        for shard, array, first, count in part:
            flat.append(array)
            places_of.append((first, place + shard * wide, count))
    smem = pl.BlockSpec(memory_space=pltpu.SMEM)
    hbm = pl.BlockSpec(memory_space=pl.ANY)
    operands = [right, left, sib, *flat] + ([before] if stage > 0 else [])
    one = jax.ShapeDtypeStruct((rows, cols), jnp.float32)
    both = jax.ShapeDtypeStruct((CORES * rows, cols), jnp.float32)
    return pl.pallas_call(
        functools.partial(main_kernel, lay, stage, places_of, rows),
        out_shape=[one, one] if late else both,
        in_specs=[smem] + [hbm] * len(operands),
        out_specs=[hbm, hbm] if late else hbm,
        scratch_shapes=[
            pltpu.VMEM(right.shape, jnp.bfloat16),
            pltpu.VMEM((lay.room(len(parts)), BLOCK, BLOCK), jnp.bfloat16),
            pltpu.VMEM((2, CORES * rows, GROUP * BLOCK), jnp.bfloat16),
            pltpu.VMEM((CORES * rows + BLOCK, cols), jnp.float32),
            pltpu.VMEM((GROUP * BLOCK, cols), jnp.bfloat16),
            pltpu.VMEM((GROUP * BLOCK, cols), jnp.bfloat16),
            pltpu.VMEM((SIDE * BLOCK, cols), jnp.float32),
            pltpu.SemaphoreType.DMA((lay.terms,)),
            pltpu.SemaphoreType.DMA((len(flat),)),
            pltpu.SemaphoreType.DMA((2, 2 * GROUP)),
            pltpu.SemaphoreType.DMA((2,)),
        ],
        compiler_params=pltpu.CompilerParams(vmem_limit_bytes=VMEM_LIMIT),
        cost_estimate=pl.CostEstimate(flops=1000, bytes_accessed=right.size * 4, transcendentals=0),
        name="late_contract" if late else "early_contract",
    )(table, *operands)


def pack_kernel(copies, *refs):
    n_out = 1 + max(copy[3] for copy in copies)
    sources, outs, sems = refs[: -1 - n_out], refs[-1 - n_out : -1], refs[-1]
    moves = [
        pltpu.make_async_copy(sources[source].at[pl.ds(first, wide)], outs[out].at[pl.ds(at, wide)], sems.at[i])
        for i, (source, first, wide, out, at) in enumerate(copies)
    ]
    for move in moves:
        move.start()
    for move in moves:
        move.wait()


def pack(arrays, copies):
    n_out = 1 + max(copy[3] for copy in copies)
    sizes = [sum(copy[2] for copy in copies if copy[3] == out) for out in range(n_out)]
    vmem = pl.BlockSpec(memory_space=pltpu.VMEM)
    return pl.pallas_call(
        functools.partial(pack_kernel, copies),
        out_shape=[jax.ShapeDtypeStruct((size, *arrays[0].shape[1:]), arrays[0].dtype) for size in sizes],
        in_specs=[vmem] * len(arrays),
        out_specs=[vmem] * n_out,
        scratch_shapes=[pltpu.SemaphoreType.DMA((len(copies),))],
        name="pack",
    )(*arrays)


def after(array, *others):
    return lax.optimization_barrier((array, *others))[0]


class Spread:
    def __init__(self, places, part, owns, first):
        self.places, self.part, self.wide, self.owns, self.first = places, part, part.shape[0], owns, first

    def over_z(self, *others):
        part = after(self.part, *others) if others else self.part
        z = self.places.z
        up, down = {0: part}, {0: part}
        for far in range(1, z // 2 + 1):
            up[far] = move(self.places, up[far - 1], dz=1)
            if far < z - far:
                down[far] = move(self.places, down[far - 1], dz=z - 1)
        self.z = [up[dz] if dz in up else down[z - dz] for dz in range(1, z)]

    def pack_z(self, *others):
        z = [after(array, *others) for array in self.z] if others else self.z
        (self.q,) = pack(z, [(i, 0, self.wide, 0, i * self.wide) for i in range(len(self.z))])
        return self.q

    def over_xy(self):
        self.lines = over_xy(self.places, self.q)

    def diagonal(self, y_last, *others):
        self.lines.update(diagonal(self.places, self.lines, y_last, *others))

    def arrays(self, own_y):
        x, z, w = self.places.x, self.places.z, self.wide
        got = [(0, self.part, 0, w), (1, self.q, 0, (z - 1) * w)]
        for (dy, dx), line in self.lines.items():
            if dy == 0 or not own_y:
                got.append(((dy * x + dx) * z, self.owns[dy, dx], self.first, w))
                got.append(((dy * x + dx) * z + 1, line, 0, (z - 1) * w))
        return got


def over_xy(places, array):
    got = {(0, dx): move(places, array, dx=dx) for dx in range(1, places.x)}
    got.update({(dy, 0): move(places, array, dy=dy) for dy in range(1, places.y)})
    return got


def diagonal(places, got, y_last, *others):
    rest = {}
    for dy in range(1, places.y):
        for dx in range(1, places.x):
            near = got[0, dx] if y_last else got[dy, 0]
            near = after(near, *others) if others else near
            rest[dy, dx] = move(places, near, dy=dy) if y_last else move(places, near, dx=dx)
    return rest


def move(places, array, **step):
    return lax.ppermute(array, AXES, places.shift(**step))


def on_device(wavefunction, left_env, right_env, filled_blocks, term_columns):
    rows, cols = wavefunction.shape
    row_blocks, col_blocks = rows // BLOCK, cols // BLOCK
    places = Places(lax.axis_size("row"), lax.axis_size("col"))
    slots = row_blocks * col_blocks
    chunks = [-(-slots * 10 // 32), -(-slots * 10 // 32), slots * 4 // 32]
    base = chunks[0] + chunks[1]
    chunks.append(slots - sum(chunks))
    lay = Layout(places, row_blocks, col_blocks, left_env.shape[0], chunks)

    own, part1, part2 = compress(wavefunction, filled_blocks, [(0, base), (0, chunks[0]), (chunks[0], base)])
    owns = over_xy(places, own)
    near = list(owns.values())
    one, two = Spread(places, part1, owns, 0), Spread(places, part2, owns, chunks[0])
    swap = places.shift(dcore=1)
    sib = lax.ppermute(left_env, AXES, swap)
    table = plan(lay, filled_blocks, term_columns)
    most = jnp.max(filled_blocks.reshape(places.rows, row_blocks, places.cols, col_blocks).sum(axis=(1, 3)))

    one.over_z()
    one.pack_z(*near)
    one.q, table, most = lax.optimization_barrier((one.q, table, most))
    one.over_xy()
    two.over_z(one.q)
    owns.update(diagonal(places, owns, True, two.z[0], two.z[-1]))
    two.pack_z(*owns.values(), *one.lines.values())
    two.over_xy()
    one.diagonal(True, two.q)
    sums = contract(lay, 0, table, after(right_env, two.q), left_env, sib, [one.arrays(True)])
    two.diagonal(False, sums)
    near = [two.lines[dy, 0] for dy in range(1, places.y)]
    sums = contract(lay, 1, table, after(right_env, *near), left_env, sib, [one.arrays(True), two.arrays(True)], sums)

    def finish(extra, _):
        low, parts = base, [one.arrays(False), two.arrays(False)]
        for wide in chunks[2 : 2 + extra]:
            (part,) = compress(wavefunction, filled_blocks, [(low, low + wide)])
            owns = over_xy(places, part)
            owns.update(diagonal(places, owns, True))
            more = Spread(places, part, owns, 0)
            more.over_z()
            more.pack_z()
            more.over_xy()
            more.diagonal(False)
            parts.append(more.arrays(False))
            low += wide
        return contract(lay, 2, table, right_env, left_env, sib, parts, sums)

    levels = jnp.where(most > base, 1, 0) + jnp.where(most > base + chunks[2], 1, 0)
    own, theirs = lax.switch(levels, [functools.partial(finish, extra) for extra in range(3)], 0)
    return (own + lax.ppermute(theirs, AXES, swap)).astype(jnp.bfloat16)


def solution(mesh):
    in_specs = (P("row", "col"), P(None, "row", None), P(None, None, "col"), P(), P())
    out_specs = P("row", "col")
    return jax.shard_map(
        on_device, mesh=mesh, in_specs=in_specs, out_specs=out_specs, check_vma=False
    )
```

```python
import functools

import jax
import jax.numpy as jnp
from jax import lax
from jax.experimental import pallas as pl
from jax.experimental.pallas import tpu as pltpu
from jax.sharding import PartitionSpec as P

BLOCK = 128
CORES = 2
STAGES = 3
ITEMS = 2
GROUP = 8
SIDE = 4
CHUNK = 8
AXES = ("row", "col")
VMEM_LIMIT = 58 * 1024 * 1024


class Places:
    def __init__(self, row_devices, col_devices):
        self.rows, self.cols = row_devices, col_devices
        self.y = row_devices // CORES
        self.x = 1
        while self.x * self.x * 4 <= col_devices and col_devices % (self.x * 2) == 0:
            self.x *= 2
        self.z = col_devices // self.x

    def flat(self, y, core, z, x):
        return (y * CORES + core) * self.cols + z * self.x + x

    def shift(self, dy=0, dz=0, dx=0, dcore=0):
        perm = []
        for y in range(self.y):
            for core in range(CORES):
                for z in range(self.z):
                    for x in range(self.x):
                        there = self.flat(
                            (y + dy) % self.y, (core + dcore) % CORES, (z + dz) % self.z, (x + dx) % self.x
                        )
                        perm.append((self.flat(y, core, z, x), there))
        return perm


def compress_kernel(ranges, row_blocks, col_blocks, filled, psi, *rest):
    outs, sems = rest[: len(ranges)], rest[len(ranges)]
    row0 = lax.axis_index("row") * row_blocks
    col0 = lax.axis_index("col") * col_blocks

    def copy(i, slot, kb, cb):
        return pltpu.make_async_copy(
            psi.at[pl.ds(kb * BLOCK, BLOCK), pl.ds(cb * BLOCK, BLOCK)], outs[i].at[slot - ranges[i][0]], sems.at[i, slot]
        )

    count = jnp.int32(0)
    for kb in range(row_blocks):
        for cb in range(col_blocks):
            here = filled[row0 + kb, col0 + cb]
            for i, (low, high) in enumerate(ranges):
                @pl.when((here != 0) & (count >= low) & (count < high))
                def _():
                    copy(i, count, kb, cb).start()
            count = count + here
    for i, (low, high) in enumerate(ranges):
        for slot in range(low, high):
            @pl.when(slot < count)
            def _():
                copy(i, slot, 0, 0).wait()


def compress(psi, filled, ranges):
    row_blocks, col_blocks = psi.shape[0] // BLOCK, psi.shape[1] // BLOCK
    return pl.pallas_call(
        functools.partial(compress_kernel, ranges, row_blocks, col_blocks),
        out_shape=[jax.ShapeDtypeStruct((high - low, BLOCK, BLOCK), psi.dtype) for low, high in ranges],
        in_specs=[pl.BlockSpec(memory_space=pltpu.SMEM), pl.BlockSpec(memory_space=pltpu.VMEM)],
        out_specs=[pl.BlockSpec(memory_space=pltpu.VMEM)] * len(ranges),
        scratch_shapes=[pltpu.SemaphoreType.DMA((len(ranges), row_blocks * col_blocks))],
        name="compress",
    )(filled, psi)


class Layout:
    def __init__(self, places, row_blocks, col_blocks, terms, chunks):
        self.places, self.row_blocks, self.col_blocks, self.terms, self.chunks = places, row_blocks, col_blocks, terms, chunks
        self.slots = row_blocks * col_blocks
        self.base = chunks[0] + chunks[1]
        self.states = places.y * row_blocks
        self.old_right = places.cols * col_blocks
        self.shards = places.y * places.z * places.x
        self.stride = self.old_right + CHUNK
        self.pairs = self.states * terms + GROUP
        self.tile = 2 if col_blocks % 2 == 0 else 1
        self.tiles = col_blocks // self.tile
        self.new_left = CORES * row_blocks
        self.trash = self.new_left
        self.items = self.tiles * ((self.new_left + 1) // 2) + ITEMS
        self.runs = []
        slot, place = 0, 1
        for wide in chunks:
            self.runs.append((slot, wide, place))
            slot += wide
            place += wide * self.shards

        self.lengths = [
            self.states + 1,
            (self.states + 1) * self.stride,
            (self.states + 1) * self.stride,
            STAGES * self.pairs,
            STAGES * self.pairs,
            2 * self.items,
            self.items,
            self.new_left * col_blocks,
            STAGES + 1,
        ]

    def room(self, chunks):
        return 1 + self.shards * sum(self.chunks[:chunks])

    def lists(self, table):
        at, lists = 0, []
        for length in self.lengths:
            lists.append(List(table, at))
            at += length
        return lists


class List:
    def __init__(self, table, at):
        self.table, self.at = table, at

    def __getitem__(self, i):
        return self.table[self.at + i]

    def __setitem__(self, i, value):
        self.table[self.at + i] = jnp.int32(value)


def plan_kernel(lay, filled, terms, table, used, ready):
    counts, spots, blocks, pair_q, pair_t, lefts, item_tile, allowed, totals = lay.lists(table)
    pz, px, py = lay.places.z, lay.places.x, lay.places.y
    row, col = lax.axis_index("row"), lax.axis_index("col")
    core, y_me = row % CORES, row // CORES
    z_me, x_me = col // px, col % px

    def one_state(q, carry):
        y = q // lay.row_blocks
        kb = q % lay.row_blocks

        @pl.when(kb == 0)
        def _():
            for dev in range(lay.places.cols):
                used[dev] = 0

        dy = (y_me - y + py) % py
        k_block = (y * CORES + core) * lay.row_blocks + kb
        n = jnp.int32(0)
        most = jnp.int32(0)
        for dev in range(lay.places.cols):
            dz = (z_me - dev // px + pz) % pz
            dx = (x_me - dev % px + px) % px
            shard = (dy * px + dx) * pz + dz
            slot = used[dev]
            for cb in range(lay.col_blocks):
                c = dev * lay.col_blocks + cb
                here = filled[k_block, c]
                spot = jnp.int32(0)
                for first, wide, place in lay.runs:
                    spot = jnp.where(slot >= first, place + shard * wide + slot - first, spot)
                spots[q * lay.stride + n] = spot
                blocks[q * lay.stride + n] = c
                n = n + here
                slot = slot + here
            used[dev] = slot
            most = jnp.maximum(most, slot)

        def pad(i, carry):
            spots[q * lay.stride + i] = 0
            blocks[q * lay.stride + i] = 0
            return carry

        lax.fori_loop(n, lay.stride, pad, 0)
        counts[q] = n
        when = jnp.where((y == y_me) & (most <= lay.base), jnp.where(most <= lay.chunks[0], 0, 1), 2)
        ready[q] = when
        n_first, n_own = carry
        for t in range(lay.terms):
            on = jnp.where((terms[t, k_block] != 0) & (n > 0), 1, 0)
            n_first = n_first + jnp.where(when == 0, on, 0)
            n_own = n_own + jnp.where(when <= 1, on, 0)
        return n_first, n_own

    n_first, n_own = lax.fori_loop(0, lay.states, one_state, (jnp.int32(0), jnp.int32(0)))
    n_first = n_first // GROUP * GROUP
    n_own = n_own - n_first
    have = (jnp.int32(0), jnp.int32(0), jnp.int32(0))
    for t in range(lay.terms):

        def one_pair(q, have):
            n0, n1, n2 = have
            k_block = (q // lay.row_blocks * CORES + core) * lay.row_blocks + q % lay.row_blocks
            on = jnp.where((terms[t, k_block] != 0) & (counts[q] > 0), 1, 0)
            to0 = jnp.where((ready[q] == 0) & (n0 < n_first), on, 0)
            to1 = jnp.where((ready[q] <= 1) & (n1 < n_own), on - to0, 0)
            at = jnp.where(to0 != 0, n0, jnp.where(to1 != 0, lay.pairs + n1, 2 * lay.pairs + n2))
            pair_q[at] = q
            pair_t[at] = t
            return n0 + to0, n1 + to1, n2 + on - to0 - to1

        have = lax.fori_loop(0, lay.states, one_pair, have)
    n_late = have[2]
    counts[lay.states] = 0

    def pad_state(i, carry):
        spots[lay.states * lay.stride + i] = 0
        blocks[lay.states * lay.stride + i] = 0
        return carry

    lax.fori_loop(0, lay.stride, pad_state, 0)
    for i in range(GROUP):
        for at in (lay.pairs + n_own + i, 2 * lay.pairs + n_late + i):
            pair_q[at] = lay.states
            pair_t[at] = lay.terms - 1
    totals[0] = n_first // GROUP
    totals[1] = (n_own + GROUP - 1) // GROUP
    totals[2] = (n_late + GROUP - 1) // GROUP
    items = jnp.int32(0)
    for tile in range(lay.tiles):
        n = jnp.int32(0)
        for a in range(lay.new_left):
            side, ab = a // lay.row_blocks, a % lay.row_blocks
            a_block = (y_me * CORES + (core + side) % CORES) * lay.row_blocks + ab
            some = jnp.int32(0)
            for i in range(lay.tile):
                here = filled[a_block, col * lay.col_blocks + tile * lay.tile + i]
                allowed[a * lay.col_blocks + tile * lay.tile + i] = here
                some = some | here
            lefts[2 * items + n] = a
            item_tile[items + n // 2] = tile
            n = n + some
        lefts[2 * items + n] = lay.trash
        items = items + (n + 1) // 2
    for i in range(ITEMS):
        lefts[2 * (items + i)] = lay.trash
        lefts[2 * (items + i) + 1] = lay.trash
        item_tile[items + i] = 0
    totals[STAGES] = (items + ITEMS - 1) // ITEMS


def plan(lay, filled, terms):
    smem = pl.BlockSpec(memory_space=pltpu.SMEM)
    return pl.pallas_call(
        functools.partial(plan_kernel, lay),
        out_shape=jax.ShapeDtypeStruct((sum(lay.lengths),), jnp.int32),
        in_specs=[smem, smem],
        out_specs=smem,
        scratch_shapes=[pltpu.SMEM((lay.places.cols,), jnp.int32), pltpu.SMEM((lay.states,), jnp.int32)],
        name="plan",
    )(filled, terms)


def main_kernel(lay, stage, places_of, rows, *refs):
    late = stage == STAGES - 1
    n_psi = len(places_of)
    table, right, left, sib = refs[:4]
    counts, spots, blocks, pair_q, pair_t, lefts, item_tile, allowed, totals = lay.lists(table)
    psi_in, refs = refs[4 : 4 + n_psi], refs[4 + n_psi :]
    before = None
    if stage > 0:
        before, refs = refs[0], refs[1:]
    if late:
        (out_own, out_sib), refs = refs[:2], refs[2:]
    else:
        out, refs = refs[0], refs[1:]
    right_v, psi_v, left_v, acc, w_hi, w_lo, w_acc, right_sem, psi_sem, left_sem, out_sem = refs
    core = lax.axis_index("row") % CORES
    list_at = stage * lay.pairs
    everything = CORES * rows

    def left_copies(g, slot, act):
        for i in range(GROUP):
            q = jnp.minimum(pair_q[list_at + g * GROUP + i], lay.states - 1)
            t = pair_t[list_at + g * GROUP + i]
            y, kb = q // lay.row_blocks, q % lay.row_blocks
            at = pl.ds(pl.multiple_of(((y * CORES + core) * lay.row_blocks + kb) * BLOCK, BLOCK), BLOCK)
            lanes = pl.ds(i * BLOCK, BLOCK)
            for side, source in enumerate((left, sib)):
                act(
                    pltpu.make_async_copy(
                        source.at[t, :, at], left_v.at[slot, pl.ds(side * rows, rows), lanes], left_sem.at[slot, 2 * i + side]
                    )
                )

    def right_copy(t):
        return pltpu.make_async_copy(right.at[t], right_v.at[t], right_sem.at[t])

    start, stop = 0, totals[stage]
    loads = []
    for i, (first, place, wide) in enumerate(places_of):
        loads.append(pltpu.make_async_copy(psi_in[i].at[pl.ds(first, wide)], psi_v.at[pl.ds(place, wide)], psi_sem.at[i]))
    for load in loads:
        load.start()
    if stage > 0:
        sums = pltpu.make_async_copy(before, acc.at[pl.ds(0, everything)], out_sem.at[0])
    first_t = pair_t[list_at + start * GROUP]
    last_t = pair_t[list_at + jnp.maximum(stop * GROUP - 1, 0)]

    @pl.when(stop > start)
    def _():
        right_copy(first_t).start()

    psi_v[0] = jnp.zeros((BLOCK, BLOCK), psi_v.dtype)
    if stage > 0:
        acc[pl.ds(everything, BLOCK), :] = jnp.zeros((BLOCK, acc.shape[1]), acc.dtype)
    else:
        acc[...] = jnp.zeros_like(acc)
    for load in loads:
        load.wait()

    @pl.when(stop > start)
    def _():
        left_copies(start, start % 2, lambda c: c.start())

    if stage > 0:
        sums.start()

    def one_group(g, next_t):
        slot = g % 2
        need_t = pair_t[list_at + g * GROUP + GROUP - 1]

        def one_term(t, carry):
            right_copy(t).wait()

            @pl.when(t < last_t)
            def _():
                right_copy(t + 1).start()

            return carry

        lax.fori_loop(next_t, need_t + 1, one_term, 0)

        @pl.when(g + 1 < stop)
        def _():
            left_copies(g + 1, 1 - slot, lambda c: c.start())

        for low in range(0, GROUP, SIDE):
            qs = [pair_q[list_at + g * GROUP + low + i] for i in range(SIDE)]
            ts = [pair_t[list_at + g * GROUP + low + i] for i in range(SIDE)]
            longest = counts[qs[0]]
            for q in qs[1:]:
                longest = jnp.maximum(longest, counts[q])
            w_acc[...] = jnp.zeros_like(w_acc)

            def one_chunk(j, c1):
                for i in range(SIDE):
                    at = qs[i] * lay.stride + j * CHUNK
                    lhs = jnp.concatenate([psi_v[spots[at + m]] for m in range(CHUNK)], axis=1)
                    rhs = jnp.concatenate(
                        [
                            right_v[ts[i], pl.ds(pl.multiple_of(blocks[at + m] * BLOCK, BLOCK), BLOCK), :]
                            for m in range(CHUNK)
                        ],
                        axis=0,
                    )
                    w_acc[i * BLOCK : (i + 1) * BLOCK, :] += jnp.dot(lhs, rhs, preferred_element_type=jnp.float32)
                return c1

            lax.fori_loop(0, (longest + CHUNK - 1) // CHUNK, one_chunk, 0)
            whole = w_acc[...]
            hi = whole.astype(jnp.bfloat16)
            w_hi[low * BLOCK : (low + SIDE) * BLOCK, :] = hi
            w_lo[low * BLOCK : (low + SIDE) * BLOCK, :] = (whole - hi.astype(jnp.float32)).astype(jnp.bfloat16)
        left_copies(g, slot, lambda c: c.wait())
        if stage > 0:

            @pl.when(g == start)
            def _():
                sums.wait()


        def some_items(depth, m, c0):
            for j in range(ITEMS):
                item = m * ITEMS + j
                width = lay.tile * BLOCK
                lanes = pl.ds(pl.multiple_of(item_tile[item] * width, width), width)
                a = [lefts[2 * item + i] for i in range(2)]
                source = [pl.multiple_of(jnp.minimum(b, lay.new_left - 1) * BLOCK, BLOCK) for b in a]
                lhs = jnp.concatenate([left_v[slot, pl.ds(b, BLOCK), :depth] for b in source], axis=0)
                gain = jnp.dot(lhs, w_hi[:depth, lanes], preferred_element_type=jnp.float32)
                gain = gain + jnp.dot(lhs, w_lo[:depth, lanes], preferred_element_type=jnp.float32)
                for i in range(2):
                    acc[pl.ds(pl.multiple_of(a[i] * BLOCK, BLOCK), BLOCK), lanes] += gain[i * BLOCK : (i + 1) * BLOCK]
            return c0

        short = pair_q[list_at + g * GROUP + SIDE] == lay.states
        steps = totals[STAGES]
        lax.fori_loop(0, jnp.where(short, 0, steps), functools.partial(some_items, GROUP * BLOCK), 0)
        lax.fori_loop(0, jnp.where(short, steps, 0), functools.partial(some_items, SIDE * BLOCK), 0)
        return jnp.maximum(next_t, need_t + 1)

    lax.fori_loop(start, stop, one_group, first_t)
    if stage > 0:

        @pl.when(stop <= start)
        def _():
            sums.wait()

    if late:
        for a in range(lay.new_left):
            for cb in range(lay.col_blocks):
                @pl.when(allowed[a * lay.col_blocks + cb] == 0)
                def _():
                    acc[pl.ds(a * BLOCK, BLOCK), pl.ds(cb * BLOCK, BLOCK)] = jnp.zeros((BLOCK, BLOCK), acc.dtype)

        stores = [
            pltpu.make_async_copy(acc.at[pl.ds(rows, rows)], out_sib, out_sem.at[1]),
            pltpu.make_async_copy(acc.at[pl.ds(0, rows)], out_own, out_sem.at[0]),
        ]
    else:
        stores = [pltpu.make_async_copy(acc.at[pl.ds(0, everything)], out, out_sem.at[0])]
    for store in stores:
        store.start()
    for store in stores:
        store.wait()


def contract(lay, stage, table, right, left, sib, parts, before=None):
    late = stage == STAGES - 1
    rows = lay.row_blocks * BLOCK
    cols = lay.col_blocks * BLOCK
    flat, places_of = [], []
    for (_, wide, place), part in zip(lay.runs, parts):
        for shard, array, first, count in part:
            flat.append(array)
            places_of.append((first, place + shard * wide, count))
    smem = pl.BlockSpec(memory_space=pltpu.SMEM)
    hbm = pl.BlockSpec(memory_space=pl.ANY)
    operands = [right, left, sib, *flat] + ([before] if stage > 0 else [])
    one = jax.ShapeDtypeStruct((rows, cols), jnp.float32)
    both = jax.ShapeDtypeStruct((CORES * rows, cols), jnp.float32)
    return pl.pallas_call(
        functools.partial(main_kernel, lay, stage, places_of, rows),
        out_shape=[one, one] if late else both,
        in_specs=[smem] + [hbm] * len(operands),
        out_specs=[hbm, hbm] if late else hbm,
        scratch_shapes=[
            pltpu.VMEM(right.shape, jnp.bfloat16),
            pltpu.VMEM((lay.room(len(parts)), BLOCK, BLOCK), jnp.bfloat16),
            pltpu.VMEM((2, CORES * rows, GROUP * BLOCK), jnp.bfloat16),
            pltpu.VMEM((CORES * rows + BLOCK, cols), jnp.float32),
            pltpu.VMEM((GROUP * BLOCK, cols), jnp.bfloat16),
            pltpu.VMEM((GROUP * BLOCK, cols), jnp.bfloat16),
            pltpu.VMEM((SIDE * BLOCK, cols), jnp.float32),
            pltpu.SemaphoreType.DMA((lay.terms,)),
            pltpu.SemaphoreType.DMA((len(flat),)),
            pltpu.SemaphoreType.DMA((2, 2 * GROUP)),
            pltpu.SemaphoreType.DMA((2,)),
        ],
        compiler_params=pltpu.CompilerParams(vmem_limit_bytes=VMEM_LIMIT),
        cost_estimate=pl.CostEstimate(flops=1000, bytes_accessed=right.size * 4, transcendentals=0),
        name="late_contract" if late else "early_contract",
    )(table, *operands)


def pack_kernel(copies, *refs):
    n_out = 1 + max(copy[3] for copy in copies)
    sources, outs, sems = refs[: -1 - n_out], refs[-1 - n_out : -1], refs[-1]
    moves = [
        pltpu.make_async_copy(sources[source].at[pl.ds(first, wide)], outs[out].at[pl.ds(at, wide)], sems.at[i])
        for i, (source, first, wide, out, at) in enumerate(copies)
    ]
    for move in moves:
        move.start()
    for move in moves:
        move.wait()


def pack(arrays, copies):
    n_out = 1 + max(copy[3] for copy in copies)
    sizes = [sum(copy[2] for copy in copies if copy[3] == out) for out in range(n_out)]
    vmem = pl.BlockSpec(memory_space=pltpu.VMEM)
    return pl.pallas_call(
        functools.partial(pack_kernel, copies),
        out_shape=[jax.ShapeDtypeStruct((size, *arrays[0].shape[1:]), arrays[0].dtype) for size in sizes],
        in_specs=[vmem] * len(arrays),
        out_specs=[vmem] * n_out,
        scratch_shapes=[pltpu.SemaphoreType.DMA((len(copies),))],
        name="pack",
    )(*arrays)


def after(array, *others):
    return lax.optimization_barrier((array, *others))[0]


class Spread:
    def __init__(self, places, part, owns, first):
        self.places, self.part, self.wide, self.owns, self.first = places, part, part.shape[0], owns, first

    def over_z(self, *others):
        part = after(self.part, *others) if others else self.part
        z = self.places.z
        up, down = {0: part}, {0: part}
        for far in range(1, z // 2 + 1):
            up[far] = move(self.places, up[far - 1], dz=1)
            if far < z - far:
                down[far] = move(self.places, down[far - 1], dz=z - 1)
        self.z = [up[dz] if dz in up else down[z - dz] for dz in range(1, z)]

    def pack_z(self, *others):
        z = [after(array, *others) for array in self.z] if others else self.z
        (self.q,) = pack(z, [(i, 0, self.wide, 0, i * self.wide) for i in range(len(self.z))])
        return self.q

    def over_xy(self):
        self.lines = over_xy(self.places, self.q)

    def diagonal(self, y_last, *others):
        self.lines.update(diagonal(self.places, self.lines, y_last, *others))

    def arrays(self, own_y=True, other_y=True):
        x, z, w = self.places.x, self.places.z, self.wide
        got = [(0, self.part, 0, w), (1, self.q, 0, (z - 1) * w)] if own_y else []
        for (dy, dx), line in self.lines.items():
            if own_y if dy == 0 else other_y:
                first = self.first if dy == 0 or dx == 0 else 0
                got.append(((dy * x + dx) * z, self.owns[dy, dx], first, w))
                got.append(((dy * x + dx) * z + 1, line, 0, (z - 1) * w))
        return got


def over_xy(places, array):
    got = {(0, dx): move(places, array, dx=dx) for dx in range(1, places.x)}
    got.update({(dy, 0): move(places, array, dy=dy) for dy in range(1, places.y)})
    return got


def diagonal(places, got, y_last, *others):
    rest = {}
    for dy in range(1, places.y):
        for dx in range(1, places.x):
            near = got[0, dx] if y_last else got[dy, 0]
            near = after(near, *others) if others else near
            rest[dy, dx] = move(places, near, dy=dy) if y_last else move(places, near, dx=dx)
    return rest


def move(places, array, **step):
    return lax.ppermute(array, AXES, places.shift(**step))


def on_device(wavefunction, left_env, right_env, filled_blocks, term_columns):
    rows, cols = wavefunction.shape
    row_blocks, col_blocks = rows // BLOCK, cols // BLOCK
    places = Places(lax.axis_size("row"), lax.axis_size("col"))
    slots = row_blocks * col_blocks
    chunks = [-(-slots * 10 // 32), -(-slots * 10 // 32), slots * 4 // 32]
    base = chunks[0] + chunks[1]
    chunks.append(slots - sum(chunks))
    lay = Layout(places, row_blocks, col_blocks, left_env.shape[0], chunks)

    own, part1, part2 = compress(wavefunction, filled_blocks, [(0, base), (0, chunks[0]), (chunks[0], base)])
    owns = over_xy(places, own)
    near = list(owns.values())
    one, two = Spread(places, part1, owns, 0), Spread(places, part2, owns, chunks[0])
    swap = places.shift(dcore=1)
    sib = lax.ppermute(left_env, AXES, swap)
    table = plan(lay, filled_blocks, term_columns)
    most = jnp.max(filled_blocks.reshape(places.rows, row_blocks, places.cols, col_blocks).sum(axis=(1, 3)))

    one.over_z()
    one.pack_z(*near)
    one.q, table, most = lax.optimization_barrier((one.q, table, most))
    one.over_xy()
    two.over_z(one.q)
    two.pack_z(*near, *one.lines.values())
    two.over_xy()
    one.diagonal(True, two.q)
    sums = contract(lay, 0, table, after(right_env, two.q), left_env, sib, [one.arrays(other_y=False)])
    two.diagonal(False, sums)
    for spread, y_last in ((one, True), (two, False)):
        low, high = spread.first, spread.first + spread.wide
        mine = {key: array[low:high] for key, array in owns.items()}
        spread.owns = {**owns, **diagonal(places, mine, y_last, sums)}
    near = [two.lines[dy, 0] for dy in range(1, places.y)]
    own_y = [one.arrays(other_y=False), two.arrays(other_y=False)]
    sums = contract(lay, 1, table, after(right_env, *near), left_env, sib, own_y, sums)

    def finish(extra, _):
        low, parts = base, [one.arrays(extra > 0), two.arrays(extra > 0)]
        for wide in chunks[2 : 2 + extra]:
            (part,) = compress(wavefunction, filled_blocks, [(low, low + wide)])
            owns = over_xy(places, part)
            owns.update(diagonal(places, owns, True))
            more = Spread(places, part, owns, 0)
            more.over_z()
            more.pack_z()
            more.over_xy()
            more.diagonal(False)
            parts.append(more.arrays())
            low += wide
        return contract(lay, 2, table, right_env, left_env, sib, parts, sums)

    levels = jnp.where(most > base, 1, 0) + jnp.where(most > base + chunks[2], 1, 0)
    own, theirs = lax.switch(levels, [functools.partial(finish, extra) for extra in range(3)], 0)
    return (own + lax.ppermute(theirs, AXES, swap)).astype(jnp.bfloat16)


def solution(mesh):
    in_specs = (P("row", "col"), P(None, "row", None), P(None, None, "col"), P(), P())
    out_specs = P("row", "col")
    return jax.shard_map(
        on_device, mesh=mesh, in_specs=in_specs, out_specs=out_specs, check_vma=False
    )
```

```python
import functools

import jax
import jax.numpy as jnp
from jax import lax
from jax.experimental import pallas as pl
from jax.experimental.pallas import tpu as pltpu
from jax.sharding import PartitionSpec as P

BLOCK = 128
CORES = 2
STAGES = 3
ITEMS = 2
GROUP = 8
SIDE = 4
CHUNK = 8
AXES = ("row", "col")
VMEM_LIMIT = 58 * 1024 * 1024


class Places:
    def __init__(self, row_devices, col_devices):
        self.rows, self.cols = row_devices, col_devices
        self.y = row_devices // CORES
        self.x = 1
        while self.x * self.x * 4 <= col_devices and col_devices % (self.x * 2) == 0:
            self.x *= 2
        self.z = col_devices // self.x

    def flat(self, y, core, z, x):
        return (y * CORES + core) * self.cols + z * self.x + x

    def shift(self, dy=0, dz=0, dx=0, dcore=0):
        perm = []
        for y in range(self.y):
            for core in range(CORES):
                for z in range(self.z):
                    for x in range(self.x):
                        there = self.flat(
                            (y + dy) % self.y, (core + dcore) % CORES, (z + dz) % self.z, (x + dx) % self.x
                        )
                        perm.append((self.flat(y, core, z, x), there))
        return perm


def compress_kernel(ranges, row_blocks, col_blocks, filled, psi, *rest):
    outs, sems = rest[: len(ranges)], rest[len(ranges)]
    row0 = lax.axis_index("row") * row_blocks
    col0 = lax.axis_index("col") * col_blocks

    def copy(i, slot, kb, cb):
        return pltpu.make_async_copy(
            psi.at[pl.ds(kb * BLOCK, BLOCK), pl.ds(cb * BLOCK, BLOCK)], outs[i].at[slot - ranges[i][0]], sems.at[i, slot]
        )

    count = jnp.int32(0)
    for kb in range(row_blocks):
        for cb in range(col_blocks):
            here = filled[row0 + kb, col0 + cb]
            for i, (low, high) in enumerate(ranges):
                @pl.when((here != 0) & (count >= low) & (count < high))
                def _():
                    copy(i, count, kb, cb).start()
            count = count + here
    for i, (low, high) in enumerate(ranges):
        for slot in range(low, high):
            @pl.when(slot < count)
            def _():
                copy(i, slot, 0, 0).wait()


def compress(psi, filled, ranges):
    row_blocks, col_blocks = psi.shape[0] // BLOCK, psi.shape[1] // BLOCK
    return pl.pallas_call(
        functools.partial(compress_kernel, ranges, row_blocks, col_blocks),
        out_shape=[jax.ShapeDtypeStruct((high - low, BLOCK, BLOCK), psi.dtype) for low, high in ranges],
        in_specs=[pl.BlockSpec(memory_space=pltpu.SMEM), pl.BlockSpec(memory_space=pltpu.VMEM)],
        out_specs=[pl.BlockSpec(memory_space=pltpu.VMEM)] * len(ranges),
        scratch_shapes=[pltpu.SemaphoreType.DMA((len(ranges), row_blocks * col_blocks))],
        name="compress",
    )(filled, psi)


class Layout:
    def __init__(self, places, row_blocks, col_blocks, terms, chunks):
        self.places, self.row_blocks, self.col_blocks, self.terms, self.chunks = places, row_blocks, col_blocks, terms, chunks
        self.slots = row_blocks * col_blocks
        self.base = chunks[0] + chunks[1]
        self.states = places.y * row_blocks
        self.old_right = places.cols * col_blocks
        self.shards = places.y * places.z * places.x
        self.stride = self.old_right + CHUNK
        self.pairs = self.states * terms + GROUP
        self.tile = 2 if col_blocks % 2 == 0 else 1
        self.tiles = col_blocks // self.tile
        self.new_left = CORES * row_blocks
        self.trash = self.new_left
        self.items = self.tiles * ((self.new_left + 1) // 2) + ITEMS
        self.runs = []
        slot, place = 0, 1
        for wide in chunks:
            self.runs.append((slot, wide, place))
            slot += wide
            place += wide * self.shards

        self.lengths = [
            self.states + 1,
            (self.states + 1) * self.stride,
            (self.states + 1) * self.stride,
            STAGES * self.pairs,
            STAGES * self.pairs,
            2 * self.items,
            self.items,
            self.new_left * col_blocks,
            STAGES + 1,
        ]

    def room(self, chunks):
        return 1 + self.shards * sum(self.chunks[:chunks])

    def lists(self, table):
        at, lists = 0, []
        for length in self.lengths:
            lists.append(List(table, at))
            at += length
        return lists


class List:
    def __init__(self, table, at):
        self.table, self.at = table, at

    def __getitem__(self, i):
        return self.table[self.at + i]

    def __setitem__(self, i, value):
        self.table[self.at + i] = jnp.int32(value)


def plan_kernel(lay, filled, terms, table, used, ready):
    counts, spots, blocks, pair_q, pair_t, lefts, item_tile, allowed, totals = lay.lists(table)
    pz, px, py = lay.places.z, lay.places.x, lay.places.y
    row, col = lax.axis_index("row"), lax.axis_index("col")
    core, y_me = row % CORES, row // CORES
    z_me, x_me = col // px, col % px

    def one_state(q, carry):
        y = q // lay.row_blocks
        kb = q % lay.row_blocks

        @pl.when(kb == 0)
        def _():
            for dev in range(lay.places.cols):
                used[dev] = 0

        dy = (y_me - y + py) % py
        k_block = (y * CORES + core) * lay.row_blocks + kb
        n = jnp.int32(0)
        most = jnp.int32(0)
        for dev in range(lay.places.cols):
            dz = (z_me - dev // px + pz) % pz
            dx = (x_me - dev % px + px) % px
            shard = (dy * px + dx) * pz + dz
            slot = used[dev]
            for cb in range(lay.col_blocks):
                c = dev * lay.col_blocks + cb
                here = filled[k_block, c]
                spot = jnp.int32(0)
                for first, wide, place in lay.runs:
                    spot = jnp.where(slot >= first, place + shard * wide + slot - first, spot)
                spots[q * lay.stride + n] = spot
                blocks[q * lay.stride + n] = c
                n = n + here
                slot = slot + here
            used[dev] = slot
            most = jnp.maximum(most, slot)

        def pad(i, carry):
            spots[q * lay.stride + i] = 0
            blocks[q * lay.stride + i] = 0
            return carry

        lax.fori_loop(n, lay.stride, pad, 0)
        counts[q] = n
        when = jnp.where((y == y_me) & (most <= lay.base), jnp.where(most <= lay.chunks[0], 0, 1), 2)
        ready[q] = when
        n_first, n_own = carry
        for t in range(lay.terms):
            on = jnp.where((terms[t, k_block] != 0) & (n > 0), 1, 0)
            n_first = n_first + jnp.where(when == 0, on, 0)
            n_own = n_own + jnp.where(when <= 1, on, 0)
        return n_first, n_own

    n_first, n_own = lax.fori_loop(0, lay.states, one_state, (jnp.int32(0), jnp.int32(0)))
    n_first = n_first // GROUP * GROUP
    n_own = n_own - n_first
    have = (jnp.int32(0), jnp.int32(0), jnp.int32(0))
    for t in range(lay.terms):

        def one_pair(q, have):
            n0, n1, n2 = have
            k_block = (q // lay.row_blocks * CORES + core) * lay.row_blocks + q % lay.row_blocks
            on = jnp.where((terms[t, k_block] != 0) & (counts[q] > 0), 1, 0)
            to0 = jnp.where((ready[q] == 0) & (n0 < n_first), on, 0)
            to1 = jnp.where((ready[q] <= 1) & (n1 < n_own), on - to0, 0)
            at = jnp.where(to0 != 0, n0, jnp.where(to1 != 0, lay.pairs + n1, 2 * lay.pairs + n2))
            pair_q[at] = q
            pair_t[at] = t
            return n0 + to0, n1 + to1, n2 + on - to0 - to1

        have = lax.fori_loop(0, lay.states, one_pair, have)
    n_late = have[2]
    counts[lay.states] = 0

    def pad_state(i, carry):
        spots[lay.states * lay.stride + i] = 0
        blocks[lay.states * lay.stride + i] = 0
        return carry

    lax.fori_loop(0, lay.stride, pad_state, 0)
    for i in range(GROUP):
        for at in (lay.pairs + n_own + i, 2 * lay.pairs + n_late + i):
            pair_q[at] = lay.states
            pair_t[at] = lay.terms - 1
    totals[0] = n_first // GROUP
    totals[1] = (n_own + GROUP - 1) // GROUP
    totals[2] = (n_late + GROUP - 1) // GROUP
    items = jnp.int32(0)
    for tile in range(lay.tiles):
        n = jnp.int32(0)
        for a in range(lay.new_left):
            side, ab = a // lay.row_blocks, a % lay.row_blocks
            a_block = (y_me * CORES + (core + side) % CORES) * lay.row_blocks + ab
            some = jnp.int32(0)
            for i in range(lay.tile):
                here = filled[a_block, col * lay.col_blocks + tile * lay.tile + i]
                allowed[a * lay.col_blocks + tile * lay.tile + i] = here
                some = some | here
            lefts[2 * items + n] = a
            item_tile[items + n // 2] = tile
            n = n + some
        lefts[2 * items + n] = lay.trash
        items = items + (n + 1) // 2
    for i in range(ITEMS):
        lefts[2 * (items + i)] = lay.trash
        lefts[2 * (items + i) + 1] = lay.trash
        item_tile[items + i] = 0
    totals[STAGES] = (items + ITEMS - 1) // ITEMS


def plan(lay, filled, terms):
    smem = pl.BlockSpec(memory_space=pltpu.SMEM)
    return pl.pallas_call(
        functools.partial(plan_kernel, lay),
        out_shape=jax.ShapeDtypeStruct((sum(lay.lengths),), jnp.int32),
        in_specs=[smem, smem],
        out_specs=smem,
        scratch_shapes=[pltpu.SMEM((lay.places.cols,), jnp.int32), pltpu.SMEM((lay.states,), jnp.int32)],
        name="plan",
    )(filled, terms)


def main_kernel(lay, stage, places_of, rows, *refs):
    late = stage == STAGES - 1
    n_psi = len(places_of)
    table, right, left, sib = refs[:4]
    counts, spots, blocks, pair_q, pair_t, lefts, item_tile, allowed, totals = lay.lists(table)
    psi_in, refs = refs[4 : 4 + n_psi], refs[4 + n_psi :]
    before = None
    if stage > 0:
        before, refs = refs[0], refs[1:]
    if late:
        (out_own, out_sib), refs = refs[:2], refs[2:]
    else:
        out, refs = refs[0], refs[1:]
    right_v, psi_v, left_v, acc, w_hi, w_lo, w_acc, right_sem, psi_sem, left_sem, out_sem = refs
    core = lax.axis_index("row") % CORES
    list_at = stage * lay.pairs
    everything = CORES * rows

    def left_copies(g, slot, act):
        for i in range(GROUP):
            q = jnp.minimum(pair_q[list_at + g * GROUP + i], lay.states - 1)
            t = pair_t[list_at + g * GROUP + i]
            y, kb = q // lay.row_blocks, q % lay.row_blocks
            at = pl.ds(pl.multiple_of(((y * CORES + core) * lay.row_blocks + kb) * BLOCK, BLOCK), BLOCK)
            lanes = pl.ds(i * BLOCK, BLOCK)
            for side, source in enumerate((left, sib)):
                act(
                    pltpu.make_async_copy(
                        source.at[t, :, at], left_v.at[slot, pl.ds(side * rows, rows), lanes], left_sem.at[slot, 2 * i + side]
                    )
                )

    def right_copy(t):
        return pltpu.make_async_copy(right.at[t], right_v.at[t], right_sem.at[t])

    start, stop = 0, totals[stage]
    loads = []
    for i, (first, place, wide) in enumerate(places_of):
        loads.append(pltpu.make_async_copy(psi_in[i].at[pl.ds(first, wide)], psi_v.at[pl.ds(place, wide)], psi_sem.at[i]))
    for load in loads:
        load.start()
    if stage > 0:
        sums = pltpu.make_async_copy(before, acc.at[pl.ds(0, everything)], out_sem.at[0])
    first_t = pair_t[list_at + start * GROUP]
    last_t = pair_t[list_at + jnp.maximum(stop * GROUP - 1, 0)]

    @pl.when(stop > start)
    def _():
        right_copy(first_t).start()

    psi_v[0] = jnp.zeros((BLOCK, BLOCK), psi_v.dtype)
    if stage > 0:
        acc[pl.ds(everything, BLOCK), :] = jnp.zeros((BLOCK, acc.shape[1]), acc.dtype)
    else:
        acc[...] = jnp.zeros_like(acc)
    for load in loads:
        load.wait()

    @pl.when(stop > start)
    def _():
        left_copies(start, start % 2, lambda c: c.start())

    if stage > 0:
        sums.start()

    def one_group(g, next_t):
        slot = g % 2
        need_t = pair_t[list_at + g * GROUP + GROUP - 1]

        def one_term(t, carry):
            right_copy(t).wait()

            @pl.when(t < last_t)
            def _():
                right_copy(t + 1).start()

            return carry

        lax.fori_loop(next_t, need_t + 1, one_term, 0)

        @pl.when(g + 1 < stop)
        def _():
            left_copies(g + 1, 1 - slot, lambda c: c.start())

        for low in range(0, GROUP, SIDE):
            qs = [pair_q[list_at + g * GROUP + low + i] for i in range(SIDE)]
            ts = [pair_t[list_at + g * GROUP + low + i] for i in range(SIDE)]
            longest = counts[qs[0]]
            for q in qs[1:]:
                longest = jnp.maximum(longest, counts[q])

            def chunk_dot(i, j):
                at = qs[i] * lay.stride + j * CHUNK
                lhs = jnp.concatenate([psi_v[spots[at + m]] for m in range(CHUNK)], axis=1)
                rhs = jnp.concatenate(
                    [
                        right_v[ts[i], pl.ds(pl.multiple_of(blocks[at + m] * BLOCK, BLOCK), BLOCK), :]
                        for m in range(CHUNK)
                    ],
                    axis=0,
                )
                return jnp.dot(lhs, rhs, preferred_element_type=jnp.float32)

            @pl.when(longest == 0)
            def _():
                w_acc[...] = jnp.zeros_like(w_acc)

            @pl.when(longest > 0)
            def _():
                for i in range(SIDE):
                    w_acc[i * BLOCK : (i + 1) * BLOCK, :] = chunk_dot(i, 0)

            def one_chunk(j, c1):
                for i in range(SIDE):
                    w_acc[i * BLOCK : (i + 1) * BLOCK, :] += chunk_dot(i, j)
                return c1

            lax.fori_loop(1, (longest + CHUNK - 1) // CHUNK, one_chunk, 0)
            whole = w_acc[...]
            hi = whole.astype(jnp.bfloat16)
            w_hi[low * BLOCK : (low + SIDE) * BLOCK, :] = hi
            w_lo[low * BLOCK : (low + SIDE) * BLOCK, :] = (whole - hi.astype(jnp.float32)).astype(jnp.bfloat16)
        left_copies(g, slot, lambda c: c.wait())
        if stage > 0:

            @pl.when(g == start)
            def _():
                sums.wait()


        def some_items(depth, m, c0):
            for j in range(ITEMS):
                item = m * ITEMS + j
                width = lay.tile * BLOCK
                lanes = pl.ds(pl.multiple_of(item_tile[item] * width, width), width)
                a = [lefts[2 * item + i] for i in range(2)]
                source = [pl.multiple_of(jnp.minimum(b, lay.new_left - 1) * BLOCK, BLOCK) for b in a]
                lhs = jnp.concatenate([left_v[slot, pl.ds(b, BLOCK), :depth] for b in source], axis=0)
                gain = jnp.dot(lhs, w_hi[:depth, lanes], preferred_element_type=jnp.float32)
                gain = gain + jnp.dot(lhs, w_lo[:depth, lanes], preferred_element_type=jnp.float32)
                for i in range(2):
                    acc[pl.ds(pl.multiple_of(a[i] * BLOCK, BLOCK), BLOCK), lanes] += gain[i * BLOCK : (i + 1) * BLOCK]
            return c0

        short = pair_q[list_at + g * GROUP + SIDE] == lay.states
        steps = totals[STAGES]
        lax.fori_loop(0, jnp.where(short, 0, steps), functools.partial(some_items, GROUP * BLOCK), 0)
        lax.fori_loop(0, jnp.where(short, steps, 0), functools.partial(some_items, SIDE * BLOCK), 0)
        return jnp.maximum(next_t, need_t + 1)

    lax.fori_loop(start, stop, one_group, first_t)
    if stage > 0:

        @pl.when(stop <= start)
        def _():
            sums.wait()

    if late:
        for a in range(lay.new_left):
            for cb in range(lay.col_blocks):
                @pl.when(allowed[a * lay.col_blocks + cb] == 0)
                def _():
                    acc[pl.ds(a * BLOCK, BLOCK), pl.ds(cb * BLOCK, BLOCK)] = jnp.zeros((BLOCK, BLOCK), acc.dtype)

        stores = [
            pltpu.make_async_copy(acc.at[pl.ds(rows, rows)], out_sib, out_sem.at[1]),
            pltpu.make_async_copy(acc.at[pl.ds(0, rows)], out_own, out_sem.at[0]),
        ]
    else:
        stores = [pltpu.make_async_copy(acc.at[pl.ds(0, everything)], out, out_sem.at[0])]
    for store in stores:
        store.start()
    for store in stores:
        store.wait()


def contract(lay, stage, table, right, left, sib, parts, before=None):
    late = stage == STAGES - 1
    rows = lay.row_blocks * BLOCK
    cols = lay.col_blocks * BLOCK
    flat, places_of = [], []
    for (_, wide, place), part in zip(lay.runs, parts):
        for shard, array, first, count in part:
            flat.append(array)
            places_of.append((first, place + shard * wide, count))
    smem = pl.BlockSpec(memory_space=pltpu.SMEM)
    hbm = pl.BlockSpec(memory_space=pl.ANY)
    operands = [right, left, sib, *flat] + ([before] if stage > 0 else [])
    one = jax.ShapeDtypeStruct((rows, cols), jnp.float32)
    both = jax.ShapeDtypeStruct((CORES * rows, cols), jnp.float32)
    return pl.pallas_call(
        functools.partial(main_kernel, lay, stage, places_of, rows),
        out_shape=[one, one] if late else both,
        in_specs=[smem] + [hbm] * len(operands),
        out_specs=[hbm, hbm] if late else hbm,
        scratch_shapes=[
            pltpu.VMEM(right.shape, jnp.bfloat16),
            pltpu.VMEM((lay.room(len(parts)), BLOCK, BLOCK), jnp.bfloat16),
            pltpu.VMEM((2, CORES * rows, GROUP * BLOCK), jnp.bfloat16),
            pltpu.VMEM((CORES * rows + BLOCK, cols), jnp.float32),
            pltpu.VMEM((GROUP * BLOCK, cols), jnp.bfloat16),
            pltpu.VMEM((GROUP * BLOCK, cols), jnp.bfloat16),
            pltpu.VMEM((SIDE * BLOCK, cols), jnp.float32),
            pltpu.SemaphoreType.DMA((lay.terms,)),
            pltpu.SemaphoreType.DMA((len(flat),)),
            pltpu.SemaphoreType.DMA((2, 2 * GROUP)),
            pltpu.SemaphoreType.DMA((2,)),
        ],
        compiler_params=pltpu.CompilerParams(vmem_limit_bytes=VMEM_LIMIT),
        cost_estimate=pl.CostEstimate(flops=1000, bytes_accessed=right.size * 4, transcendentals=0),
        name="late_contract" if late else "early_contract",
    )(table, *operands)


def pack_kernel(copies, *refs):
    n_out = 1 + max(copy[3] for copy in copies)
    sources, outs, sems = refs[: -1 - n_out], refs[-1 - n_out : -1], refs[-1]
    moves = [
        pltpu.make_async_copy(sources[source].at[pl.ds(first, wide)], outs[out].at[pl.ds(at, wide)], sems.at[i])
        for i, (source, first, wide, out, at) in enumerate(copies)
    ]
    for move in moves:
        move.start()
    for move in moves:
        move.wait()


def pack(arrays, copies):
    n_out = 1 + max(copy[3] for copy in copies)
    sizes = [sum(copy[2] for copy in copies if copy[3] == out) for out in range(n_out)]
    vmem = pl.BlockSpec(memory_space=pltpu.VMEM)
    return pl.pallas_call(
        functools.partial(pack_kernel, copies),
        out_shape=[jax.ShapeDtypeStruct((size, *arrays[0].shape[1:]), arrays[0].dtype) for size in sizes],
        in_specs=[vmem] * len(arrays),
        out_specs=[vmem] * n_out,
        scratch_shapes=[pltpu.SemaphoreType.DMA((len(copies),))],
        name="pack",
    )(*arrays)


def after(array, *others):
    return lax.optimization_barrier((array, *others))[0]


class Spread:
    def __init__(self, places, part, owns, first):
        self.places, self.part, self.wide, self.owns, self.first = places, part, part.shape[0], owns, first

    def over_z(self, *others):
        part = after(self.part, *others) if others else self.part
        z = self.places.z
        up, down = {0: part}, {0: part}
        for far in range(1, z // 2 + 1):
            up[far] = move(self.places, up[far - 1], dz=1)
            if far < z - far:
                down[far] = move(self.places, down[far - 1], dz=z - 1)
        self.z = [up[dz] if dz in up else down[z - dz] for dz in range(1, z)]

    def pack_z(self, *others):
        z = [after(array, *others) for array in self.z] if others else self.z
        (self.q,) = pack(z, [(i, 0, self.wide, 0, i * self.wide) for i in range(len(self.z))])
        return self.q

    def over_xy(self):
        self.lines = over_xy(self.places, self.q)

    def diagonal(self, y_last, *others):
        self.lines.update(diagonal(self.places, self.lines, y_last, *others))

    def arrays(self, own_y=True, other_y=True):
        x, z, w = self.places.x, self.places.z, self.wide
        got = [(0, self.part, 0, w), (1, self.q, 0, (z - 1) * w)] if own_y else []
        for (dy, dx), line in self.lines.items():
            if own_y if dy == 0 else other_y:
                first = self.first if dy == 0 or dx == 0 else 0
                got.append(((dy * x + dx) * z, self.owns[dy, dx], first, w))
                got.append(((dy * x + dx) * z + 1, line, 0, (z - 1) * w))
        return got


def over_xy(places, array):
    got = {(0, dx): move(places, array, dx=dx) for dx in range(1, places.x)}
    got.update({(dy, 0): move(places, array, dy=dy) for dy in range(1, places.y)})
    return got


def diagonal(places, got, y_last, *others):
    rest = {}
    for dy in range(1, places.y):
        for dx in range(1, places.x):
            near = got[0, dx] if y_last else got[dy, 0]
            near = after(near, *others) if others else near
            rest[dy, dx] = move(places, near, dy=dy) if y_last else move(places, near, dx=dx)
    return rest


def move(places, array, **step):
    return lax.ppermute(array, AXES, places.shift(**step))


def on_device(wavefunction, left_env, right_env, filled_blocks, term_columns):
    rows, cols = wavefunction.shape
    row_blocks, col_blocks = rows // BLOCK, cols // BLOCK
    places = Places(lax.axis_size("row"), lax.axis_size("col"))
    slots = row_blocks * col_blocks
    chunks = [-(-slots * 10 // 32), -(-slots * 10 // 32), slots * 4 // 32]
    base = chunks[0] + chunks[1]
    chunks.append(slots - sum(chunks))
    lay = Layout(places, row_blocks, col_blocks, left_env.shape[0], chunks)

    own, part1, part2 = compress(wavefunction, filled_blocks, [(0, base), (0, chunks[0]), (chunks[0], base)])
    owns = over_xy(places, own)
    near = list(owns.values())
    one, two = Spread(places, part1, owns, 0), Spread(places, part2, owns, chunks[0])
    swap = places.shift(dcore=1)
    sib = lax.ppermute(left_env, AXES, swap)
    table = plan(lay, filled_blocks, term_columns)
    most = jnp.max(filled_blocks.reshape(places.rows, row_blocks, places.cols, col_blocks).sum(axis=(1, 3)))

    one.over_z()
    for spread, y_last in ((one, True), (two, False)):
        low, high = spread.first, spread.first + spread.wide
        mine = {key: after(array, one.z[0])[low:high] for key, array in owns.items()}
        spread.owns = {**owns, **diagonal(places, mine, y_last)}
        near += [array for key, array in spread.owns.items() if key not in owns]
    one.pack_z(*near)
    one.over_xy()
    two.over_z(one.q)
    two.pack_z(*near, *one.lines.values())
    two.q, table, most = lax.optimization_barrier((two.q, table, most))
    two.over_xy()
    one.diagonal(True, two.q)
    sums = contract(lay, 0, table, after(right_env, two.q), left_env, sib, [one.arrays(other_y=False)])
    two.diagonal(False, sums)
    near = [two.lines[dy, 0] for dy in range(1, places.y)]
    own_y = [one.arrays(other_y=False), two.arrays(other_y=False)]
    sums = contract(lay, 1, table, after(right_env, *near), left_env, sib, own_y, sums)

    def finish(extra, _):
        low, parts = base, [one.arrays(extra > 0), two.arrays(extra > 0)]
        for wide in chunks[2 : 2 + extra]:
            (part,) = compress(wavefunction, filled_blocks, [(low, low + wide)])
            owns = over_xy(places, part)
            owns.update(diagonal(places, owns, True))
            more = Spread(places, part, owns, 0)
            more.over_z()
            more.pack_z()
            more.over_xy()
            more.diagonal(False)
            parts.append(more.arrays())
            low += wide
        return contract(lay, 2, table, right_env, left_env, sib, parts, sums)

    levels = jnp.where(most > base, 1, 0) + jnp.where(most > base + chunks[2], 1, 0)
    own, theirs = lax.switch(levels, [functools.partial(finish, extra) for extra in range(3)], 0)
    return (own + lax.ppermute(theirs, AXES, swap)).astype(jnp.bfloat16)


def solution(mesh):
    in_specs = (P("row", "col"), P(None, "row", None), P(None, None, "col"), P(), P())
    out_specs = P("row", "col")
    return jax.shard_map(
        on_device, mesh=mesh, in_specs=in_specs, out_specs=out_specs, check_vma=False
    )
```

```python
import functools
import math

import jax
import jax.numpy as jnp
from jax import lax
from jax.experimental import pallas as pl
from jax.experimental.pallas import tpu as pltpu
from jax.sharding import PartitionSpec as P

BLOCK = 128
CORES = 2
STAGES = 3
ITEMS = 2
GROUP = 8
SIDE = 4
CHUNK = 8
AXES = ("row", "col")
VMEM_LIMIT = 58 * 1024 * 1024
VMEM_SPARE = 6 * 1024 * 1024


class Places:
    def __init__(self, row_devices, col_devices):
        self.rows, self.cols = row_devices, col_devices
        self.y = row_devices // CORES
        self.x = 1
        while self.x * self.x * 4 <= col_devices and col_devices % (self.x * 2) == 0:
            self.x *= 2
        self.z = col_devices // self.x

    def flat(self, y, core, z, x):
        return (y * CORES + core) * self.cols + z * self.x + x

    def shift(self, dy=0, dz=0, dx=0, dcore=0):
        perm = []
        for y in range(self.y):
            for core in range(CORES):
                for z in range(self.z):
                    for x in range(self.x):
                        there = self.flat(
                            (y + dy) % self.y, (core + dcore) % CORES, (z + dz) % self.z, (x + dx) % self.x
                        )
                        perm.append((self.flat(y, core, z, x), there))
        return perm


def compress_kernel(ranges, row_blocks, col_blocks, filled, psi, *rest):
    outs, sems = rest[: len(ranges)], rest[len(ranges)]
    row0 = lax.axis_index("row") * row_blocks
    col0 = lax.axis_index("col") * col_blocks

    def copy(i, slot, kb, cb):
        return pltpu.make_async_copy(
            psi.at[pl.ds(kb * BLOCK, BLOCK), pl.ds(cb * BLOCK, BLOCK)], outs[i].at[slot - ranges[i][0]], sems.at[i, slot]
        )

    count = jnp.int32(0)
    for kb in range(row_blocks):
        for cb in range(col_blocks):
            here = filled[row0 + kb, col0 + cb]
            for i, (low, high) in enumerate(ranges):
                @pl.when((here != 0) & (count >= low) & (count < high))
                def _():
                    copy(i, count, kb, cb).start()
            count = count + here
    for i, (low, high) in enumerate(ranges):
        for slot in range(low, high):
            @pl.when(slot < count)
            def _():
                copy(i, slot, 0, 0).wait()


def compress(psi, filled, ranges):
    row_blocks, col_blocks = psi.shape[0] // BLOCK, psi.shape[1] // BLOCK
    return pl.pallas_call(
        functools.partial(compress_kernel, ranges, row_blocks, col_blocks),
        out_shape=[jax.ShapeDtypeStruct((high - low, BLOCK, BLOCK), psi.dtype) for low, high in ranges],
        in_specs=[pl.BlockSpec(memory_space=pltpu.SMEM), pl.BlockSpec(memory_space=pltpu.VMEM)],
        out_specs=[pl.BlockSpec(memory_space=pltpu.VMEM)] * len(ranges),
        scratch_shapes=[pltpu.SemaphoreType.DMA((len(ranges), row_blocks * col_blocks))],
        name="compress",
    )(filled, psi)


class Layout:
    def __init__(self, places, row_blocks, col_blocks, terms, chunks):
        self.places, self.row_blocks, self.col_blocks, self.terms, self.chunks = places, row_blocks, col_blocks, terms, chunks
        self.slots = row_blocks * col_blocks
        self.base = chunks[0] + chunks[1]
        self.states = places.y * row_blocks
        self.old_right = places.cols * col_blocks
        self.shards = places.y * places.z * places.x
        self.stride = self.old_right + CHUNK
        self.pairs = self.states * terms + GROUP
        self.tile = 2 if col_blocks % 2 == 0 else 1
        self.tiles = col_blocks // self.tile
        self.new_left = CORES * row_blocks
        self.trash = self.new_left
        self.items = self.tiles * ((self.new_left + 1) // 2) + ITEMS
        self.runs = []
        slot, place = 0, 1
        for wide in chunks:
            self.runs.append((slot, wide, place))
            slot += wide
            place += wide * self.shards

        self.lengths = [
            self.states + 1,
            (self.states + 1) * self.stride,
            (self.states + 1) * self.stride,
            STAGES * self.pairs,
            STAGES * self.pairs,
            2 * self.items,
            self.items,
            self.new_left * col_blocks,
            STAGES + 1,
        ]

    def room(self, chunks):
        return 1 + self.shards * sum(self.chunks[:chunks])

    def lists(self, table):
        at, lists = 0, []
        for length in self.lengths:
            lists.append(List(table, at))
            at += length
        return lists


class List:
    def __init__(self, table, at):
        self.table, self.at = table, at

    def __getitem__(self, i):
        return self.table[self.at + i]

    def __setitem__(self, i, value):
        self.table[self.at + i] = jnp.int32(value)


def plan_kernel(lay, filled, terms, table, used, ready):
    counts, spots, blocks, pair_q, pair_t, lefts, item_tile, allowed, totals = lay.lists(table)
    pz, px, py = lay.places.z, lay.places.x, lay.places.y
    row, col = lax.axis_index("row"), lax.axis_index("col")
    core, y_me = row % CORES, row // CORES
    z_me, x_me = col // px, col % px

    def one_state(q, carry):
        y = q // lay.row_blocks
        kb = q % lay.row_blocks

        @pl.when(kb == 0)
        def _():
            for dev in range(lay.places.cols):
                used[dev] = 0

        dy = (y_me - y + py) % py
        k_block = (y * CORES + core) * lay.row_blocks + kb
        n = jnp.int32(0)
        most = jnp.int32(0)
        for dev in range(lay.places.cols):
            dz = (z_me - dev // px + pz) % pz
            dx = (x_me - dev % px + px) % px
            shard = (dy * px + dx) * pz + dz
            slot = used[dev]
            for cb in range(lay.col_blocks):
                c = dev * lay.col_blocks + cb
                here = filled[k_block, c]
                spot = jnp.int32(0)
                for first, wide, place in lay.runs:
                    spot = jnp.where(slot >= first, place + shard * wide + slot - first, spot)
                spots[q * lay.stride + n] = spot
                blocks[q * lay.stride + n] = c
                n = n + here
                slot = slot + here
            used[dev] = slot
            most = jnp.maximum(most, slot)

        def pad(i, carry):
            spots[q * lay.stride + i] = 0
            blocks[q * lay.stride + i] = 0
            return carry

        lax.fori_loop(n, lay.stride, pad, 0)
        counts[q] = n
        when = jnp.where((y == y_me) & (most <= lay.base), jnp.where(most <= lay.chunks[0], 0, 1), 2)
        ready[q] = when
        n_first, n_own = carry
        for t in range(lay.terms):
            on = jnp.where((terms[t, k_block] != 0) & (n > 0), 1, 0)
            n_first = n_first + jnp.where(when == 0, on, 0)
            n_own = n_own + jnp.where(when <= 1, on, 0)
        return n_first, n_own

    n_first, n_own = lax.fori_loop(0, lay.states, one_state, (jnp.int32(0), jnp.int32(0)))
    n_first = n_first // GROUP * GROUP
    n_own = n_own - n_first
    have = (jnp.int32(0), jnp.int32(0), jnp.int32(0))
    for t in range(lay.terms):

        def one_pair(q, have):
            n0, n1, n2 = have
            k_block = (q // lay.row_blocks * CORES + core) * lay.row_blocks + q % lay.row_blocks
            on = jnp.where((terms[t, k_block] != 0) & (counts[q] > 0), 1, 0)
            to0 = jnp.where((ready[q] == 0) & (n0 < n_first), on, 0)
            to1 = jnp.where((ready[q] <= 1) & (n1 < n_own), on - to0, 0)
            at = jnp.where(to0 != 0, n0, jnp.where(to1 != 0, lay.pairs + n1, 2 * lay.pairs + n2))
            pair_q[at] = q
            pair_t[at] = t
            return n0 + to0, n1 + to1, n2 + on - to0 - to1

        have = lax.fori_loop(0, lay.states, one_pair, have)
    n_late = have[2]
    counts[lay.states] = 0

    def pad_state(i, carry):
        spots[lay.states * lay.stride + i] = 0
        blocks[lay.states * lay.stride + i] = 0
        return carry

    lax.fori_loop(0, lay.stride, pad_state, 0)
    for i in range(GROUP):
        for at in (lay.pairs + n_own + i, 2 * lay.pairs + n_late + i):
            pair_q[at] = lay.states
            pair_t[at] = lay.terms - 1
    totals[0] = n_first // GROUP
    totals[1] = (n_own + GROUP - 1) // GROUP
    totals[2] = (n_late + GROUP - 1) // GROUP
    items = jnp.int32(0)
    for tile in range(lay.tiles):
        n = jnp.int32(0)
        for a in range(lay.new_left):
            side, ab = a // lay.row_blocks, a % lay.row_blocks
            a_block = (y_me * CORES + (core + side) % CORES) * lay.row_blocks + ab
            some = jnp.int32(0)
            for i in range(lay.tile):
                here = filled[a_block, col * lay.col_blocks + tile * lay.tile + i]
                allowed[a * lay.col_blocks + tile * lay.tile + i] = here
                some = some | here
            lefts[2 * items + n] = a
            item_tile[items + n // 2] = tile
            n = n + some
        lefts[2 * items + n] = lay.trash
        items = items + (n + 1) // 2
    for i in range(ITEMS):
        lefts[2 * (items + i)] = lay.trash
        lefts[2 * (items + i) + 1] = lay.trash
        item_tile[items + i] = 0
    totals[STAGES] = (items + ITEMS - 1) // ITEMS


def plan(lay, filled, terms):
    smem = pl.BlockSpec(memory_space=pltpu.SMEM)
    return pl.pallas_call(
        functools.partial(plan_kernel, lay),
        out_shape=jax.ShapeDtypeStruct((sum(lay.lengths),), jnp.int32),
        in_specs=[smem, smem],
        out_specs=smem,
        scratch_shapes=[pltpu.SMEM((lay.places.cols,), jnp.int32), pltpu.SMEM((lay.states,), jnp.int32)],
        name="plan",
    )(filled, terms)


def main_kernel(lay, stage, places_of, rows, *refs):
    late = stage == STAGES - 1
    n_psi = len(places_of)
    table, right, left, sib = refs[:4]
    counts, spots, blocks, pair_q, pair_t, lefts, item_tile, allowed, totals = lay.lists(table)
    psi_in, refs = refs[4 : 4 + n_psi], refs[4 + n_psi :]
    before = None
    if stage > 0:
        before, refs = refs[0], refs[1:]
    if late:
        (out_own, out_sib), refs = refs[:2], refs[2:]
    else:
        out, refs = refs[0], refs[1:]
    right_v, psi_v, left_v, acc, w_hi, w_lo, w_acc, right_sem, psi_sem, left_sem, out_sem = refs
    core = lax.axis_index("row") % CORES
    list_at = stage * lay.pairs
    everything = CORES * rows

    def left_copies(g, slot, act):
        for i in range(GROUP):
            q = jnp.minimum(pair_q[list_at + g * GROUP + i], lay.states - 1)
            t = pair_t[list_at + g * GROUP + i]
            y, kb = q // lay.row_blocks, q % lay.row_blocks
            at = pl.ds(pl.multiple_of(((y * CORES + core) * lay.row_blocks + kb) * BLOCK, BLOCK), BLOCK)
            lanes = pl.ds(i * BLOCK, BLOCK)
            for side, source in enumerate((left, sib)):
                act(
                    pltpu.make_async_copy(
                        source.at[t, :, at], left_v.at[slot, pl.ds(side * rows, rows), lanes], left_sem.at[slot, 2 * i + side]
                    )
                )

    def right_copy(t):
        return pltpu.make_async_copy(right.at[t], right_v.at[t], right_sem.at[t])

    start, stop = 0, totals[stage]
    loads = []
    for i, (first, place, wide) in enumerate(places_of):
        loads.append(pltpu.make_async_copy(psi_in[i].at[pl.ds(first, wide)], psi_v.at[pl.ds(place, wide)], psi_sem.at[i]))
    for load in loads:
        load.start()
    if stage > 0:
        sums = pltpu.make_async_copy(before, acc.at[pl.ds(0, everything)], out_sem.at[0])
    first_t = pair_t[list_at + start * GROUP]
    last_t = pair_t[list_at + jnp.maximum(stop * GROUP - 1, 0)]

    @pl.when(stop > start)
    def _():
        right_copy(first_t).start()

    psi_v[0] = jnp.zeros((BLOCK, BLOCK), psi_v.dtype)
    if stage > 0:
        acc[pl.ds(everything, BLOCK), :] = jnp.zeros((BLOCK, acc.shape[1]), acc.dtype)
    else:
        acc[...] = jnp.zeros_like(acc)
    for load in loads:
        load.wait()

    @pl.when(stop > start)
    def _():
        left_copies(start, start % 2, lambda c: c.start())

    if stage > 0:
        sums.start()

    def one_group(g, next_t):
        slot = g % 2
        need_t = pair_t[list_at + g * GROUP + GROUP - 1]

        def one_term(t, carry):
            right_copy(t).wait()

            @pl.when(t < last_t)
            def _():
                right_copy(t + 1).start()

            return carry

        lax.fori_loop(next_t, need_t + 1, one_term, 0)

        @pl.when(g + 1 < stop)
        def _():
            left_copies(g + 1, 1 - slot, lambda c: c.start())

        for low in range(0, GROUP, SIDE):
            qs = [pair_q[list_at + g * GROUP + low + i] for i in range(SIDE)]
            ts = [pair_t[list_at + g * GROUP + low + i] for i in range(SIDE)]
            longest = counts[qs[0]]
            for q in qs[1:]:
                longest = jnp.maximum(longest, counts[q])

            def chunk_dot(i, j):
                at = qs[i] * lay.stride + j * CHUNK
                lhs = jnp.concatenate([psi_v[spots[at + m]] for m in range(CHUNK)], axis=1)
                rhs = jnp.concatenate(
                    [
                        right_v[ts[i], pl.ds(pl.multiple_of(blocks[at + m] * BLOCK, BLOCK), BLOCK), :]
                        for m in range(CHUNK)
                    ],
                    axis=0,
                )
                return jnp.dot(lhs, rhs, preferred_element_type=jnp.float32)

            @pl.when(longest == 0)
            def _():
                w_acc[...] = jnp.zeros_like(w_acc)

            @pl.when(longest > 0)
            def _():
                for i in range(SIDE):
                    w_acc[i * BLOCK : (i + 1) * BLOCK, :] = chunk_dot(i, 0)

            def one_chunk(j, c1):
                for i in range(SIDE):
                    w_acc[i * BLOCK : (i + 1) * BLOCK, :] += chunk_dot(i, j)
                return c1

            lax.fori_loop(1, (longest + CHUNK - 1) // CHUNK, one_chunk, 0)
            whole = w_acc[...]
            hi = whole.astype(jnp.bfloat16)
            w_hi[low * BLOCK : (low + SIDE) * BLOCK, :] = hi
            w_lo[low * BLOCK : (low + SIDE) * BLOCK, :] = (whole - hi.astype(jnp.float32)).astype(jnp.bfloat16)
        left_copies(g, slot, lambda c: c.wait())
        if stage > 0:

            @pl.when(g == start)
            def _():
                sums.wait()


        def some_items(depth, m, c0):
            for j in range(ITEMS):
                item = m * ITEMS + j
                width = lay.tile * BLOCK
                lanes = pl.ds(pl.multiple_of(item_tile[item] * width, width), width)
                a = [lefts[2 * item + i] for i in range(2)]
                source = [pl.multiple_of(jnp.minimum(b, lay.new_left - 1) * BLOCK, BLOCK) for b in a]
                lhs = jnp.concatenate([left_v[slot, pl.ds(b, BLOCK), :depth] for b in source], axis=0)
                gain = jnp.dot(lhs, w_hi[:depth, lanes], preferred_element_type=jnp.float32)
                gain = gain + jnp.dot(lhs, w_lo[:depth, lanes], preferred_element_type=jnp.float32)
                for i in range(2):
                    acc[pl.ds(pl.multiple_of(a[i] * BLOCK, BLOCK), BLOCK), lanes] += gain[i * BLOCK : (i + 1) * BLOCK]
            return c0

        short = pair_q[list_at + g * GROUP + SIDE] == lay.states
        steps = totals[STAGES]
        lax.fori_loop(0, jnp.where(short, 0, steps), functools.partial(some_items, GROUP * BLOCK), 0)
        lax.fori_loop(0, jnp.where(short, steps, 0), functools.partial(some_items, SIDE * BLOCK), 0)
        return jnp.maximum(next_t, need_t + 1)

    lax.fori_loop(start, stop, one_group, first_t)
    if stage > 0:

        @pl.when(stop <= start)
        def _():
            sums.wait()

    if late:
        for a in range(lay.new_left):
            for cb in range(lay.col_blocks):
                @pl.when(allowed[a * lay.col_blocks + cb] == 0)
                def _():
                    acc[pl.ds(a * BLOCK, BLOCK), pl.ds(cb * BLOCK, BLOCK)] = jnp.zeros((BLOCK, BLOCK), acc.dtype)

        stores = [
            pltpu.make_async_copy(acc.at[pl.ds(rows, rows)], out_sib, out_sem.at[1]),
            pltpu.make_async_copy(acc.at[pl.ds(0, rows)], out_own, out_sem.at[0]),
        ]
    else:
        stores = [pltpu.make_async_copy(acc.at[pl.ds(0, everything)], out, out_sem.at[0])]
    for store in stores:
        store.start()
    for store in stores:
        store.wait()


def contract(lay, stage, table, right, left, sib, parts, before=None):
    late = stage == STAGES - 1
    rows = lay.row_blocks * BLOCK
    cols = lay.col_blocks * BLOCK
    flat, places_of = [], []
    for (_, wide, place), part in zip(lay.runs, parts):
        for shard, array, first, count in part:
            flat.append(array)
            places_of.append((first, place + shard * wide, count))
    smem = pl.BlockSpec(memory_space=pltpu.SMEM)
    hbm = pl.BlockSpec(memory_space=pl.ANY)
    operands = [right, left, sib, *flat] + ([before] if stage > 0 else [])
    one = jax.ShapeDtypeStruct((rows, cols), jnp.float32)
    both = jax.ShapeDtypeStruct((CORES * rows, cols), jnp.float32)
    shapes = [
        (right.shape, jnp.bfloat16),
        ((lay.room(len(parts)), BLOCK, BLOCK), jnp.bfloat16),
        ((2, CORES * rows, GROUP * BLOCK), jnp.bfloat16),
        ((CORES * rows + BLOCK, cols), jnp.float32),
        ((GROUP * BLOCK, cols), jnp.bfloat16),
        ((GROUP * BLOCK, cols), jnp.bfloat16),
        ((SIDE * BLOCK, cols), jnp.float32),
    ]
    grant = VMEM_SPARE + sum(math.prod(shape) * jnp.dtype(kind).itemsize for shape, kind in shapes)
    return pl.pallas_call(
        functools.partial(main_kernel, lay, stage, places_of, rows),
        out_shape=[one, one] if late else both,
        in_specs=[smem] + [hbm] * len(operands),
        out_specs=[hbm, hbm] if late else hbm,
        scratch_shapes=[
            *[pltpu.VMEM(shape, kind) for shape, kind in shapes],
            pltpu.SemaphoreType.DMA((lay.terms,)),
            pltpu.SemaphoreType.DMA((len(flat),)),
            pltpu.SemaphoreType.DMA((2, 2 * GROUP)),
            pltpu.SemaphoreType.DMA((2,)),
        ],
        compiler_params=pltpu.CompilerParams(vmem_limit_bytes=min(grant, VMEM_LIMIT)),
        cost_estimate=pl.CostEstimate(flops=1000, bytes_accessed=right.size * 4, transcendentals=0),
        name="late_contract" if late else "early_contract",
    )(table, *operands)


def pack_kernel(copies, *refs):
    n_out = 1 + max(copy[3] for copy in copies)
    sources, outs, sems = refs[: -1 - n_out], refs[-1 - n_out : -1], refs[-1]
    moves = [
        pltpu.make_async_copy(sources[source].at[pl.ds(first, wide)], outs[out].at[pl.ds(at, wide)], sems.at[i])
        for i, (source, first, wide, out, at) in enumerate(copies)
    ]
    for move in moves:
        move.start()
    for move in moves:
        move.wait()


def pack(arrays, copies):
    n_out = 1 + max(copy[3] for copy in copies)
    sizes = [sum(copy[2] for copy in copies if copy[3] == out) for out in range(n_out)]
    vmem = pl.BlockSpec(memory_space=pltpu.VMEM)
    return pl.pallas_call(
        functools.partial(pack_kernel, copies),
        out_shape=[jax.ShapeDtypeStruct((size, *arrays[0].shape[1:]), arrays[0].dtype) for size in sizes],
        in_specs=[vmem] * len(arrays),
        out_specs=[vmem] * n_out,
        scratch_shapes=[pltpu.SemaphoreType.DMA((len(copies),))],
        name="pack",
    )(*arrays)


def after(array, *others):
    return lax.optimization_barrier((array, *others))[0]


class Spread:
    def __init__(self, places, part, owns, first):
        self.places, self.part, self.wide, self.owns, self.first = places, part, part.shape[0], owns, first

    def over_z(self, *others):
        part = after(self.part, *others) if others else self.part
        z = self.places.z
        up, down = {0: part}, {0: part}
        for far in range(1, z // 2 + 1):
            up[far] = move(self.places, up[far - 1], dz=1)
            if far < z - far:
                down[far] = move(self.places, down[far - 1], dz=z - 1)
        self.z = [up[dz] if dz in up else down[z - dz] for dz in range(1, z)]

    def pack_z(self, *others):
        z = [after(array, *others) for array in self.z] if others else self.z
        (self.q,) = pack(z, [(i, 0, self.wide, 0, i * self.wide) for i in range(len(self.z))])
        return self.q

    def over_xy(self):
        self.lines = over_xy(self.places, self.q)

    def diagonal(self, y_last, *others):
        self.lines.update(diagonal(self.places, self.lines, y_last, *others))

    def arrays(self, own_y=True, other_y=True):
        x, z, w = self.places.x, self.places.z, self.wide
        got = [(0, self.part, 0, w), (1, self.q, 0, (z - 1) * w)] if own_y else []
        for (dy, dx), line in self.lines.items():
            if own_y if dy == 0 else other_y:
                first = self.first if dy == 0 or dx == 0 else 0
                got.append(((dy * x + dx) * z, self.owns[dy, dx], first, w))
                got.append(((dy * x + dx) * z + 1, line, 0, (z - 1) * w))
        return got


def over_xy(places, array):
    got = {(0, dx): move(places, array, dx=dx) for dx in range(1, places.x)}
    got.update({(dy, 0): move(places, array, dy=dy) for dy in range(1, places.y)})
    return got


def diagonal(places, got, y_last, *others):
    rest = {}
    for dy in range(1, places.y):
        for dx in range(1, places.x):
            near = got[0, dx] if y_last else got[dy, 0]
            near = after(near, *others) if others else near
            rest[dy, dx] = move(places, near, dy=dy) if y_last else move(places, near, dx=dx)
    return rest


def move(places, array, **step):
    return lax.ppermute(array, AXES, places.shift(**step))


def on_device(wavefunction, left_env, right_env, filled_blocks, term_columns):
    rows, cols = wavefunction.shape
    row_blocks, col_blocks = rows // BLOCK, cols // BLOCK
    places = Places(lax.axis_size("row"), lax.axis_size("col"))
    slots = row_blocks * col_blocks
    chunks = [-(-slots * 10 // 32), -(-slots * 10 // 32), slots * 4 // 32]
    base = chunks[0] + chunks[1]
    chunks.append(slots - sum(chunks))
    lay = Layout(places, row_blocks, col_blocks, left_env.shape[0], chunks)

    own, part1, part2 = compress(wavefunction, filled_blocks, [(0, base), (0, chunks[0]), (chunks[0], base)])
    owns = over_xy(places, own)
    near = list(owns.values())
    one, two = Spread(places, part1, owns, 0), Spread(places, part2, owns, chunks[0])
    swap = places.shift(dcore=1)
    sib = lax.ppermute(left_env, AXES, swap)
    table = plan(lay, filled_blocks, term_columns)
    most = jnp.max(filled_blocks.reshape(places.rows, row_blocks, places.cols, col_blocks).sum(axis=(1, 3)))

    one.over_z()
    for spread, y_last in ((one, True), (two, False)):
        low, high = spread.first, spread.first + spread.wide
        mine = {key: after(array, one.z[0])[low:high] for key, array in owns.items()}
        spread.owns = {**owns, **diagonal(places, mine, y_last)}
        near += [array for key, array in spread.owns.items() if key not in owns]
    one.pack_z(*near)
    one.over_xy()
    two.over_z(one.q)
    two.pack_z(*near, *one.lines.values())
    two.q, table, most = lax.optimization_barrier((two.q, table, most))
    two.over_xy()
    one.diagonal(True, two.q)
    sums = contract(lay, 0, table, after(right_env, two.q), left_env, sib, [one.arrays(other_y=False)])
    two.diagonal(False, sums)
    near = [two.lines[dy, 0] for dy in range(1, places.y)]
    own_y = [one.arrays(other_y=False), two.arrays(other_y=False)]
    sums = contract(lay, 1, table, after(right_env, *near), left_env, sib, own_y, sums)

    def finish(extra, _):
        low, parts = base, [one.arrays(extra > 0), two.arrays(extra > 0)]
        for wide in chunks[2 : 2 + extra]:
            (part,) = compress(wavefunction, filled_blocks, [(low, low + wide)])
            owns = over_xy(places, part)
            owns.update(diagonal(places, owns, True))
            more = Spread(places, part, owns, 0)
            more.over_z()
            more.pack_z()
            more.over_xy()
            more.diagonal(False)
            parts.append(more.arrays())
            low += wide
        return contract(lay, 2, table, right_env, left_env, sib, parts, sums)

    levels = jnp.where(most > base, 1, 0) + jnp.where(most > base + chunks[2], 1, 0)
    own, theirs = lax.switch(levels, [functools.partial(finish, extra) for extra in range(3)], 0)
    return (own + lax.ppermute(theirs, AXES, swap)).astype(jnp.bfloat16)


def solution(mesh):
    in_specs = (P("row", "col"), P(None, "row", None), P(None, None, "col"), P(), P())
    out_specs = P("row", "col")
    return jax.shard_map(
        on_device, mesh=mesh, in_specs=in_specs, out_specs=out_specs, check_vma=False
    )
```
